32 devices in a mesh: dp: 4 (over x, core), fsdp: 8 (over z, y).
Axes of the slice: x: 2, y: 2, z: 4, core: 2. Of those that a mesh axis runs over, the one named last changes fastest.
Arguments:
- tokens: bfloat16 [23040, 512], P(('dp', 'fsdp')), may hold values from -6 to 6
- cotangent: bfloat16 [23040, 512], P(('dp', 'fsdp')), may hold values from -6 to 6
- segment_ids: int32 [23040], P(('dp', 'fsdp')), may hold values from 0 to 14, as said below
- pad_mask: int32 [23040], P(('dp', 'fsdp')), may hold values from 0 to 1, as said below
- expert_ids: int32 [23040, 2], P(('dp', 'fsdp')), may hold values from 0 to 7, as said below
- priority: int32 [32, 720], P(('dp', 'fsdp')), may hold values from 0 to 719, each once within a row
- ln1_gain: bfloat16 [512], P('fsdp'), may hold values from 0.5 to 1.5
- ln1_shift: bfloat16 [512], P('fsdp'), may hold values from -1.25 to 1.25
- w_qkv: bfloat16 [512, 1536], P('fsdp'), may hold values from -0.25 to 0.25
- b_qv: bfloat16 [1024], P('fsdp'), may hold values from -1.25 to 1.25
- w_o: bfloat16 [512, 512], P('fsdp'), may hold values from -2 to 2
- b_o: bfloat16 [512], P('fsdp'), may hold values from -1.25 to 1.25
- ln2_gain: bfloat16 [512], P('fsdp'), may hold values from 0.5 to 1.5
- ln2_shift: bfloat16 [512], P('fsdp'), may hold values from -1.25 to 1.25
- w_router: bfloat16 [512, 8], P('fsdp'), may hold values from -0.1875 to 0.1875
- w_in: bfloat16 [8, 512, 2048], P('fsdp'), may hold values from -0.25 to 0.25
- b_in: bfloat16 [8, 2048], P('fsdp'), may hold values from -0.625 to 0.625
- w_out: bfloat16 [8, 2048, 512], P('fsdp'), may hold values from -0.5 to 0.5
- b_out: bfloat16 [8, 512], P('fsdp'), may hold values from -3 to 3
Outputs:
- output: bfloat16 [23040, 512], P(('dp', 'fsdp'))
- d_tokens: float32 [23040, 512], P(('dp', 'fsdp'))
- d_ln1_gain: float32 [512], P('fsdp')
- d_ln1_shift: float32 [512], P('fsdp')
- d_w_qkv: float32 [512, 1536], P('fsdp')
- d_b_qv: float32 [1024], P('fsdp')
- d_w_o: float32 [512, 512], P('fsdp')
- d_b_o: float32 [512], P('fsdp')
- d_ln2_gain: float32 [512], P('fsdp')
- d_ln2_shift: float32 [512], P('fsdp')
- d_w_router: float32 [512, 8], P('fsdp')
- d_w_in: float32 [8, 512, 2048], P('fsdp')
- d_b_in: float32 [8, 2048], P('fsdp')
- d_w_out: float32 [8, 2048, 512], P('fsdp')
- d_b_out: float32 [8, 512], P('fsdp')
The draws below stay inside these ranges and needn't reach their ends.
Inputs may be any that keep to these rules, and one draw needn't show every extreme that they name: `segment_ids`: within each sequence of 720 slots the numbers never fall; each image holds 49 or 144 slots; padding slots carry 14 and come last. `pad_mask`: 1 exactly at the slots whose segment number is under 14. `expert_ids`: the two experts of a slot differ. `priority`: each row holds each of 0 to 719 once.
All inputs are finite; a program needn't handle non-finite values.
Results may differ from the reference program's by a relative error of at most 0.025.
Values may be sent and summed in bfloat16 or wider, within the bound.
A program may use at most 192 MiB of HBM per device.

```python
from functools import partial
import jax
import jax.numpy as jnp
from jax import lax

D = 512
HEADS = 8
HEAD = 64
FF = 2048
EXPERTS = 8
SLOTS = 720
IMG_BIG = 144
IMG_SMALL = 49
MAXIMG = 14
TOK_DEV = 720
TOKENS = 23040
CAP = 189
N_DP = 4
N_FSDP = 8


def image_layout(key):
    sequences = TOKENS // SLOTS
    key_big, key_small, key_order = jax.random.split(jax.random.fold_in(key, 11), 3)
    count_big = jax.random.randint(key_big, (sequences, 1), 1, SLOTS // IMG_BIG + 1)
    count_small = jnp.maximum((SLOTS - count_big * IMG_BIG) // IMG_SMALL - jax.random.randint(key_small, (sequences, 1), 0, 2), 0)
    position = jnp.arange(MAXIMG, dtype=jnp.int32)[None, :]
    image_sizes = jnp.where(position < count_big, IMG_BIG, jnp.where(position < count_big + count_small, IMG_SMALL, 0))
    scores = jax.random.randint(key_order, (sequences, MAXIMG), 0, 1 << 20) * MAXIMG + position
    shuffle = jnp.argsort(scores, axis=1)
    image_sizes = jnp.take_along_axis(image_sizes, shuffle, axis=1)
    image_ends = jnp.cumsum(image_sizes, axis=1)
    slot_index = jnp.arange(SLOTS, dtype=jnp.int32)
    segment = jnp.sum((image_ends[:, None, :] <= slot_index[None, :, None]).astype(jnp.int32), axis=2)
    live_mask = (slot_index[None, :] < image_ends[:, -1:]).astype(jnp.int32)
    return (segment.astype(jnp.int32).reshape(TOKENS), live_mask.reshape(TOKENS))


def draw_segment_ids(key, part):
    segment, live_mask = image_layout(key)
    return segment


def draw_pad_mask(key, part):
    segment, live_mask = image_layout(key)
    return live_mask


def draw_expert_ids(key, part):
    key = jax.random.fold_in(key, 3)
    key_load, key_score = jax.random.split(key)
    popularity = jax.random.randint(key_load, (EXPERTS,), 2, 5)
    scores = jax.random.randint(key_score, (TOKENS, EXPERTS), 0, 1 << 14) * popularity[None, :] * EXPERTS + jnp.arange(EXPERTS, dtype=jnp.int32)[None, :]
    _, chosen = lax.top_k(scores, 2)
    return chosen.astype(jnp.int32)


def levels(rng, extent, cuts, low, top_value):
    def one(dim, blocks):
        heights = jax.random.uniform(jax.random.fold_in(jax.random.fold_in(rng, 6), dim), (blocks,), jnp.float32, low / len(cuts), top_value / len(cuts))
        return jnp.repeat(jnp.exp(heights), extent[dim] // blocks).reshape((-1,) + (1,) * (len(extent) - dim - 1))

    factor_of = one(*cuts[0])
    for cut in cuts[1:]:
        factor_of = factor_of * one(*cut)
    return factor_of


def noise(key, extent, width, bound, shards=(), kind=jnp.bfloat16):
    values = jax.random.normal(key, extent, jnp.float32) * width
    if len(shards) > 0:
        values = levels(key, extent, shards, -0.22, 0.18) * values
    return jnp.clip(values, min=-bound, max=bound).astype(kind)


def setup_inputs(seed: int = 0) -> dict:
    key_of = jax.random.split(jax.random.key(seed), 20)
    tokens = noise(key_of[0], (TOKENS, D), 1.0, 6.0, ((0, 32),))
    cotangent = noise(key_of[1], (TOKENS, D), 1.0, 6.0, ((0, 32),))
    segment_ids = draw_segment_ids(jax.random.fold_in(key_of[19], 71), 0)
    pad_mask = draw_pad_mask(jax.random.fold_in(key_of[19], 71), 0)
    expert_ids = draw_expert_ids(jax.random.fold_in(key_of[19], 71), 0)
    priority = jax.vmap(lambda own: jax.random.permutation(own, TOK_DEV))(jax.random.split(key_of[5], (N_DP * N_FSDP))).reshape((N_DP * N_FSDP, TOK_DEV)).astype(jnp.int32)
    ln1_gain = jnp.clip(1.0 + 0.1 * jax.random.normal(key_of[6], (D,), jnp.float32), 0.5, 1.5).astype(jnp.bfloat16)
    ln1_shift = noise(key_of[7], (D,), 0.2, 1.25, ((0, 8),))
    w_qkv = noise(key_of[8], (D, 3 * D), D ** -0.5, 0.25, ((0, 8),))
    b_qv = noise(key_of[9], (2 * D,), 0.2, 1.25, ((0, 8),))
    w_o = noise(key_of[10], (D, D), (D // 64) ** -0.5, 2.0, ((0, 8),))
    b_o = noise(key_of[11], (D,), 0.2, 1.25, ((0, 8),))
    ln2_gain = jnp.clip(1.0 + 0.1 * jax.random.normal(key_of[12], (D,), jnp.float32), 0.5, 1.5).astype(jnp.bfloat16)
    ln2_shift = noise(key_of[13], (D,), 0.2, 1.25, ((0, 8),))
    w_router = noise(key_of[14], (D, EXPERTS), (D * 16 // 9) ** -0.5, 0.1875, ((0, 8),))
    w_in = noise(key_of[15], (EXPERTS, D, FF), D ** -0.5, 0.25, ((0, 8),))
    b_in = noise(key_of[16], (EXPERTS, FF), 0.1, 0.625, ((0, 8),))
    w_out = noise(key_of[17], (EXPERTS, FF, D), (max(1, 4 * FF // (EXPERTS * EXPERTS))) ** -0.5, 0.5, ((0, 8),))
    b_out = noise(key_of[18], (EXPERTS, D), 0.5, 3.0, ((0, 8),))
    return dict(tokens=tokens, cotangent=cotangent, segment_ids=segment_ids, pad_mask=pad_mask, expert_ids=expert_ids, priority=priority, ln1_gain=ln1_gain, ln1_shift=ln1_shift, w_qkv=w_qkv, b_qv=b_qv, w_o=w_o, b_o=b_o, ln2_gain=ln2_gain, ln2_shift=ln2_shift, w_router=w_router, w_in=w_in, b_in=b_in, w_out=w_out, b_out=b_out)


EPS = 1e-06

@jax.custom_vjp
def low(v):
    return lax.optimization_barrier(v.astype(jnp.bfloat16)).astype(jnp.float32)

@jax.custom_vjp
def low_back(v):
    return v

def low_keep(v):
    return (low(v), None)

def low_pass(kept, grad):
    return (grad,)

def back_keep(v):
    return (v, None)

def back_low(kept, grad):
    return (low(grad),)
low.defvjp(low_keep, low_pass)
low_back.defvjp(back_keep, back_low)

def matmul(left, right):
    return jnp.dot(left, right, precision=lax.Precision.HIGHEST, preferred_element_type=jnp.float32)

def contract(form, left, right):
    return jnp.einsum(form, left, right, precision=lax.Precision.HIGHEST, preferred_element_type=jnp.float32)

def layer_norm(tensor, gain_vec, shift_vec):
    row_mean = lax.optimization_barrier(jnp.mean(tensor, axis=-1, keepdims=True))
    centred = tensor - row_mean
    inv_std = lax.rsqrt(lax.optimization_barrier(jnp.mean(centred * centred, axis=-1, keepdims=True)) + EPS)
    return centred * inv_std * gain_vec + shift_vec

def split_heads(tensor):
    return tensor.reshape(tensor.shape[0], HEADS, HEAD)

def allowed_pairs(segment, live_mask):
    same_image = segment[:, None] == segment[None, :]
    self_pair = jnp.arange(segment.shape[0])[:, None] == jnp.arange(segment.shape[0])[None, :]
    return same_image & ((live_mask[None, :] > 0) | self_pair)

def make_slots(expert_list, priority_row, live_mask, experts, capacity):
    count_tok = expert_list.shape[0]
    at_rank = jnp.zeros((count_tok,), jnp.int32).at[priority_row].set(jnp.arange(count_tok, dtype=jnp.int32))
    ranked = expert_list[at_rank]
    ranked_live = live_mask[at_rank]
    visit_ids = jnp.concatenate([ranked[:, 0], ranked[:, 1]])
    visit_live = jnp.concatenate([ranked_live, ranked_live])
    one_hot = (visit_ids[:, None] == jnp.arange(experts, dtype=jnp.int32)[None, :]).astype(jnp.int32) * visit_live[:, None]
    position = lax.optimization_barrier(jnp.sum(jnp.cumsum(one_hot, axis=0) * one_hot, axis=1)) - 1
    slot_visit = jnp.where((visit_live > 0) & (position < capacity), position, capacity).astype(jnp.int32)
    by_rank = jnp.stack([slot_visit[:count_tok], slot_visit[count_tok:]], axis=1)
    return by_rank[priority_row]

def moe_block(weights_f32, pieces):
    gain_one, shift_one, w_qkv, b_qv, w_o, b_o, gain_two, shift_two, w_router, w_in, b_in, w_out, b_out = weights_f32
    tokens_dev, segment, live_mask, expert_list, slot_index = pieces
    count_tok = tokens_dev.shape[0]
    sequences = count_tok // SLOTS
    head_scale = HEAD ** (-0.5)
    normed_in = low(layer_norm(tokens_dev, gain_one, shift_one))
    qkv = matmul(normed_in, w_qkv)
    queries = low(low_back(qkv[:, :D] + b_qv[:D]))
    key_rows = low(low_back(qkv[:, D:2 * D]))
    value_rows = low(low_back(qkv[:, 2 * D:] + b_qv[D:]))

    @jax.checkpoint
    def attention(seq_pieces):
        query_seq, key_seq, value_seq, segment_seq, live_seq = seq_pieces
        raw_scores = low_back(contract('qhd,khd->hqk', split_heads(query_seq), split_heads(key_seq)) * head_scale)
        masked = jnp.where(allowed_pairs(segment_seq, live_seq)[None], raw_scores, -1e+30)
        softmaxed = jax.nn.softmax(masked, axis=-1)
        return contract('hqk,khd->qhd', low(softmaxed), split_heads(value_seq)).reshape(SLOTS, D)

    def per_seq(tensor):
        return tensor.reshape((sequences, SLOTS) + tensor.shape[1:])
    mixed = lax.map(attention, (per_seq(queries), per_seq(key_rows), per_seq(value_rows), per_seq(segment), per_seq(live_mask)))
    mixed = low(low_back(mixed.reshape(count_tok, D)))
    attn_out = low_back(matmul(mixed, w_o) + b_o)
    middle = tokens_dev + attn_out
    routed = low(layer_norm(middle, gain_two, shift_two))
    logits = low_back(matmul(routed, w_router))
    gate_probs = jax.nn.softmax(logits, axis=-1)
    chosen = jnp.take_along_axis(gate_probs, expert_list, axis=1)
    flat_index = jnp.where(slot_index < CAP, expert_list * CAP + slot_index, EXPERTS * CAP).reshape(-1)
    dispatched = jnp.zeros((EXPERTS * CAP + 1, D), jnp.float32).at[flat_index].add(jnp.repeat(routed, 2, axis=0))
    buffer_rows = low_back(dispatched[:-1].reshape(EXPERTS, CAP, D))
    pre_act = low_back(contract('ecd,edf->ecf', buffer_rows, w_in) + b_in[:, None, :])
    hidden = low(jax.nn.gelu(pre_act, approximate=False))
    expert_out = low(low_back(contract('ecf,efd->ecd', hidden, w_out) + b_out[:, None, :]))
    expert_table = jnp.concatenate([expert_out.reshape(EXPERTS * CAP, D), jnp.zeros((1, D), jnp.float32)])
    picked = expert_table[flat_index].reshape(count_tok, 2, D)
    return middle + lax.optimization_barrier(jnp.sum(chosen[:, :, None] * picked, axis=1))

def reference(tokens, cotangent, segment_ids, pad_mask, expert_ids, priority, ln1_gain, ln1_shift, w_qkv, b_qv, w_o, b_o, ln2_gain, ln2_shift, w_router, w_in, b_in, w_out, b_out):
    groups = priority.shape[0]
    live_all = pad_mask.reshape(groups, TOK_DEV)
    expert_all = expert_ids.reshape(groups, TOK_DEV, 2)
    slot_all = jax.vmap(partial(make_slots, experts=EXPERTS, capacity=CAP))(expert_all, priority, live_all)
    weights_f32 = jax.tree.map(lambda item: item.astype(jnp.float32), (ln1_gain, ln1_shift, w_qkv, b_qv, w_o, b_o, ln2_gain, ln2_shift, w_router, w_in, b_in, w_out, b_out))
    fixed_inputs = (segment_ids.reshape(groups, TOK_DEV), live_all, expert_all, slot_all)

    def forward(weight_set, tokens_all):

        @jax.checkpoint
        def device_step(state_carry, pieces):
            return (state_carry, moe_block(weight_set, pieces))
        _, outputs = lax.scan(device_step, jnp.zeros((), jnp.float32), (tokens_all,) + fixed_inputs)
        return outputs
    result, pullback = jax.vjp(forward, weights_f32, tokens.astype(jnp.float32).reshape(groups, TOK_DEV, D))
    weight_grads, d_tokens = pullback(cotangent.astype(jnp.float32).reshape(groups, TOK_DEV, D))
    return (result.reshape(TOKENS, D).astype(jnp.bfloat16), d_tokens.reshape(TOKENS, D), weight_grads[0], weight_grads[1], weight_grads[2], weight_grads[3], weight_grads[4], weight_grads[5], weight_grads[6], weight_grads[7], weight_grads[8], weight_grads[9], weight_grads[10], weight_grads[11], weight_grads[12])
```

```python
import functools

import jax
import jax.numpy as jnp
from jax import lax
from jax.experimental import pallas as pl
from jax.experimental.pallas import tpu as pltpu
from jax.sharding import PartitionSpec as P

MESH = pl.DeviceIdType.MESH
BF16 = jnp.bfloat16
F32 = jnp.float32
SLOTS = 720
WIDTH = 512
PAIRS = 4
EPS = 1e-06
WINDOWS = ((0, 384), (96, 624), (336, 720))
QBLK = 240
KWIN = 528
ROWBLK = 240


def nt(left, right):
    return lax.dot_general(left, right, (((1,), (1,)), ((), ())), preferred_element_type=F32)


def tn(left, right):
    return lax.dot_general(left, right, (((0,), (0,)), ((), ())), preferred_element_type=F32)


def nn(left, right):
    return jnp.dot(left, right, preferred_element_type=F32)


def normalize(value):
    centred = value - jnp.mean(value, axis=-1, keepdims=True)
    inv_std = lax.rsqrt(jnp.mean(centred * centred, axis=-1, keepdims=True) + EPS)
    return centred * inv_std, inv_std


def aligned(index, size):
    return pl.ds(pl.multiple_of(index * size, size), size)


class Place:
    def __init__(self, n_f, n_d):
        self.n_f, self.n_d, self.n_x = n_f, n_d, n_d // 2
        self.me = lax.axis_index("fsdp")
        self.d = lax.axis_index("dp")
        self.x = lax.div(self.d, 2)
        self.core = lax.rem(self.d, 2)

    def ahead(self, k):
        return lax.rem(self.me + k, self.n_f)

    def fsdp_peer(self, k):
        return (self.d, self.ahead(k))

    def x_index(self, i):
        return lax.rem(self.x + i, self.n_x)

    def x_peer(self, i):
        return (self.x_index(i) * 2 + self.core, self.me)

    def partner(self):
        return (self.x * 2 + 1 - self.core, self.me)

    def enter(self):
        bar = pltpu.get_barrier_semaphore()

        def greet(k, _):
            pl.semaphore_signal(bar, inc=1, device_id=self.fsdp_peer(k), device_id_type=MESH)
            return 0

        lax.fori_loop(1, self.n_f, greet, 0)
        for i in range(1, self.n_x):
            pl.semaphore_signal(bar, inc=1, device_id=self.x_peer(i), device_id_type=MESH)
        pl.semaphore_signal(bar, inc=1, device_id=self.partner(), device_id_type=MESH)
        pl.semaphore_wait(bar, self.n_f - 1 + self.n_x - 1 + 1)


def remote(src, dst, send_sem, recv_sem, device):
    return pltpu.make_async_remote_copy(
        src_ref=src,
        dst_ref=dst,
        send_sem=send_sem,
        recv_sem=recv_sem,
        device_id=device,
        device_id_type=MESH,
    )


def loop(low, high, body):
    def step(k, carry):
        body(k)
        return carry

    lax.fori_loop(low, high, step, 0)


def front_kernel(
    n_f,
    n_d,
    experts,
    cap,
    cap_rows,
    tok,
    cot,
    cols,
    rows,
    wsh,
    vsh,
    x_out,
    g_out,
    p_out,
    qkv_out,
    mix_out,
    mid_out,
    w_out,
    v_out,
    place_out,
    wfull,
    vall,
    vecs,
    bias,
    scores,
    probs,
    qkv,
    normed,
    mixed,
    middle,
    routed,
    place,
    send_x,
    send_g,
    s_w,
    r_w,
    s_v,
    r_v,
    s_dx,
    r_dx,
    s_dc,
    r_dc,
    s_g,
    r_g,
    s_x,
    r_x,
    s_own,
    s_out,
):
    at = Place(n_f, n_d)
    shard = WIDTH // n_f
    colw = wsh.shape[1] // n_d

    def cols_of(d):
        return aligned(d, colw)

    def w_piece(owner, d):
        return wfull.at[aligned(owner, shard), cols_of(d)]

    at.enter()

    def send_w(k):
        return remote(
            wsh.at[:, cols_of(at.d)], w_piece(at.me, at.d), s_w.at[k], r_w.at[k], at.fsdp_peer(k)
        )

    def send_v(k):
        return remote(vsh, vall.at[at.me], s_v.at[k], r_v.at[k], at.fsdp_peer(k))

    def share_x(i, k):
        piece = w_piece(at.ahead(n_f - k), at.d)
        return remote(piece, piece, s_dx.at[i - 1, k], r_dx.at[i - 1, k], at.x_peer(i))

    def share_core(i, k):
        piece = w_piece(at.ahead(n_f - k), at.x_index(at.n_x - i) * 2 + at.core)
        return remote(piece, piece, s_dc.at[i, k], r_dc.at[i, k], at.partner())

    loop(1, n_f, lambda k: send_v(k).start())
    loop(1, n_f, lambda k: send_w(k).start())
    wfull[aligned(at.me, shard), :] = wsh[...]
    vall[at.me] = vsh[...]

    lane_e = lax.broadcasted_iota(jnp.int32, (SLOTS, experts), 1)
    sub_e = lax.broadcasted_iota(jnp.int32, (experts, SLOTS), 0)
    live_c, live_r = cols[:, 1:2] > 0, rows[1:2, :] > 0
    pri_c, pri_r = cols[:, 4:5], rows[4:5, :]
    first_c = [jnp.where((cols[:, 2 + k : 3 + k] == lane_e) & live_c, 1.0, 0.0) for k in range(2)]
    first_r = [jnp.where((rows[2 + k : 3 + k, :] == sub_e) & live_r, 1.0, 0.0) for k in range(2)]
    before_c = jnp.where(pri_r < pri_c, 1.0, 0.0).astype(BF16)
    before_r = jnp.where(pri_c < pri_r, 1.0, 0.0).astype(BF16)
    rank_c = [nn(before_c, hot.astype(BF16)) for hot in first_c]
    rank_r = [nn(hot.astype(BF16), before_r) for hot in first_r]
    rank_c[1] = rank_c[1] + jnp.sum(first_c[0], axis=0, keepdims=True)
    rank_r[1] = rank_r[1] + jnp.sum(first_r[0], axis=1, keepdims=True)
    spot_c, spot_r = [], []
    for k in range(2):
        slot = jnp.sum(first_c[k] * rank_c[k], axis=1, keepdims=True)
        spot = cols[:, 2 + k : 3 + k].astype(F32) * cap_rows + slot
        spot_c.append(jnp.where(live_c & (slot < cap), spot, -1.0))
        slot = jnp.sum(first_r[k] * rank_r[k], axis=0, keepdims=True)
        spot = rows[2 + k : 3 + k, :].astype(F32) * cap_rows + slot
        spot_r.append(jnp.where(live_r & (slot < cap), spot, -1.0))
        place[:, k : k + 1] = spot_c[k]
    slot_iota = lax.broadcasted_iota(jnp.int32, (cap_rows, SLOTS), 0)

    def pick(expert):
        mine = (slot_iota + expert * cap_rows).astype(F32)
        return jnp.where((mine == spot_r[0]) | (mine == spot_r[1]), 1.0, 0.0).astype(BF16)

    for b, (low, high) in enumerate(WINDOWS):
        queries = slice(b * QBLK, (b + 1) * QBLK)
        shape = (high - low, QBLK)
        same = cols[low:high, 0:1] == rows[0:1, queries]
        itself = (lax.broadcasted_iota(jnp.int32, shape, 0) + low) == (
            lax.broadcasted_iota(jnp.int32, shape, 1) + b * QBLK
        )
        allowed = same & ((cols[low:high, 1:2] > 0) | itself)
        bias[b, : high - low, :] = jnp.where(allowed, 0.0, -1e30)

    loop(1, n_f, lambda k: send_v(k).wait_recv())
    total = vall[0].astype(F32)
    for owner in range(1, n_f):
        total = total + vall[owner].astype(F32)
    vecs[...] = total

    def first_norm(i):
        block = aligned(i, ROWBLK)
        value, _ = normalize(tok[block, :].astype(F32))
        normed[block, :] = (value * vecs[0:1, :] + vecs[1:2, :]).astype(BF16)

    loop(0, SLOTS // ROWBLK, first_norm)

    def pass_on(k):
        send_w(k).wait_recv()
        for i in range(1, at.n_x):
            share_x(i, k).start()
        share_core(0, k).start()

    loop(1, n_f, pass_on)

    def send_rows(buffer, out, send, recv, k):
        expert = at.ahead(k)
        return remote(
            buffer.at[aligned(expert, cap_rows), :],
            out.at[n_f - k],
            send.at[k],
            recv.at[n_f - k],
            at.fsdp_peer(k),
        )

    def own_rows(buffer, out, sem):
        return pltpu.make_async_copy(buffer.at[aligned(at.me, cap_rows), :], out.at[0], sem)

    def dispatch_g(k):
        expert = at.ahead(k)
        send_g[aligned(expert, cap_rows), :] = nn(pick(expert), cot[...]).astype(BF16)
        send_rows(send_g, g_out, s_g, r_g, k).start()

    loop(1, n_f, dispatch_g)
    send_g[aligned(at.me, cap_rows), :] = nn(pick(at.me), cot[...]).astype(BF16)
    own_rows(send_g, g_out, s_own.at[0]).start()

    for i in range(1, at.n_x):

        def cross(k, i=i):
            piece = w_piece(at.ahead(n_f - k), at.x_index(at.n_x - i) * 2 + at.core)
            remote(piece, piece, s_dx.at[i - 1, k], r_dx.at[i - 1, k], at.x_peer(i)).wait_recv()
            share_core(i, k).start()

        loop(1, n_f, cross)
    for i in range(at.n_x):

        def arrive(k, i=i):
            piece = w_piece(at.ahead(n_f - k), at.x_index(at.n_x - i) * 2 + 1 - at.core)
            remote(piece, piece, s_dc.at[i, k], r_dc.at[i, k], at.partner()).wait_recv()

        loop(1, n_f, arrive)
    copies = [
        pltpu.make_async_copy(wfull, w_out, s_out.at[0]),
        pltpu.make_async_copy(vecs, v_out, s_out.at[1]),
        pltpu.make_async_copy(place, place_out, s_out.at[2]),
    ]
    for copy in copies:
        copy.start()

    bias_row = [vecs[2:3, :], jnp.zeros((1, WIDTH), F32), vecs[3:4, :]]
    for part in range(3):
        for half in range(2):
            low = part * WIDTH + half * 256
            out = nn(normed[...], wfull[:, low : low + 256])
            out = out + bias_row[part][:, half * 256 : half * 256 + 256]
            if part == 0:
                out = out * 0.125
            for j in range(2):
                qkv[part * PAIRS + half * 2 + j] = out[:, j * 128 : j * 128 + 128].astype(BF16)
    copies.append(pltpu.make_async_copy(qkv, qkv_out, s_out.at[3]))
    copies[-1].start()

    lane = lax.broadcasted_iota(jnp.int32, (1, 128), 1)
    halves = (lane < 64, lane >= 64)

    def attend(pair):
        for b, (low, high) in enumerate(WINDOWS):
            query = qkv[pair, b * QBLK : (b + 1) * QBLK, :]
            keys = qkv[PAIRS + pair, low:high, :]
            for h in range(2):
                one = jnp.where(halves[h], query, jnp.zeros_like(query))
                scores[b, h, : high - low, :] = nt(keys, one) + bias[b, : high - low, :]
        for b, (low, high) in enumerate(WINDOWS):
            for h in range(2):
                value = scores[b, h, : high - low, :]
                power = jnp.exp(value - jnp.max(value, axis=0, keepdims=True))
                share = 1.0 / jnp.sum(power, axis=0, keepdims=True)
                probs[2 * pair + h, b, : high - low, :] = (power * share).astype(BF16)
        for b, (low, high) in enumerate(WINDOWS):
            values = qkv[2 * PAIRS + pair, low:high, :]
            both = [tn(probs[2 * pair + h, b, : high - low, :], values) for h in range(2)]
            mixed[b * QBLK : (b + 1) * QBLK, aligned(pair, 128)] = jnp.where(
                halves[0], both[0], both[1]
            ).astype(BF16)

    loop(0, PAIRS, attend)
    copies.append(pltpu.make_async_copy(probs, p_out, s_out.at[4]))
    copies[-1].start()
    copies.append(pltpu.make_async_copy(mixed, mix_out, s_out.at[5]))
    copies[-1].start()

    def second_norm(i):
        block = aligned(i, ROWBLK)
        total = nn(mixed[block, :], wfull[:, 3 * WIDTH : 4 * WIDTH])
        total = tok[block, :].astype(F32) + total + vecs[4:5, :]
        middle[block, :] = total
        value, _ = normalize(total)
        routed[block, :] = (value * vecs[5:6, :] + vecs[6:7, :]).astype(BF16)

    loop(0, SLOTS // ROWBLK, second_norm)
    copies.append(pltpu.make_async_copy(middle, mid_out, s_out.at[6]))
    copies[-1].start()

    def dispatch_x(k):
        expert = at.ahead(k)
        send_x[aligned(expert, cap_rows), :] = nn(pick(expert), routed[...]).astype(BF16)
        send_rows(send_x, x_out, s_x, r_x, k).start()

    loop(1, n_f, dispatch_x)
    send_x[aligned(at.me, cap_rows), :] = nn(pick(at.me), routed[...]).astype(BF16)
    own_rows(send_x, x_out, s_own.at[1]).start()

    for copy in copies:
        copy.wait()
    own_rows(send_g, g_out, s_own.at[0]).wait()
    own_rows(send_x, x_out, s_own.at[1]).wait()

    def sent(k):
        send_v(k).wait_send()
        send_w(k).wait_send()
        for i in range(1, at.n_x):
            share_x(i, k).wait_send()
        for i in range(at.n_x):
            share_core(i, k).wait_send()

    loop(1, n_f, sent)
    loop(1, n_f, lambda k: send_rows(send_g, g_out, s_g, r_g, k).wait())
    loop(1, n_f, lambda k: send_rows(send_x, x_out, s_x, r_x, k).wait())


def front(n_f, n_d, experts, cap, cap_rows, tok, cot, cols, rows, wsh, vsh):
    vmem = pl.BlockSpec(memory_space=pltpu.VMEM)
    hbm = pl.BlockSpec(memory_space=pl.ANY)
    n_x = n_d // 2
    vec_rows = vsh.shape[0]
    sds = jax.ShapeDtypeStruct
    dma = pltpu.SemaphoreType.DMA
    return pl.pallas_call(
        functools.partial(front_kernel, n_f, n_d, experts, cap, cap_rows),
        out_shape=(
            sds((n_f, cap_rows, WIDTH), BF16),
            sds((n_f, cap_rows, WIDTH), BF16),
            sds((2 * PAIRS, 3, KWIN, QBLK), BF16),
            sds((3 * PAIRS, SLOTS, 128), BF16),
            sds((SLOTS, WIDTH), BF16),
            sds((SLOTS, WIDTH), F32),
            sds((WIDTH, 4 * WIDTH), BF16),
            sds((vec_rows, WIDTH), F32),
            sds((SLOTS, 2), F32),
        ),
        in_specs=[vmem] * 6,
        out_specs=[hbm] * 9,
        scratch_shapes=[
            pltpu.VMEM((WIDTH, 4 * WIDTH), BF16),
            pltpu.VMEM((n_f, vec_rows, WIDTH), BF16),
            pltpu.VMEM((vec_rows, WIDTH), F32),
            pltpu.VMEM((3, KWIN, QBLK), F32),
            pltpu.VMEM((3, 2, KWIN, QBLK), F32),
            pltpu.VMEM((2 * PAIRS, 3, KWIN, QBLK), BF16),
            pltpu.VMEM((3 * PAIRS, SLOTS, 128), BF16),
            pltpu.VMEM((SLOTS, WIDTH), BF16),
            pltpu.VMEM((SLOTS, WIDTH), BF16),
            pltpu.VMEM((SLOTS, WIDTH), F32),
            pltpu.VMEM((SLOTS, WIDTH), BF16),
            pltpu.VMEM((SLOTS, 2), F32),
            pltpu.VMEM((n_f * cap_rows, WIDTH), BF16),
            pltpu.VMEM((n_f * cap_rows, WIDTH), BF16),
            dma((n_f,)),
            dma((n_f,)),
            dma((n_f,)),
            dma((n_f,)),
            dma((max(n_x - 1, 1), n_f)),
            dma((max(n_x - 1, 1), n_f)),
            dma((n_x, n_f)),
            dma((n_x, n_f)),
            dma((n_f,)),
            dma((n_f,)),
            dma((n_f,)),
            dma((n_f,)),
            dma((2,)),
            dma((7,)),
        ],
        compiler_params=pltpu.CompilerParams(
            collective_id=0, has_side_effects=True, vmem_limit_bytes=48 << 20
        ),
        name="front",
    )(tok, cot, cols, rows, wsh, vsh)


def spread(vector, n_f, me):
    size = vector.shape[-1]
    whole = jnp.tile(vector, (1,) * (vector.ndim - 1) + (n_f,))
    return jnp.where(jnp.arange(size * n_f) // size == me, whole, jnp.zeros_like(whole))


def norm_back(grad_in, normed, inv_std, gain_vec):
    scaled = grad_in * gain_vec
    corrected = (
        scaled
        - jnp.mean(scaled, axis=-1, keepdims=True)
        - normed * jnp.mean(scaled * normed, axis=-1, keepdims=True)
    )
    return (inv_std * corrected, jnp.sum(grad_in * normed, axis=0), jnp.sum(grad_in, axis=0))


def shards(
    tokens,
    cotangent,
    segment_ids,
    pad_mask,
    expert_ids,
    priority,
    ln1_gain,
    ln1_shift,
    w_qkv,
    b_qv,
    w_o,
    b_o,
    ln2_gain,
    ln2_shift,
    w_router,
    w_in,
    b_in,
    w_out,
    b_out,
    n_f,
    n_d,
):
    me = lax.axis_index("fsdp")
    count_tok = tokens.shape[0]
    experts = w_router.shape[1]
    cap = (21 * count_tok + 10 * experts - 1) // (10 * experts)
    cap_rows = -(-cap // 16) * 16
    zero_row = jnp.zeros_like(segment_ids)
    rows = jnp.stack(
        [segment_ids, pad_mask, expert_ids[:, 0], expert_ids[:, 1], priority[0]] + [zero_row] * 3
    )
    cols = rows.T
    wsh = jnp.concatenate([w_qkv, w_o], axis=1)
    whole = functools.partial(spread, n_f=n_f, me=me)
    vec_rows = -(-(8 + experts) // 16) * 16
    vsh = jnp.concatenate(
        [
            whole(ln1_gain)[None],
            whole(ln1_shift)[None],
            whole(b_qv).reshape(2, WIDTH),
            whole(b_o)[None],
            whole(ln2_gain)[None],
            whole(ln2_shift)[None],
            jnp.zeros((1, WIDTH), BF16),
            whole(w_router.T),
            jnp.zeros((vec_rows - 8 - experts, WIDTH), BF16),
        ]
    )
    x_in, g_in, probs, qkv, mixed, middle, wfull, vecs, place = front(
        n_f, n_d, experts, cap, cap_rows, tokens, cotangent, cols, rows, wsh, vsh
    )
    router = vecs[8 : 8 + experts].astype(BF16)
    x = x_in.reshape(-1, WIDTH)
    g = g_in.reshape(-1, WIDTH).astype(F32)
    gates = jax.nn.softmax(nt(x, router), axis=-1)
    hot = (jnp.arange(experts) == me).astype(F32)
    chosen = jnp.sum(gates * hot, axis=-1, keepdims=True)
    pre = nn(x, w_in[0]) + b_in[0].astype(F32)
    act, gelu_back = jax.vjp(functools.partial(jax.nn.gelu, approximate=False), pre)
    act = act.astype(BF16)
    result = nn(act, w_out[0]) + b_out[0].astype(F32)
    d_result = (chosen * g).astype(BF16)
    d_chosen = jnp.sum(g * result, axis=-1, keepdims=True)
    d_logits = (d_chosen * chosen * (hot - gates)).astype(BF16)
    d_pre = gelu_back(nt(d_result, w_out[0]))[0].astype(BF16)
    d_rows = nt(d_pre, w_in[0]) + nn(d_logits, router)
    d_w_in = tn(x, d_pre)
    d_w_out = tn(act, d_result)
    d_b_in = jnp.sum(d_pre.astype(F32), axis=0)
    d_b_out = jnp.sum(d_result.astype(F32), axis=0)
    d_router_t = tn(d_logits, x)

    def back(value):
        value = value.astype(BF16).reshape(n_f, cap_rows, WIDTH)
        value = jnp.roll(value, me, axis=0)
        return lax.all_to_all(value, "fsdp", split_axis=0, concat_axis=0, tiled=True).reshape(
            -1, WIDTH
        )

    table_d = back(d_rows)
    table_o = back(chosen * result)
    lanes = jnp.arange(n_f * cap_rows).astype(F32)[None]
    picks = ((lanes == place[:, 0:1]) | (lanes == place[:, 1:2])).astype(BF16)
    output = (middle + nn(picks, table_o)).astype(BF16)
    d_routed = nn(picks, table_d)
    norm_two, inv_two = normalize(middle)
    grads = cotangent.astype(F32)
    d_mid, d_g2, d_s2 = norm_back(d_routed, norm_two, inv_two, vecs[5:6])
    d_middle = grads + d_mid
    d_attn = d_middle.astype(BF16)
    d_w_o = tn(mixed, d_attn)
    d_b_o = jnp.sum(d_attn.astype(F32), axis=0)
    d_mixed = nt(d_attn, wfull[:, 3 * WIDTH :]).astype(BF16)
    d_parts = [[], [], []]
    for pair in range(PAIRS):
        for h in range(2):
            dq, dk, dv = [], jnp.zeros((SLOTS, 64), F32), jnp.zeros((SLOTS, 64), F32)
            take = slice(h * 64, h * 64 + 64)
            for b, (low, high) in enumerate(WINDOWS):
                qs = slice(b * QBLK, (b + 1) * QBLK)
                p = probs[2 * pair + h, b, : high - low, :]
                do = d_mixed[qs, pair * 128 + h * 64 : pair * 128 + h * 64 + 64]
                dp = nt(qkv[8 + pair, low:high, take], do)
                t = p.astype(F32) * dp
                ds = (t - p.astype(F32) * jnp.sum(t, axis=0, keepdims=True)).astype(BF16)
                dq.append(tn(ds, qkv[4 + pair, low:high, take]) * 0.125)
                dk = dk.at[low:high].add(nn(ds, qkv[pair, qs, take]))
                dv = dv.at[low:high].add(nn(p, do))
            d_parts[0].append(jnp.concatenate(dq, axis=0))
            d_parts[1].append(dk)
            d_parts[2].append(dv)
    d_qkv = jnp.concatenate(d_parts[0] + d_parts[1] + d_parts[2], axis=1).astype(BF16)
    norm_one, inv_one = normalize(tokens.astype(F32))
    normed = (norm_one * vecs[0:1] + vecs[1:2]).astype(BF16)
    d_w_qkv = tn(normed, d_qkv)
    sums = jnp.sum(d_qkv.astype(F32), axis=0)
    d_b_qv = jnp.concatenate([sums[:WIDTH], sums[2 * WIDTH :]])
    d_normed = nt(d_qkv, wfull[:, : 3 * WIDTH])
    d_in, d_g1, d_s1 = norm_back(d_normed, norm_one, inv_one, vecs[0:1])
    d_tokens = d_middle + d_in

    def spread_sum(value):
        value = lax.psum_scatter(value.astype(BF16), "fsdp", scatter_dimension=0, tiled=True)
        return lax.psum(value, "dp").astype(F32)

    def batch_sum(value):
        return lax.psum(value.astype(BF16), "dp").astype(F32)[None]

    return (
        output,
        d_tokens,
        spread_sum(d_g1),
        spread_sum(d_s1),
        spread_sum(d_w_qkv),
        spread_sum(d_b_qv),
        spread_sum(d_w_o),
        spread_sum(d_b_o),
        spread_sum(d_g2),
        spread_sum(d_s2),
        spread_sum(d_router_t.T),
        batch_sum(d_w_in),
        batch_sum(d_b_in),
        batch_sum(d_w_out),
        batch_sum(d_b_out),
    )


def solution(mesh):
    both, one = P(("dp", "fsdp")), P("fsdp")
    n_f, n_d = mesh.shape["fsdp"], mesh.shape["dp"]
    return jax.shard_map(
        functools.partial(shards, n_f=n_f, n_d=n_d),
        mesh=mesh,
        in_specs=(both,) * 6 + (one,) * 13,
        out_specs=(both,) * 2 + (one,) * 13,
        check_vma=False,
    )
```

```python
import functools

import jax
import jax.numpy as jnp
from jax import lax
from jax.experimental import pallas as pl
from jax.experimental.pallas import tpu as pltpu
from jax.sharding import PartitionSpec as P

MESH = pl.DeviceIdType.MESH
BF16 = jnp.bfloat16
F32 = jnp.float32
SLOTS = 720
WIDTH = 512
PAIRS = 4
EPS = 1e-06
WINDOWS = ((0, 384, 0), (96, 624, 384), (336, 720, 912))
KEYS = 1296
QBLK = 240
ROWBLK = 240
TILE = 128
FTILE = 512
CHUNKS = 4


def nt(left, right):
    return lax.dot_general(left, right, (((1,), (1,)), ((), ())), preferred_element_type=F32)


def tn(left, right):
    return lax.dot_general(left, right, (((0,), (0,)), ((), ())), preferred_element_type=F32)


def nn(left, right):
    return jnp.dot(left, right, preferred_element_type=F32)


def normalize(value):
    centred = value - jnp.mean(value, axis=-1, keepdims=True)
    inv_std = lax.rsqrt(jnp.mean(centred * centred, axis=-1, keepdims=True) + EPS)
    return centred * inv_std, inv_std


def aligned(index, size):
    return pl.ds(pl.multiple_of(index * size, size), size)


class Place:
    def __init__(self, n_f, n_d):
        self.n_f, self.n_d, self.n_x = n_f, n_d, n_d // 2
        self.me = lax.axis_index("fsdp")
        self.d = lax.axis_index("dp")
        self.x = lax.div(self.d, 2)
        self.core = lax.rem(self.d, 2)

    def ahead(self, k):
        return lax.rem(self.me + k, self.n_f)

    def fsdp_peer(self, k):
        return (self.d, self.ahead(k))

    def x_index(self, i):
        return lax.rem(self.x + i, self.n_x)

    def x_peer(self, i):
        return (self.x_index(i) * 2 + self.core, self.me)

    def partner(self):
        return (self.x * 2 + 1 - self.core, self.me)

    def dp_peer(self, i):
        return (lax.rem(self.d + i, self.n_d), self.me)

    def enter(self):
        bar = pltpu.get_barrier_semaphore()

        def greet(k, _):
            pl.semaphore_signal(bar, inc=1, device_id=self.fsdp_peer(k), device_id_type=MESH)
            return 0

        lax.fori_loop(1, self.n_f, greet, 0)
        for i in range(1, self.n_d):
            pl.semaphore_signal(bar, inc=1, device_id=self.dp_peer(i), device_id_type=MESH)
        pl.semaphore_wait(bar, self.n_f - 1 + self.n_d - 1)


def remote(src, dst, send_sem, recv_sem, device):
    return pltpu.make_async_remote_copy(
        src_ref=src,
        dst_ref=dst,
        send_sem=send_sem,
        recv_sem=recv_sem,
        device_id=device,
        device_id_type=MESH,
    )


def loop(low, high, body):
    def step(k, carry):
        body(k)
        return carry

    lax.fori_loop(low, high, step, 0)


def block_kernel(
    n_f,
    n_d,
    experts,
    cap,
    cap_rows,
    tok,
    cot,
    cols,
    rows,
    wsh,
    vsh,
    w_in_hbm,
    w_out_hbm,
    b_in,
    b_out,
    o_out,
    o_tokens,
    o_expert,
    o_dense,
    o_vec,
    o_qv,
    o_bias,
    wfull,
    vecs,
    bias,
    scores,
    probs,
    qkv,
    normed,
    mixed,
    middle,
    routed,
    place,
    send_x,
    send_g,
    x_in,
    g_in,
    w_in,
    w_out,
    hidden,
    d_pre,
    ret_d,
    ret_o,
    table_d,
    ew,
    ew_core,
    ew_x,
    dense_core,
    dense_x,
    dense_f,
    final,
    pack,
    pack_dp,
    vec_f,
    qv_f,
    d_middle,
    s_w,
    r_w,
    s_v,
    r_v,
    s_dx,
    r_dx,
    s_dc,
    r_dc,
    s_g,
    r_g,
    s_x,
    r_x,
    s_d,
    r_d,
    s_o,
    r_o,
    s_ec,
    r_ec,
    s_ex,
    r_ex,
    s_ea,
    r_ea,
    s_eb,
    r_eb,
    s_gc,
    r_gc,
    s_gx,
    r_gx,
    s_gf,
    r_gf,
    s_gd,
    r_gd,
    s_p,
    r_p,
    s_vf,
    r_vf,
    s_qf,
    r_qf,
    s_own,
    ready,
):
    at = Place(n_f, n_d)
    n_x = at.n_x
    shard = WIDTH // n_f
    colw = wsh.shape[1] // n_d
    other = 1 - at.core

    def cols_of(d):
        return aligned(d, colw)

    def w_piece(owner, d):
        return wfull.at[aligned(owner, shard), cols_of(d)]

    def x_back(i):
        return at.x_index(n_x - i)

    load_in = pltpu.make_async_copy(w_in_hbm, w_in, s_own.at[0])
    load_out = pltpu.make_async_copy(w_out_hbm, w_out, s_own.at[1])
    load_in.start()
    load_out.start()
    at.enter()

    def send_w(k):
        return remote(
            wsh.at[:, cols_of(at.d)], w_piece(at.me, at.d), s_w.at[k], r_w.at[k], at.fsdp_peer(k)
        )

    vec_rows = vsh.shape[0]

    def vec_piece(owner):
        return hidden.at[aligned(owner, vec_rows), 0:WIDTH]

    def send_v(k):
        return remote(vsh, vec_piece(at.me), s_v.at[k], r_v.at[k], at.fsdp_peer(k))

    def share_x(i, k):
        piece = w_piece(at.ahead(n_f - k), at.d)
        return remote(piece, piece, s_dx.at[i - 1, k], r_dx.at[i - 1, k], at.x_peer(i))

    def share_core(i, k):
        piece = w_piece(at.ahead(n_f - k), x_back(i) * 2 + at.core)
        return remote(piece, piece, s_dc.at[i, k], r_dc.at[i, k], at.partner())

    loop(1, n_f, lambda k: send_v(k).start())
    loop(1, n_f, lambda k: send_w(k).start())
    wfull[aligned(at.me, shard), :] = wsh[...]
    vec_piece(at.me)[...] = vsh[...]

    expert_iota = lax.broadcasted_iota(jnp.int32, (experts, SLOTS), 0)
    live = rows[1:2, :] > 0
    before = jnp.where(cols[:, 4:5] < rows[4:5, :], 1.0, 0.0).astype(BF16)
    chose = [
        jnp.where((rows[2 + k : 3 + k, :] == expert_iota) & live, 1.0, 0.0) for k in range(2)
    ]
    rank = [nn(one.astype(BF16), before) for one in chose]
    rank[1] = rank[1] + jnp.sum(chose[0], axis=1, keepdims=True)
    spot_r = []
    for k in range(2):
        slot = jnp.sum(chose[k] * rank[k], axis=0, keepdims=True)
        spot = rows[2 + k : 3 + k, :].astype(F32) * cap_rows + slot
        spot_r.append(jnp.where(live & (slot < cap), spot, -1.0))
    place[...] = jnp.transpose(jnp.concatenate(spot_r + [jnp.zeros((6, SLOTS), F32)], axis=0))
    slot_iota = lax.broadcasted_iota(jnp.int32, (cap_rows, SLOTS), 0)

    def pick(expert):
        mine = (slot_iota + expert * cap_rows).astype(F32)
        return jnp.where((mine == spot_r[0]) | (mine == spot_r[1]), 1.0, 0.0).astype(BF16)

    for b, (low, high, row) in enumerate(WINDOWS):
        queries = slice(b * QBLK, (b + 1) * QBLK)
        shape = (high - low, QBLK)
        same = cols[low:high, 0:1] == rows[0:1, queries]
        itself = (lax.broadcasted_iota(jnp.int32, shape, 0) + low) == (
            lax.broadcasted_iota(jnp.int32, shape, 1) + b * QBLK
        )
        allowed = same & ((cols[low:high, 1:2] > 0) | itself)
        bias[row : row + high - low, 0:QBLK] = jnp.where(allowed, 0.0, -1e30)

    loop(1, n_f, lambda k: send_v(k).wait_recv())
    vecs[...] = vec_piece(0)[...].astype(F32)

    def add_vectors(owner):
        vecs[...] += vec_piece(owner)[...].astype(F32)

    loop(1, n_f, add_vectors)

    def first_norm(i):
        block = aligned(i, ROWBLK)
        value, _ = normalize(tok[block, :].astype(F32))
        normed[block, :] = (value * vecs[0:1, :] + vecs[1:2, :]).astype(BF16)

    loop(0, SLOTS // ROWBLK, first_norm)

    def pass_on(k):
        send_w(k).wait_recv()
        for i in range(1, n_x):
            share_x(i, k).start()
        share_core(0, k).start()

    loop(1, n_f, pass_on)

    def order(step):
        return 1 + lax.rem(2 * n_f - 4 - step, n_f - 1)

    def send_rows(buffer, into, send, recv, k):
        return remote(
            buffer.at[aligned(at.ahead(k), cap_rows), :],
            into.at[aligned(n_f - k, cap_rows), :],
            send.at[k],
            recv.at[n_f - k],
            at.fsdp_peer(k),
        )

    def dispatch(source, buffer, into, send, recv):
        def one(step):
            k = order(step)
            expert = at.ahead(k)
            buffer[aligned(expert, cap_rows), :] = nn(pick(expert), source[...]).astype(BF16)
            send_rows(buffer, into, send, recv, k).start()

        loop(0, n_f - 1, one)
        into[0:cap_rows, :] = nn(pick(at.me), source[...]).astype(BF16)

    dispatch(cot, send_g, g_in, s_g, r_g)

    for i in range(1, n_x):

        def cross(k, i=i):
            piece = w_piece(at.ahead(n_f - k), x_back(i) * 2 + at.core)
            remote(piece, piece, s_dx.at[i - 1, k], r_dx.at[i - 1, k], at.x_peer(i)).wait_recv()
            share_core(i, k).start()

        loop(1, n_f, cross)
    for i in range(n_x):

        def arrive(k, i=i):
            piece = w_piece(at.ahead(n_f - k), x_back(i) * 2 + other)
            remote(piece, piece, s_dc.at[i, k], r_dc.at[i, k], at.partner()).wait_recv()

        loop(1, n_f, arrive)

    def project(pair):
        out = nn(normed[...], wfull[:, pl.ds(pl.multiple_of(pair * 384, 128), 384)])
        lanes = aligned(pair, TILE)
        qkv[pair] = ((out[:, 0:128] + vecs[2:3, lanes]) * 0.125).astype(BF16)
        qkv[PAIRS + pair] = out[:, 128:256].astype(BF16)
        qkv[2 * PAIRS + pair] = (out[:, 256:384] + vecs[3:4, lanes]).astype(BF16)

    loop(0, PAIRS, project)

    lane = lax.broadcasted_iota(jnp.int32, (1, TILE), 1)
    halves = (lane < 64, lane >= 64)

    def attend(pair):
        for b, (low, high, row) in enumerate(WINDOWS):
            window = slice(row, row + high - low)
            query = qkv[pair, b * QBLK : (b + 1) * QBLK, :]
            keys = qkv[PAIRS + pair, low:high, :]
            for h in range(2):
                one = jnp.where(halves[h], query, jnp.zeros_like(query))
                scores[h, window, :] = nt(keys, one) + bias[window, 0:QBLK]
        for b, (low, high, row) in enumerate(WINDOWS):
            window = slice(row, row + high - low)
            for h in range(2):
                value = scores[h, window, :]
                power = jnp.exp(value - jnp.max(value, axis=0, keepdims=True))
                share = 1.0 / jnp.sum(power, axis=0, keepdims=True)
                probs[2 * pair + h, window, :] = (power * share).astype(BF16)
        for b, (low, high, row) in enumerate(WINDOWS):
            window = slice(row, row + high - low)
            values = qkv[2 * PAIRS + pair, low:high, :]
            both = [tn(probs[2 * pair + h, window, :], values) for h in range(2)]
            mixed[b * QBLK : (b + 1) * QBLK, aligned(pair, TILE)] = jnp.where(
                halves[0], both[0], both[1]
            ).astype(BF16)

    loop(0, PAIRS, attend)

    def second_norm(i):
        block = aligned(i, ROWBLK)
        total = nn(mixed[block, :], wfull[:, 3 * WIDTH : 4 * WIDTH])
        total = tok[block, :].astype(F32) + total + vecs[4:5, :]
        middle[block, :] = total
        value, _ = normalize(total)
        routed[block, :] = (value * vecs[5:6, :] + vecs[6:7, :]).astype(BF16)

    loop(0, SLOTS // ROWBLK, second_norm)
    dispatch(routed, send_x, x_in, s_x, r_x)

    load_in.wait()
    load_out.wait()
    pack[...] = jnp.zeros_like(pack)
    router = vecs[8 : 8 + experts, :].astype(BF16)
    chunk_rows = n_f * cap_rows // CHUNKS
    sources = n_f // CHUNKS
    f_tiles = w_in.shape[1] // FTILE
    bias_at = 8 + experts
    hot = jnp.where(lax.broadcasted_iota(jnp.int32, (1, experts), 1) == at.me, 1.0, 0.0)

    def give_back(buffer, into, send, recv, r):
        return remote(
            buffer.at[aligned(r, cap_rows), :],
            into.at[aligned(at.me, cap_rows), :],
            send.at[r],
            recv.at[r],
            at.fsdp_peer(r),
        )

    acc_o, acc_d = d_middle.at[0:chunk_rows, :], d_middle.at[chunk_rows : 2 * chunk_rows, :]

    def expert_chunk(step):
        pos = lax.rem(step + 1, CHUNKS)
        block = aligned(pos, chunk_rows)
        first = pos * sources

        def arrive(r):
            @pl.when(r > 0)
            def _():
                send_rows(send_g, g_in, s_g, r_g, n_f - r).wait_recv()
                send_rows(send_x, x_in, s_x, r_x, n_f - r).wait_recv()

        loop(first, first + sources, arrive)
        x_rows = x_in[block, :]
        logits = nt(x_rows, router)
        gates = jnp.exp(logits - jnp.max(logits, axis=-1, keepdims=True))
        gates = gates / jnp.sum(gates, axis=-1, keepdims=True)
        chosen = jnp.sum(gates * hot, axis=-1, keepdims=True)
        g_rows = (chosen * g_in[block, :].astype(F32)).astype(BF16)
        g_in[block, :] = g_rows
        pack[bias_at + 4 : bias_at + 5, :] += jnp.sum(g_rows.astype(F32), axis=0, keepdims=True)
        acc_o[...] = jnp.broadcast_to(b_out[...].astype(F32), acc_o.shape)
        acc_d[...] = jnp.zeros_like(acc_d)
        def tile(f):
            lanes = aligned(f, FTILE)
            pre = nn(x_in[block, :], w_in[:, lanes]) + b_in[:, lanes].astype(F32)
            d_act = nt(g_in[block, :], w_out[lanes, :])
            cdf = 0.5 + 0.5 * lax.erf(pre * 0.7071067811865476)
            act = (pre * cdf).astype(BF16)
            slope = cdf + pre * jnp.exp(-0.5 * pre * pre) * 0.3989422804014327
            d_row = (d_act * slope).astype(BF16)
            hidden[block, lanes] = act
            d_pre[block, lanes] = d_row
            pack[pl.ds(bias_at + f, 1), :] += jnp.sum(
                d_row.astype(F32), axis=0, keepdims=True
            )
            acc_o[...] += nn(act, w_out[lanes, :])
            acc_d[...] += nt(d_row, w_in[:, lanes])

        loop(0, f_tiles, tile)
        result = acc_o[...]
        weight = jnp.sum(g_in[block, :].astype(F32) * result, axis=-1, keepdims=True)
        d_logits = (weight * (hot - gates)).astype(BF16)
        pack[8:bias_at, :] += tn(d_logits, x_in[block, :])
        ret_d[block, :] = (acc_d[...] + nn(d_logits, router)).astype(BF16)
        ret_o[block, :] = (chosen * result).astype(BF16)

        def back(r):
            @pl.when(r > 0)
            def _():
                give_back(ret_d, table_d, s_d, r_d, r).start()

        loop(first, first + sources, back)

    loop(0, CHUNKS, expert_chunk)
    mine = aligned(at.me, cap_rows)
    table_d[mine, :] = ret_d[0:cap_rows, :]

    part = FTILE // n_x
    per_core = f_tiles // 2

    def e_tile(core, j):
        return (core * per_core + j // 2) * 2 + j % 2

    def to_partner(j):
        return remote(ew.at[e_tile(other, j)], ew_core.at[j], s_ec.at[j], r_ec.at[j], at.partner())

    def to_x(i, j):
        src = ew.at[e_tile(at.core, j), aligned(at.x_index(i), part), :]
        return remote(src, ew_x.at[i - 1, j], s_ex.at[i - 1, j], r_ex.at[i - 1, j], at.x_peer(i))

    def e_part(core, j, x):
        return e_tile(core, j), aligned(x, part)

    def all_x(i, j):
        tile, mine = e_part(at.core, j, at.x)
        src, dst = ew.at[tile, mine, :], o_expert.at[tile, mine, :]
        return remote(src, dst, s_ea.at[i - 1, j], r_ea.at[i - 1, j], at.x_peer(i))

    def from_x(i, j):
        tile, theirs = e_part(at.core, j, x_back(i))
        dst = o_expert.at[tile, theirs, :]
        return remote(dst, dst, s_ea.at[i - 1, j], r_ea.at[i - 1, j], at.x_peer(i))

    def to_core(i, j, core):
        tile, piece = e_part(core, j, x_back(i))
        dst = o_expert.at[tile, piece, :]
        src = ew.at[tile, piece, :] if i == 0 else dst
        return remote(src, dst, s_eb.at[i, j], r_eb.at[i, j], at.partner())

    def to_self(j):
        tile, mine = e_part(at.core, j, at.x)
        return pltpu.make_async_copy(
            ew.at[tile, mine, :], o_expert.at[tile, mine, :], s_own.at[2 + j]
        )

    n_mine = 2 * per_core

    def grad_tiles(core, f):
        tile = core * per_core + f
        lanes = aligned(tile, FTILE)
        ew[2 * tile] = tn(x_in[...], d_pre[:, lanes]).astype(BF16)
        ew[2 * tile + 1] = tn(hidden[:, lanes], g_in[...]).astype(BF16)

    def theirs(f):
        grad_tiles(other, f)
        to_partner(2 * f).start()
        to_partner(2 * f + 1).start()

    loop(0, per_core, theirs)
    loop(0, per_core, lambda f: grad_tiles(at.core, f))

    def sum_cores(j):
        to_partner(j).wait_recv()
        tile = e_tile(at.core, j)
        ew[tile] = (ew[tile].astype(F32) + ew_core[j].astype(F32)).astype(BF16)
        for i in range(1, n_x):
            to_x(i, j).start()

    loop(0, n_mine, sum_cores)

    table_o = send_x

    def left(k):
        send_rows(send_x, x_in, s_x, r_x, k).wait_send()

    loop(1, n_f, left)
    table_o[mine, :] = ret_o[0:cap_rows, :]

    def tell(k):
        pl.semaphore_signal(ready, inc=1, device_id=at.fsdp_peer(k), device_id_type=MESH)

    loop(1, n_f, tell)
    loop(1, n_f, lambda r: give_back(ret_d, table_d, s_d, r_d, r).wait_send())
    pl.semaphore_wait(ready, n_f - 1)
    loop(1, n_f, lambda r: give_back(ret_o, table_o, s_o, r_o, r).start())

    def returned(buffer, into, send, recv, r):
        home = at.ahead(n_f - r)
        return remote(
            buffer.at[aligned(r, cap_rows), :],
            into.at[aligned(home, cap_rows), :],
            send.at[r],
            recv.at[r],
            at.fsdp_peer(r),
        )

    loop(1, n_f, lambda r: returned(ret_d, table_d, s_d, r_d, r).wait_recv())

    loop(1, n_f, lambda k: send_rows(send_g, g_in, s_g, r_g, k).wait_send())
    d_mixed = send_g

    table_iota = lax.broadcasted_iota(jnp.int32, (ROWBLK, n_f * cap_rows), 1).astype(F32)

    def gather_rows(block):
        hit = (table_iota == place[block, 0:1]) | (table_iota == place[block, 1:2])
        return jnp.where(hit, 1.0, 0.0).astype(BF16)

    def norm_back(grad, value, inv_std, gain):
        scaled = grad * gain
        return inv_std * (
            scaled
            - jnp.mean(scaled, axis=-1, keepdims=True)
            - value * jnp.mean(scaled * value, axis=-1, keepdims=True)
        )

    def second_back(i):
        block = aligned(i, ROWBLK)
        grad = nn(gather_rows(block), table_d[...])
        value, inv_std = normalize(middle[block, :])
        pack[5:6, :] += jnp.sum(grad * value, axis=0, keepdims=True)
        pack[6:7, :] += jnp.sum(grad, axis=0, keepdims=True)
        total = cot[block, :].astype(F32) + norm_back(grad, value, inv_std, vecs[5:6, :])
        d_middle[block, :] = total
        low = total.astype(BF16)
        routed[block, :] = low
        pack[4:5, :] += jnp.sum(low.astype(F32), axis=0, keepdims=True)
        d_mixed[block, :] = nt(low, wfull[:, 3 * WIDTH : 4 * WIDTH]).astype(BF16)

    loop(0, SLOTS // ROWBLK, second_back)

    def e_spread(j):
        for i in range(1, n_x):
            to_x(i, j).wait_recv()
        tile = e_tile(at.core, j)
        own = aligned(at.x, part)
        total = ew[tile, own, :].astype(F32)
        for i in range(1, n_x):
            total = total + ew_x[i - 1, j].astype(F32)
        ew[tile, own, :] = total.astype(BF16)
        for i in range(1, n_x):
            all_x(i, j).start()
        to_core(0, j, at.core).start()
        to_self(j).start()

    def e_forward(j):
        for i in range(1, n_x):
            from_x(i, j).wait_recv()
            to_core(i, j, at.core).start()

    d_wo = tn(mixed[...], routed[...])
    for pair in range(PAIRS):
        hidden[WIDTH * 2 : WIDTH * 3, (4 * pair + 3) * TILE : (4 * pair + 4) * TILE] = d_wo[:, pair * TILE : (pair + 1) * TILE].astype(BF16)

    units = 16 // n_d
    pairs_in_unit = PAIRS // units

    def own_rows(owner):
        return pl.ds(pl.multiple_of(WIDTH * 2 + owner * shard, shard), shard)

    def dense(tile):
        return hidden.at[WIDTH * 2 : WIDTH * 3, aligned(tile, TILE)]

    def g_core(u, x):
        src = dense(u * n_d + x * 2 + other)
        return remote(src, dense_core.at[u, x], s_gc.at[u, x], r_gc.at[u, x], at.partner())

    def g_x(u, i):
        src = dense(u * n_d + at.x_index(i) * 2 + at.core)
        return remote(
            src, dense_x.at[u, i - 1], s_gx.at[u, i - 1], r_gx.at[u, i - 1], at.x_peer(i)
        )

    def g_f(u, k):
        src = hidden.at[own_rows(at.ahead(k)), aligned(u * n_d + at.d, TILE)]
        return remote(src, dense_f.at[u, k], s_gf.at[u, k], r_gf.at[u, k], at.fsdp_peer(k))

    def g_d(u, i):
        src = final.at[u * n_d + at.d]
        return remote(src, src, s_gd.at[u, i], r_gd.at[u, i], at.dp_peer(i))

    def g_d_from(u, i):
        dst = final.at[u * n_d + lax.rem(at.d + n_d - i, n_d)]
        return remote(dst, dst, s_gd.at[u, i], r_gd.at[u, i], at.dp_peer(i))

    def first_hop(u):
        for x in range(n_x):
            g_core(u, x).start()

    def second_hop(u):
        for x in range(n_x):
            g_core(u, x).wait_recv()
            tile = dense(u * n_d + x * 2 + at.core)
            tile[...] = (tile[...].astype(F32) + dense_core[u, x].astype(F32)).astype(BF16)
        for i in range(1, n_x):
            g_x(u, i).start()

    def third_hop(u):
        tile = dense(u * n_d + at.d)
        total = tile[...].astype(F32)
        for i in range(1, n_x):
            g_x(u, i).wait_recv()
            total = total + dense_x[u, i - 1].astype(F32)
        tile[...] = total.astype(BF16)
        loop(1, n_f, lambda k: g_f(u, k).start())

    def fourth_hop(u):
        tile = u * n_d + at.d
        dense_f[u, 0] = hidden[own_rows(at.me), aligned(tile, TILE)]
        loop(1, n_f, lambda k: g_f(u, k).wait_recv())
        total = dense_f[u, 0].astype(F32)
        for k in range(1, n_f):
            total = total + dense_f[u, k].astype(F32)
        final[tile] = total.astype(BF16)
        for i in range(1, n_d):
            g_d(u, i).start()

    hops = (first_hop, second_hop, third_hop, fourth_hop)

    def attend_back(pair):
        for b, (low, high, row) in enumerate(WINDOWS):
            window = slice(row, row + high - low)
            grad = d_mixed[b * QBLK : (b + 1) * QBLK, aligned(pair, TILE)]
            values = qkv[2 * PAIRS + pair, low:high, :]
            for h in range(2):
                one = jnp.where(halves[h], grad, jnp.zeros_like(grad))
                scores[h, window, :] = nt(values, one)
        for b, (low, high, row) in enumerate(WINDOWS):
            window = slice(row, row + high - low)
            for h in range(2):
                share = probs[2 * pair + h, window, :].astype(F32)
                moved = share * scores[h, window, :]
                moved = moved - share * jnp.sum(moved, axis=0, keepdims=True)
                d_pre[window, h * 256 : h * 256 + QBLK] = moved.astype(BF16)
        for array in (acc_k, acc_v):
            array[...] = jnp.zeros_like(array)
        for b, (low, high, row) in enumerate(WINDOWS):
            window = slice(row, row + high - low)
            block = slice(b * QBLK, (b + 1) * QBLK)
            keys = qkv[PAIRS + pair, low:high, :]
            query = qkv[pair, block, :]
            grad = d_mixed[block, aligned(pair, TILE)]
            both = [
                [
                    tn(d_pre[window, h * 256 : h * 256 + QBLK], keys),
                    nn(d_pre[window, h * 256 : h * 256 + QBLK], query),
                    nn(probs[2 * pair + h, window, :], grad),
                ]
                for h in range(2)
            ]
            d_q, d_k, d_v = [jnp.where(halves[0], one, two) for one, two in zip(*both)]
            hidden[block, pl.ds(pl.multiple_of(pair * 384, 128), 128)] = (d_q * 0.125).astype(BF16)
            acc_k[low:high, :] += d_k
            acc_v[low:high, :] += d_v
        hidden[0:SLOTS, pl.ds(pl.multiple_of(pair * 384 + 128, 128), 128)] = acc_k[...].astype(BF16)
        hidden[0:SLOTS, pl.ds(pl.multiple_of(pair * 384 + 256, 128), 128)] = acc_v[...].astype(BF16)
        d_qkv = hidden[0:SLOTS, pl.ds(pl.multiple_of(pair * 384, 128), 384)]
        sums = jnp.sum(d_qkv.astype(F32), axis=0, keepdims=True)
        pack[2:3, aligned(pair, TILE)] = sums[:, 0:128]
        pack[3:4, aligned(pair, TILE)] = sums[:, 256:384]
        d_w = tn(normed[...], d_qkv)
        for c in range(3):
            dense(4 * pair + c)[...] = d_w[:, c * TILE : (c + 1) * TILE].astype(BF16)

        @pl.when(lax.rem(pair, pairs_in_unit) == pairs_in_unit - 1)
        def _():
            unit = lax.div(pair, pairs_in_unit)
            for age, hop in enumerate(hops):

                @pl.when(unit >= age)
                def _(age=age, hop=hop):
                    hop(unit - age)

        e_spread(pair)

    acc_k, acc_v = bias.at[0:SLOTS, 0:TILE], bias.at[0:SLOTS, TILE : 2 * TILE]
    loop(0, PAIRS, attend_back)

    def later(step):
        for age, hop in enumerate(hops):
            if 0 <= step - age < units:
                hop(step - age)

    later(units)

    def first_back(i):
        block = aligned(i, ROWBLK)
        grad = nt(hidden[block, 0 : 3 * WIDTH], wfull[:, 0 : 3 * WIDTH])
        value, inv_std = normalize(tok[block, :].astype(F32))
        pack[0:1, :] += jnp.sum(grad * value, axis=0, keepdims=True)
        pack[1:2, :] += jnp.sum(grad, axis=0, keepdims=True)
        d_middle[block, :] += norm_back(grad, value, inv_std, vecs[0:1, :])

    loop(0, SLOTS // ROWBLK, first_back)
    save_tokens = pltpu.make_async_copy(d_middle.at[0:SLOTS, :], o_tokens, s_own.at[2 + n_mine])
    save_tokens.start()

    def p_dp(i):
        return remote(pack, pack_dp.at[i], s_p.at[i], r_p.at[i], at.dp_peer(i))

    for i in range(1, n_d):
        p_dp(i).start()
    later(units + 1)
    loop(0, n_mine, e_forward)

    def vec_lane(owner):
        return aligned(lax.div(owner * shard, TILE), TILE)

    def qv_lane(owner):
        return aligned(lax.div(lax.rem(owner * 2 * shard, WIDTH), TILE), TILE)

    def p_vec(k):
        src = pack_dp.at[0, 0:bias_at, vec_lane(at.ahead(k))]
        return remote(src, vec_f.at[k], s_vf.at[k], r_vf.at[k], at.fsdp_peer(k))

    def p_qv(k):
        src = pack_dp.at[0, 0:8, qv_lane(at.ahead(k))]
        return remote(src, qv_f.at[k], s_qf.at[k], r_qf.at[k], at.fsdp_peer(k))

    pack_dp[0] = pack[...]
    for i in range(1, n_d):
        p_dp(i).wait_recv()
        pack_dp[0] += pack_dp[i]
    loop(1, n_f, lambda k: [p_vec(k).start(), p_qv(k).start()])
    save_bias = pltpu.make_async_copy(
        pack_dp.at[0, bias_at : bias_at + 8, :], o_bias, s_own.at[3 + n_mine]
    )
    save_bias.start()
    later(units + 2)

    loop(1, n_f, lambda r: returned(ret_o, table_o, s_o, r_o, r).wait_recv())

    def combine(i):
        block = aligned(i, ROWBLK)
        total = middle[block, :] + nn(gather_rows(block), table_o[...])
        routed[block, :] = total.astype(BF16)

    loop(0, SLOTS // ROWBLK, combine)
    save_out = pltpu.make_async_copy(routed, o_out, s_own.at[4 + n_mine])
    save_out.start()

    loop(1, n_f, lambda k: [p_vec(k).wait_recv(), p_qv(k).wait_recv()])
    vec_f[0] = pack_dp[0, 0:bias_at, vec_lane(at.me)]
    qv_f[0] = pack_dp[0, 0:8, qv_lane(at.me)]

    def add_lanes(k):
        vec_f[0] += vec_f[k]
        qv_f[0] += qv_f[k]

    loop(1, n_f, add_lanes)
    save_vec = pltpu.make_async_copy(vec_f.at[0], o_vec, s_own.at[5 + n_mine])
    save_qv = pltpu.make_async_copy(qv_f.at[0], o_qv, s_own.at[6 + n_mine])
    save_vec.start()
    save_qv.start()
    loop(0, units, lambda u: [g_d_from(u, i).wait_recv() for i in range(1, n_d)])
    save_dense = pltpu.make_async_copy(final, o_dense, s_own.at[7 + n_mine])
    save_dense.start()

    def ended_f(k):
        send_v(k).wait_send()
        send_w(k).wait_send()
        for i in range(1, n_x):
            share_x(i, k).wait_send()
        for i in range(n_x):
            share_core(i, k).wait_send()
        give_back(ret_o, table_o, s_o, r_o, k).wait_send()
        p_vec(k).wait_send()
        p_qv(k).wait_send()

    loop(1, n_f, ended_f)

    def ended_e(j):
        to_partner(j).wait_send()
        for i in range(1, n_x):
            to_x(i, j).wait_send()
            all_x(i, j).wait_send()
        for i in range(n_x):
            to_core(i, j, at.core).wait_send()
            to_core(i, j, other).wait_recv()
        to_self(j).wait()

    loop(0, n_mine, ended_e)

    def ended_u(u):
        for x in range(n_x):
            g_core(u, x).wait_send()
        for i in range(1, n_x):
            g_x(u, i).wait_send()
        loop(1, n_f, lambda k: g_f(u, k).wait_send())
        for i in range(1, n_d):
            g_d(u, i).wait_send()

    loop(0, units, ended_u)
    for i in range(1, n_d):
        p_dp(i).wait_send()
    for copy in (save_tokens, save_bias, save_out, save_vec, save_qv, save_dense):
        copy.wait()


def block(n_f, n_d, experts, cap, cap_rows, tok, cot, cols, rows, wsh, vsh, w_in, w_out, b_in, b_out):
    vmem = pl.BlockSpec(memory_space=pltpu.VMEM)
    hbm = pl.BlockSpec(memory_space=pl.ANY)
    n_x = n_d // 2
    more_x = max(n_x - 1, 1)
    vec_rows = vsh.shape[0]
    shard = WIDTH // n_f
    table = n_f * cap_rows
    hid = w_in.shape[1]
    units = 16 // n_d
    n_mine = hid // FTILE
    pack_rows = 8 + experts + 8
    sds = jax.ShapeDtypeStruct
    vm = pltpu.VMEM
    dma = pltpu.SemaphoreType.DMA
    chunk_rows = table // CHUNKS
    pairs_of = lambda *shape: [dma(shape), dma(shape)]
    return pl.pallas_call(
        functools.partial(block_kernel, n_f, n_d, experts, cap, cap_rows),
        out_shape=(
            sds((SLOTS, WIDTH), BF16),
            sds((SLOTS, WIDTH), F32),
            sds((2 * n_mine, FTILE, WIDTH), BF16),
            sds((16, shard, TILE), BF16),
            sds((8 + experts, TILE), F32),
            sds((8, TILE), F32),
            sds((8, WIDTH), F32),
        ),
        in_specs=[vmem] * 6 + [hbm] * 2 + [vmem] * 2,
        out_specs=[hbm] * 7,
        scratch_shapes=[
            vm((WIDTH, 4 * WIDTH), BF16),
            vm((vec_rows, WIDTH), F32),
            vm((KEYS, 2 * TILE), F32),
            vm((2, KEYS, QBLK), F32),
            vm((2 * PAIRS, KEYS, QBLK), BF16),
            vm((3 * PAIRS, SLOTS, TILE), BF16),
            vm((SLOTS, WIDTH), BF16),
            vm((SLOTS, WIDTH), BF16),
            vm((SLOTS, WIDTH), F32),
            vm((SLOTS, WIDTH), BF16),
            vm((SLOTS, 8), F32),
        ]
        + [vm((table, WIDTH), BF16)] * 4
        + [
            vm((WIDTH, hid), BF16),
            vm((hid, WIDTH), BF16),
            vm((table, hid), BF16),
            vm((table, hid), BF16),
        ]
        + [vm((table, WIDTH), BF16)] * 3
        + [
            vm((2 * n_mine, FTILE, WIDTH), BF16),
            vm((n_mine, FTILE, WIDTH), BF16),
            vm((more_x, n_mine, FTILE // n_x, WIDTH), BF16),
            vm((units, n_x, WIDTH, TILE), BF16),
            vm((units, more_x, WIDTH, TILE), BF16),
            vm((units, n_f, shard, TILE), BF16),
            vm((16, shard, TILE), BF16),
            vm((pack_rows, WIDTH), F32),
            vm((n_d, pack_rows, WIDTH), F32),
            vm((n_f, 8 + experts, TILE), F32),
            vm((n_f, 8, TILE), F32),
            vm((max(2 * chunk_rows, SLOTS), WIDTH), F32),
        ]
        + pairs_of(n_f)
        + pairs_of(n_f)
        + pairs_of(more_x, n_f)
        + pairs_of(n_x, n_f)
        + pairs_of(n_f)
        + pairs_of(n_f)
        + pairs_of(n_f)
        + pairs_of(n_f)
        + pairs_of(n_mine)
        + pairs_of(more_x, n_mine)
        + pairs_of(more_x, n_mine)
        + pairs_of(n_x, n_mine)
        + pairs_of(units, n_x)
        + pairs_of(units, more_x)
        + pairs_of(units, n_f)
        + pairs_of(units, n_d)
        + pairs_of(n_d)
        + pairs_of(n_f)
        + pairs_of(n_f)
        + [dma((8 + n_mine,)), pltpu.SemaphoreType.REGULAR],
        compiler_params=pltpu.CompilerParams(
            collective_id=0, has_side_effects=True, vmem_limit_bytes=63 << 20
        ),
        name="block",
    )(tok, cot, cols, rows, wsh, vsh, w_in, w_out, b_in, b_out)


def spread(vector, n_f, me):
    size = vector.shape[-1]
    whole = jnp.tile(vector, (1,) * (vector.ndim - 1) + (n_f,))
    return jnp.where(jnp.arange(size * n_f) // size == me, whole, jnp.zeros_like(whole))


def shards(
    tokens,
    cotangent,
    segment_ids,
    pad_mask,
    expert_ids,
    priority,
    ln1_gain,
    ln1_shift,
    w_qkv,
    b_qv,
    w_o,
    b_o,
    ln2_gain,
    ln2_shift,
    w_router,
    w_in,
    b_in,
    w_out,
    b_out,
    n_f,
    n_d,
):
    me = lax.axis_index("fsdp")
    count_tok = tokens.shape[0]
    experts = w_router.shape[1]
    cap = (21 * count_tok + 10 * experts - 1) // (10 * experts)
    cap_rows = -(-cap // 16) * 16
    shard = w_qkv.shape[0]
    zero_row = jnp.zeros_like(segment_ids)
    rows = jnp.stack(
        [segment_ids, pad_mask, expert_ids[:, 0], expert_ids[:, 1], priority[0]] + [zero_row] * 3
    )
    cols = rows.T
    by_pair = w_qkv.reshape(shard, 3, PAIRS, TILE).transpose(0, 2, 1, 3).reshape(shard, -1)
    wsh = jnp.concatenate([by_pair, w_o], axis=1)
    whole = functools.partial(spread, n_f=n_f, me=me)
    vec_rows = -(-(8 + experts) // 16) * 16
    vsh = jnp.concatenate(
        [
            whole(ln1_gain)[None],
            whole(ln1_shift)[None],
            whole(b_qv).reshape(2, WIDTH),
            whole(b_o)[None],
            whole(ln2_gain)[None],
            whole(ln2_shift)[None],
            jnp.zeros((1, WIDTH), BF16),
            whole(w_router.T),
            jnp.zeros((vec_rows - 8 - experts, WIDTH), BF16),
        ]
    )
    output, d_tokens, expert_sums, dense, vec, qv, biases = block(
        n_f,
        n_d,
        experts,
        cap,
        cap_rows,
        tokens,
        cotangent,
        cols,
        rows,
        wsh,
        vsh,
        w_in[0],
        w_out[0],
        b_in,
        b_out,
    )
    n_hid = w_in.shape[2]
    d_w_in = expert_sums[0::2].transpose(1, 0, 2).reshape(1, WIDTH, n_hid).astype(F32)
    d_w_out = expert_sums[1::2].reshape(1, n_hid, WIDTH).astype(F32)
    dense = dense.reshape(PAIRS, 4, shard, TILE).astype(F32)
    d_w_qkv = dense[:, :3].transpose(2, 1, 0, 3).reshape(shard, 3 * WIDTH)
    d_w_o = dense[:, 3].transpose(1, 0, 2).reshape(shard, WIDTH)
    vec = lax.dynamic_slice_in_dim(vec, (me * shard) % TILE, shard, axis=1)
    qv = lax.dynamic_slice(qv, (2 + me * 2 * shard // WIDTH, (me * 2 * shard) % TILE), (1, 2 * shard))
    return (
        output,
        d_tokens,
        vec[0],
        vec[1],
        d_w_qkv,
        qv[0],
        d_w_o,
        vec[4],
        vec[5],
        vec[6],
        vec[8:].T,
        d_w_in,
        biases[:4].reshape(1, n_hid),
        d_w_out,
        biases[4:5],
    )


def solution(mesh):
    both, one = P(("dp", "fsdp")), P("fsdp")
    n_f, n_d = mesh.shape["fsdp"], mesh.shape["dp"]
    return jax.shard_map(
        functools.partial(shards, n_f=n_f, n_d=n_d),
        mesh=mesh,
        in_specs=(both,) * 6 + (one,) * 13,
        out_specs=(both,) * 2 + (one,) * 13,
        check_vma=False,
    )
```

```python
import functools

import jax
import jax.numpy as jnp
from jax import lax
from jax.experimental import pallas as pl
from jax.experimental.pallas import tpu as pltpu
from jax.sharding import PartitionSpec as P

MESH = pl.DeviceIdType.MESH
BF16 = jnp.bfloat16
F32 = jnp.float32
SLOTS = 720
WIDTH = 512
PAIRS = 4
EPS = 1e-06
WINDOWS = ((0, 384, 0), (96, 624, 384), (336, 720, 912))
KEYS = 1296
QBLK = 240
ROWBLK = 240
TILE = 128
FTILE = 512
CHUNKS = 4


def nt(left, right):
    return lax.dot_general(left, right, (((1,), (1,)), ((), ())), preferred_element_type=F32)


def tn(left, right):
    return lax.dot_general(left, right, (((0,), (0,)), ((), ())), preferred_element_type=F32)


def nn(left, right):
    return jnp.dot(left, right, preferred_element_type=F32)


def normalize(value):
    centred = value - jnp.mean(value, axis=-1, keepdims=True)
    inv_std = lax.rsqrt(jnp.mean(centred * centred, axis=-1, keepdims=True) + EPS)
    return centred * inv_std, inv_std


def aligned(index, size):
    return pl.ds(pl.multiple_of(index * size, size), size)


class Place:
    def __init__(self, n_f, n_d):
        self.n_f, self.n_d, self.n_x = n_f, n_d, n_d // 2
        self.me = lax.axis_index("fsdp")
        self.d = lax.axis_index("dp")
        self.x = lax.div(self.d, 2)
        self.core = lax.rem(self.d, 2)

    def ahead(self, k):
        return lax.rem(self.me + k, self.n_f)

    def fsdp_peer(self, k):
        return (self.d, self.ahead(k))

    def x_index(self, i):
        return lax.rem(self.x + i, self.n_x)

    def x_peer(self, i):
        return (self.x_index(i) * 2 + self.core, self.me)

    def partner(self):
        return (self.x * 2 + 1 - self.core, self.me)

    def dp_peer(self, i):
        return (lax.rem(self.d + i, self.n_d), self.me)

    def enter(self):
        bar = pltpu.get_barrier_semaphore()

        def greet(k, _):
            pl.semaphore_signal(bar, inc=1, device_id=self.fsdp_peer(k), device_id_type=MESH)
            return 0

        lax.fori_loop(1, self.n_f, greet, 0)
        for i in range(1, self.n_d):
            pl.semaphore_signal(bar, inc=1, device_id=self.dp_peer(i), device_id_type=MESH)
        pl.semaphore_wait(bar, self.n_f - 1 + self.n_d - 1)


def remote(src, dst, send_sem, recv_sem, device):
    return pltpu.make_async_remote_copy(
        src_ref=src,
        dst_ref=dst,
        send_sem=send_sem,
        recv_sem=recv_sem,
        device_id=device,
        device_id_type=MESH,
    )


def loop(low, high, body):
    def step(k, carry):
        body(k)
        return carry

    lax.fori_loop(low, high, step, 0)


def block_kernel(
    n_f,
    n_d,
    experts,
    cap,
    cap_rows,
    tok,
    cot,
    segment,
    pad,
    chosen_ids,
    priority,
    w_qkv,
    w_o,
    gain_one,
    shift_one,
    b_qv,
    b_o,
    gain_two,
    shift_two,
    w_router,
    w_in_hbm,
    w_out_hbm,
    b_in,
    b_out,
    o_out,
    o_tokens,
    o_expert,
    o_dense,
    o_vec,
    o_qv,
    o_bias,
    wfull,
    vsh,
    vecs,
    bias,
    scores,
    probs,
    qkv,
    normed,
    mixed,
    middle,
    routed,
    place,
    send_x,
    send_g,
    x_in,
    g_in,
    w_in,
    w_out,
    hidden,
    d_pre,
    ret_d,
    ret_o,
    table_d,
    ew,
    ew_core,
    ew_x,
    dense_core,
    dense_x,
    dense_f,
    final,
    pack,
    pack_dp,
    vec_f,
    qv_f,
    d_middle,
    s_w,
    r_w,
    s_v,
    r_v,
    s_dx,
    r_dx,
    s_dc,
    r_dc,
    s_g,
    r_g,
    s_x,
    r_x,
    s_d,
    r_d,
    s_o,
    r_o,
    s_ec,
    r_ec,
    s_ex,
    r_ex,
    s_ea,
    r_ea,
    s_eb,
    r_eb,
    s_gc,
    r_gc,
    s_gx,
    r_gx,
    s_gf,
    r_gf,
    s_gd,
    r_gd,
    s_p,
    r_p,
    s_vf,
    r_vf,
    s_qf,
    r_qf,
    s_own,
    ready,
):
    at = Place(n_f, n_d)
    n_x = at.n_x
    shard = WIDTH // n_f
    colw = 4 * WIDTH // n_d
    other = 1 - at.core

    def cols_of(d):
        return aligned(d, colw)

    def w_piece(owner, d):
        return wfull.at[aligned(owner, shard), cols_of(d)]

    def x_back(i):
        return at.x_index(n_x - i)

    load_in = pltpu.make_async_copy(w_in_hbm, w_in, s_own.at[0])
    load_out = pltpu.make_async_copy(w_out_hbm, w_out, s_own.at[1])
    load_in.start()
    load_out.start()
    at.enter()

    def send_w(k):
        piece = w_piece(at.me, at.d)
        return remote(piece, piece, s_w.at[k], r_w.at[k], at.fsdp_peer(k))

    vec_rows = vsh.shape[0]

    def vec_piece(owner):
        return hidden.at[aligned(owner, vec_rows), 0:WIDTH]

    def send_v(k):
        return remote(vsh, vec_piece(at.me), s_v.at[k], r_v.at[k], at.fsdp_peer(k))

    def share_x(i, k):
        piece = w_piece(at.ahead(n_f - k), at.d)
        return remote(piece, piece, s_dx.at[i - 1, k], r_dx.at[i - 1, k], at.x_peer(i))

    def share_core(i, k):
        piece = w_piece(at.ahead(n_f - k), x_back(i) * 2 + at.core)
        return remote(piece, piece, s_dc.at[i, k], r_dc.at[i, k], at.partner())

    own = aligned(at.me, shard)
    for pair in range(PAIRS):
        for c in range(3):
            low = (3 * pair + c) * TILE
            src = c * WIDTH + pair * TILE
            wfull[own, low : low + TILE] = w_qkv[:, src : src + TILE]
    wfull[own, 3 * WIDTH : 4 * WIDTH] = w_o[...]
    loop(1, n_f, lambda k: send_w(k).start())

    def placing(size, low):
        shape = (size, WIDTH)
        target = lax.broadcasted_iota(jnp.int32, shape, 1) + low
        source = lax.broadcasted_iota(jnp.int32, shape, 0) + at.me * size
        return jnp.where(target == source, 1.0, 0.0).astype(BF16)

    blank = jnp.zeros((1, shard), F32)
    stack = [
        blank if ref is None else ref[...].astype(F32)
        for ref in (gain_one, shift_one, None, None, b_o, gain_two, shift_two, None)
    ]
    spread = nn(jnp.concatenate(stack, axis=0).astype(BF16), placing(shard, 0))
    row_iota = lax.broadcasted_iota(jnp.int32, (8, WIDTH), 0)
    for r in range(2):
        line = nn(b_qv[...], placing(2 * shard, r * WIDTH))
        spread = spread + jnp.where(row_iota == 2 + r, line, 0.0)
    router_rows = tn(w_router[...], placing(shard, 0))
    rest = jnp.zeros((vec_rows - 8 - experts, WIDTH), F32)
    parts = [spread, router_rows] + ([rest] if vec_rows > 8 + experts else [])
    vsh[...] = jnp.concatenate(parts, axis=0).astype(BF16)
    vec_piece(at.me)[...] = vsh[...]
    loop(1, n_f, lambda k: send_v(k).start())

    seg_r, pad_r, pri_r = (ref[...].astype(F32) for ref in (segment, pad, priority))
    lines = jnp.concatenate([seg_r, pad_r, pri_r, jnp.zeros((5, SLOTS), F32)], axis=0)
    columns = jnp.transpose(lines)
    seg_c, pad_c, pri_c = (columns[:, j : j + 1] for j in range(3))
    expert_iota = lax.broadcasted_iota(jnp.int32, (experts, SLOTS), 0)
    live = pad_r > 0
    before = jnp.where(pri_c < pri_r, 1.0, 0.0).astype(BF16)
    chose = [jnp.where((chosen_ids[k : k + 1, :] == expert_iota) & live, 1.0, 0.0) for k in range(2)]
    rank = [nn(one.astype(BF16), before) for one in chose]
    rank[1] = rank[1] + jnp.sum(chose[0], axis=1, keepdims=True)
    spot_r = []
    for k in range(2):
        slot = jnp.sum(chose[k] * rank[k], axis=0, keepdims=True)
        spot = chosen_ids[k : k + 1, :].astype(F32) * cap_rows + slot
        spot_r.append(jnp.where(live & (slot < cap), spot, -1.0))
    place[...] = jnp.transpose(jnp.concatenate(spot_r + [jnp.zeros((6, SLOTS), F32)], axis=0))
    slot_iota = lax.broadcasted_iota(jnp.int32, (cap_rows, SLOTS), 0)

    def pick(expert):
        mine = (slot_iota + expert * cap_rows).astype(F32)
        return jnp.where((mine == spot_r[0]) | (mine == spot_r[1]), 1.0, 0.0).astype(BF16)

    for b, (low, high, row) in enumerate(WINDOWS):
        queries = slice(b * QBLK, (b + 1) * QBLK)
        shape = (high - low, QBLK)
        same = seg_c[low:high, :] == seg_r[:, queries]
        itself = (lax.broadcasted_iota(jnp.int32, shape, 0) + low) == (
            lax.broadcasted_iota(jnp.int32, shape, 1) + b * QBLK
        )
        allowed = same & ((pad_c[low:high, :] > 0) | itself)
        bias[row : row + high - low, 0:QBLK] = jnp.where(allowed, 0.0, -1e30)

    loop(1, n_f, lambda k: send_v(k).wait_recv())
    vecs[...] = vec_piece(0)[...].astype(F32)

    def add_vectors(owner):
        vecs[...] += vec_piece(owner)[...].astype(F32)

    loop(1, n_f, add_vectors)

    def first_norm(i):
        block = aligned(i, ROWBLK)
        value, _ = normalize(tok[block, :].astype(F32))
        normed[block, :] = (value * vecs[0:1, :] + vecs[1:2, :]).astype(BF16)

    loop(0, SLOTS // ROWBLK, first_norm)

    def pass_on(k):
        send_w(k).wait_recv()
        for i in range(1, n_x):
            share_x(i, k).start()
        share_core(0, k).start()

    loop(1, n_f, pass_on)

    def order(step):
        return 1 + lax.rem(2 * n_f - 4 - step, n_f - 1)

    def send_rows(buffer, into, send, recv, k):
        return remote(
            buffer.at[aligned(at.ahead(k), cap_rows), :],
            into.at[aligned(n_f - k, cap_rows), :],
            send.at[k],
            recv.at[n_f - k],
            at.fsdp_peer(k),
        )

    def dispatch(source, buffer, into, send, recv):
        def one(step):
            k = order(step)
            expert = at.ahead(k)
            buffer[aligned(expert, cap_rows), :] = nn(pick(expert), source[...]).astype(BF16)
            send_rows(buffer, into, send, recv, k).start()

        loop(0, n_f - 1, one)
        into[0:cap_rows, :] = nn(pick(at.me), source[...]).astype(BF16)

    dispatch(cot, send_g, g_in, s_g, r_g)

    for i in range(1, n_x):

        def cross(k, i=i):
            piece = w_piece(at.ahead(n_f - k), x_back(i) * 2 + at.core)
            remote(piece, piece, s_dx.at[i - 1, k], r_dx.at[i - 1, k], at.x_peer(i)).wait_recv()
            share_core(i, k).start()

        loop(1, n_f, cross)
    for i in range(n_x):

        def arrive(k, i=i):
            piece = w_piece(at.ahead(n_f - k), x_back(i) * 2 + other)
            remote(piece, piece, s_dc.at[i, k], r_dc.at[i, k], at.partner()).wait_recv()

        loop(1, n_f, arrive)

    def project(pair):
        out = nn(normed[...], wfull[:, pl.ds(pl.multiple_of(pair * 384, 128), 384)])
        lanes = aligned(pair, TILE)
        qkv[pair] = ((out[:, 0:128] + vecs[2:3, lanes]) * 0.125).astype(BF16)
        qkv[PAIRS + pair] = out[:, 128:256].astype(BF16)
        qkv[2 * PAIRS + pair] = (out[:, 256:384] + vecs[3:4, lanes]).astype(BF16)

    loop(0, PAIRS, project)

    lane = lax.broadcasted_iota(jnp.int32, (1, TILE), 1)
    halves = (lane < 64, lane >= 64)

    def attend(pair):
        for b, (low, high, row) in enumerate(WINDOWS):
            window = slice(row, row + high - low)
            query = qkv[pair, b * QBLK : (b + 1) * QBLK, :]
            keys = qkv[PAIRS + pair, low:high, :]
            for h in range(2):
                one = jnp.where(halves[h], query, jnp.zeros_like(query))
                scores[h, window, :] = nt(keys, one) + bias[window, 0:QBLK]
        for b, (low, high, row) in enumerate(WINDOWS):
            window = slice(row, row + high - low)
            for h in range(2):
                value = scores[h, window, :]
                power = jnp.exp(value - jnp.max(value, axis=0, keepdims=True))
                share = 1.0 / jnp.sum(power, axis=0, keepdims=True)
                probs[2 * pair + h, window, :] = (power * share).astype(BF16)
        for b, (low, high, row) in enumerate(WINDOWS):
            window = slice(row, row + high - low)
            values = qkv[2 * PAIRS + pair, low:high, :]
            both = [tn(probs[2 * pair + h, window, :], values) for h in range(2)]
            mixed[b * QBLK : (b + 1) * QBLK, aligned(pair, TILE)] = jnp.where(
                halves[0], both[0], both[1]
            ).astype(BF16)

    loop(0, PAIRS, attend)

    def second_norm(i):
        block = aligned(i, ROWBLK)
        total = nn(mixed[block, :], wfull[:, 3 * WIDTH : 4 * WIDTH])
        total = tok[block, :].astype(F32) + total + vecs[4:5, :]
        middle[block, :] = total
        value, _ = normalize(total)
        routed[block, :] = (value * vecs[5:6, :] + vecs[6:7, :]).astype(BF16)

    loop(0, SLOTS // ROWBLK, second_norm)
    dispatch(routed, send_x, x_in, s_x, r_x)

    load_in.wait()
    load_out.wait()
    pack[...] = jnp.zeros_like(pack)
    router = vecs[8 : 8 + experts, :].astype(BF16)
    chunk_rows = n_f * cap_rows // CHUNKS
    sources = n_f // CHUNKS
    f_tiles = w_in.shape[1] // FTILE
    bias_at = 8 + experts
    hot = jnp.where(lax.broadcasted_iota(jnp.int32, (1, experts), 1) == at.me, 1.0, 0.0)

    def give_back(buffer, into, send, recv, r):
        return remote(
            buffer.at[aligned(r, cap_rows), :],
            into.at[aligned(at.me, cap_rows), :],
            send.at[r],
            recv.at[r],
            at.fsdp_peer(r),
        )

    acc_o, acc_d = d_middle.at[0:chunk_rows, :], d_middle.at[chunk_rows : 2 * chunk_rows, :]

    def expert_chunk(step):
        pos = lax.rem(step + 1, CHUNKS)
        block = aligned(pos, chunk_rows)
        first = pos * sources

        def arrive(r):
            @pl.when(r > 0)
            def _():
                send_rows(send_g, g_in, s_g, r_g, n_f - r).wait_recv()
                send_rows(send_x, x_in, s_x, r_x, n_f - r).wait_recv()

        loop(first, first + sources, arrive)
        x_rows = x_in[block, :]
        logits = nt(x_rows, router)
        gates = jnp.exp(logits - jnp.max(logits, axis=-1, keepdims=True))
        gates = gates / jnp.sum(gates, axis=-1, keepdims=True)
        chosen = jnp.sum(gates * hot, axis=-1, keepdims=True)
        g_rows = (chosen * g_in[block, :].astype(F32)).astype(BF16)
        g_in[block, :] = g_rows
        pack[bias_at + 4 : bias_at + 5, :] += jnp.sum(g_rows.astype(F32), axis=0, keepdims=True)
        acc_o[...] = jnp.broadcast_to(b_out[...].astype(F32), acc_o.shape)
        acc_d[...] = jnp.zeros_like(acc_d)
        def tile(f):
            lanes = aligned(f, FTILE)
            pre = nn(x_in[block, :], w_in[:, lanes]) + b_in[:, lanes].astype(F32)
            d_act = nt(g_in[block, :], w_out[lanes, :])
            cdf = 0.5 + 0.5 * lax.erf(pre * 0.7071067811865476)
            act = (pre * cdf).astype(BF16)
            slope = cdf + pre * jnp.exp(-0.5 * pre * pre) * 0.3989422804014327
            d_row = (d_act * slope).astype(BF16)
            hidden[block, lanes] = act
            d_pre[block, lanes] = d_row
            pack[pl.ds(bias_at + f, 1), :] += jnp.sum(
                d_row.astype(F32), axis=0, keepdims=True
            )
            acc_o[...] += nn(act, w_out[lanes, :])
            acc_d[...] += nt(d_row, w_in[:, lanes])

        loop(0, f_tiles, tile)
        result = acc_o[...]
        weight = jnp.sum(g_in[block, :].astype(F32) * result, axis=-1, keepdims=True)
        d_logits = (weight * (hot - gates)).astype(BF16)
        pack[8:bias_at, :] += tn(d_logits, x_in[block, :])
        ret_d[block, :] = (acc_d[...] + nn(d_logits, router)).astype(BF16)
        ret_o[block, :] = (chosen * result).astype(BF16)

        def back(r):
            @pl.when(r > 0)
            def _():
                give_back(ret_d, table_d, s_d, r_d, r).start()

        loop(first, first + sources, back)

    loop(0, CHUNKS, expert_chunk)
    mine = aligned(at.me, cap_rows)
    table_d[mine, :] = ret_d[0:cap_rows, :]

    part = FTILE // n_x
    per_core = f_tiles // 2

    def e_tile(core, j):
        return (core * per_core + j // 2) * 2 + j % 2

    def to_partner(j):
        return remote(ew.at[e_tile(other, j)], ew_core.at[j], s_ec.at[j], r_ec.at[j], at.partner())

    def to_x(i, j):
        src = ew.at[e_tile(at.core, j), aligned(at.x_index(i), part), :]
        return remote(src, ew_x.at[i - 1, j], s_ex.at[i - 1, j], r_ex.at[i - 1, j], at.x_peer(i))

    def e_part(core, j, x):
        return e_tile(core, j), aligned(x, part)

    def all_x(i, j):
        tile, mine = e_part(at.core, j, at.x)
        src, dst = ew.at[tile, mine, :], o_expert.at[tile, mine, :]
        return remote(src, dst, s_ea.at[i - 1, j], r_ea.at[i - 1, j], at.x_peer(i))

    def from_x(i, j):
        tile, theirs = e_part(at.core, j, x_back(i))
        dst = o_expert.at[tile, theirs, :]
        return remote(dst, dst, s_ea.at[i - 1, j], r_ea.at[i - 1, j], at.x_peer(i))

    def to_core(i, j, core):
        tile, piece = e_part(core, j, x_back(i))
        dst = o_expert.at[tile, piece, :]
        src = ew.at[tile, piece, :] if i == 0 else dst
        return remote(src, dst, s_eb.at[i, j], r_eb.at[i, j], at.partner())

    def to_self(j):
        tile, mine = e_part(at.core, j, at.x)
        return pltpu.make_async_copy(
            ew.at[tile, mine, :], o_expert.at[tile, mine, :], s_own.at[2 + j]
        )

    n_mine = 2 * per_core

    def grad_tiles(core, f):
        tile = core * per_core + f
        lanes = aligned(tile, FTILE)
        ew[2 * tile] = tn(x_in[...], d_pre[:, lanes]).astype(BF16)
        ew[2 * tile + 1] = tn(hidden[:, lanes], g_in[...]).astype(BF16)

    def theirs(f):
        grad_tiles(other, f)
        to_partner(2 * f).start()
        to_partner(2 * f + 1).start()

    loop(0, per_core, theirs)
    loop(0, per_core, lambda f: grad_tiles(at.core, f))

    def sum_cores(j):
        to_partner(j).wait_recv()
        tile = e_tile(at.core, j)
        ew[tile] = (ew[tile].astype(F32) + ew_core[j].astype(F32)).astype(BF16)
        for i in range(1, n_x):
            to_x(i, j).start()

    loop(0, n_mine, sum_cores)

    table_o = send_x

    def left(k):
        send_rows(send_x, x_in, s_x, r_x, k).wait_send()

    loop(1, n_f, left)
    table_o[mine, :] = ret_o[0:cap_rows, :]

    def tell(k):
        pl.semaphore_signal(ready, inc=1, device_id=at.fsdp_peer(k), device_id_type=MESH)

    loop(1, n_f, tell)
    loop(1, n_f, lambda r: give_back(ret_d, table_d, s_d, r_d, r).wait_send())
    pl.semaphore_wait(ready, n_f - 1)
    loop(1, n_f, lambda r: give_back(ret_o, table_o, s_o, r_o, r).start())

    def returned(buffer, into, send, recv, r):
        home = at.ahead(n_f - r)
        return remote(
            buffer.at[aligned(r, cap_rows), :],
            into.at[aligned(home, cap_rows), :],
            send.at[r],
            recv.at[r],
            at.fsdp_peer(r),
        )

    loop(1, n_f, lambda r: returned(ret_d, table_d, s_d, r_d, r).wait_recv())

    loop(1, n_f, lambda k: send_rows(send_g, g_in, s_g, r_g, k).wait_send())
    d_mixed = send_g

    table_iota = lax.broadcasted_iota(jnp.int32, (ROWBLK, n_f * cap_rows), 1).astype(F32)

    def gather_rows(block):
        hit = (table_iota == place[block, 0:1]) | (table_iota == place[block, 1:2])
        return jnp.where(hit, 1.0, 0.0).astype(BF16)

    def norm_back(grad, value, inv_std, gain):
        scaled = grad * gain
        return inv_std * (
            scaled
            - jnp.mean(scaled, axis=-1, keepdims=True)
            - value * jnp.mean(scaled * value, axis=-1, keepdims=True)
        )

    def second_back(i):
        block = aligned(i, ROWBLK)
        grad = nn(gather_rows(block), table_d[...])
        value, inv_std = normalize(middle[block, :])
        pack[5:6, :] += jnp.sum(grad * value, axis=0, keepdims=True)
        pack[6:7, :] += jnp.sum(grad, axis=0, keepdims=True)
        total = cot[block, :].astype(F32) + norm_back(grad, value, inv_std, vecs[5:6, :])
        d_middle[block, :] = total
        low = total.astype(BF16)
        routed[block, :] = low
        pack[4:5, :] += jnp.sum(low.astype(F32), axis=0, keepdims=True)
        d_mixed[block, :] = nt(low, wfull[:, 3 * WIDTH : 4 * WIDTH]).astype(BF16)

    loop(0, SLOTS // ROWBLK, second_back)

    def e_spread(j):
        for i in range(1, n_x):
            to_x(i, j).wait_recv()
        tile = e_tile(at.core, j)
        own = aligned(at.x, part)
        total = ew[tile, own, :].astype(F32)
        for i in range(1, n_x):
            total = total + ew_x[i - 1, j].astype(F32)
        ew[tile, own, :] = total.astype(BF16)
        for i in range(1, n_x):
            all_x(i, j).start()
        to_core(0, j, at.core).start()
        to_self(j).start()

    def e_forward(j):
        for i in range(1, n_x):
            from_x(i, j).wait_recv()
            to_core(i, j, at.core).start()

    d_wo = tn(mixed[...], routed[...])
    for pair in range(PAIRS):
        hidden[WIDTH * 2 : WIDTH * 3, (4 * pair + 3) * TILE : (4 * pair + 4) * TILE] = d_wo[:, pair * TILE : (pair + 1) * TILE].astype(BF16)

    units = 16 // n_d
    pairs_in_unit = PAIRS // units

    def own_rows(owner):
        return pl.ds(pl.multiple_of(WIDTH * 2 + owner * shard, shard), shard)

    def dense(tile):
        return hidden.at[WIDTH * 2 : WIDTH * 3, aligned(tile, TILE)]

    def g_core(u, x):
        src = dense(u * n_d + x * 2 + other)
        return remote(src, dense_core.at[u, x], s_gc.at[u, x], r_gc.at[u, x], at.partner())

    def g_x(u, i):
        src = dense(u * n_d + at.x_index(i) * 2 + at.core)
        return remote(
            src, dense_x.at[u, i - 1], s_gx.at[u, i - 1], r_gx.at[u, i - 1], at.x_peer(i)
        )

    def g_f(u, k):
        src = hidden.at[own_rows(at.ahead(k)), aligned(u * n_d + at.d, TILE)]
        return remote(src, dense_f.at[u, k], s_gf.at[u, k], r_gf.at[u, k], at.fsdp_peer(k))

    def g_d(u, i):
        src = final.at[u * n_d + at.d]
        return remote(src, src, s_gd.at[u, i], r_gd.at[u, i], at.dp_peer(i))

    def g_d_from(u, i):
        dst = final.at[u * n_d + lax.rem(at.d + n_d - i, n_d)]
        return remote(dst, dst, s_gd.at[u, i], r_gd.at[u, i], at.dp_peer(i))

    def first_hop(u):
        for x in range(n_x):
            g_core(u, x).start()

    def second_hop(u):
        for x in range(n_x):
            g_core(u, x).wait_recv()
            tile = dense(u * n_d + x * 2 + at.core)
            tile[...] = (tile[...].astype(F32) + dense_core[u, x].astype(F32)).astype(BF16)
        for i in range(1, n_x):
            g_x(u, i).start()

    def third_hop(u):
        tile = dense(u * n_d + at.d)
        total = tile[...].astype(F32)
        for i in range(1, n_x):
            g_x(u, i).wait_recv()
            total = total + dense_x[u, i - 1].astype(F32)
        tile[...] = total.astype(BF16)
        loop(1, n_f, lambda k: g_f(u, k).start())

    def fourth_hop(u):
        tile = u * n_d + at.d
        dense_f[u, 0] = hidden[own_rows(at.me), aligned(tile, TILE)]
        loop(1, n_f, lambda k: g_f(u, k).wait_recv())
        total = dense_f[u, 0].astype(F32)
        for k in range(1, n_f):
            total = total + dense_f[u, k].astype(F32)
        final[tile] = total.astype(BF16)
        for i in range(1, n_d):
            g_d(u, i).start()

    hops = (first_hop, second_hop, third_hop, fourth_hop)

    def attend_back(pair):
        for b, (low, high, row) in enumerate(WINDOWS):
            window = slice(row, row + high - low)
            grad = d_mixed[b * QBLK : (b + 1) * QBLK, aligned(pair, TILE)]
            values = qkv[2 * PAIRS + pair, low:high, :]
            for h in range(2):
                one = jnp.where(halves[h], grad, jnp.zeros_like(grad))
                scores[h, window, :] = nt(values, one)
        for b, (low, high, row) in enumerate(WINDOWS):
            window = slice(row, row + high - low)
            for h in range(2):
                share = probs[2 * pair + h, window, :].astype(F32)
                moved = share * scores[h, window, :]
                moved = moved - share * jnp.sum(moved, axis=0, keepdims=True)
                d_pre[window, h * 256 : h * 256 + QBLK] = moved.astype(BF16)
        for array in (acc_k, acc_v):
            array[...] = jnp.zeros_like(array)
        for b, (low, high, row) in enumerate(WINDOWS):
            window = slice(row, row + high - low)
            block = slice(b * QBLK, (b + 1) * QBLK)
            keys = qkv[PAIRS + pair, low:high, :]
            query = qkv[pair, block, :]
            grad = d_mixed[block, aligned(pair, TILE)]
            both = [
                [
                    tn(d_pre[window, h * 256 : h * 256 + QBLK], keys),
                    nn(d_pre[window, h * 256 : h * 256 + QBLK], query),
                    nn(probs[2 * pair + h, window, :], grad),
                ]
                for h in range(2)
            ]
            d_q, d_k, d_v = [jnp.where(halves[0], one, two) for one, two in zip(*both)]
            hidden[block, pl.ds(pl.multiple_of(pair * 384, 128), 128)] = (d_q * 0.125).astype(BF16)
            acc_k[low:high, :] += d_k
            acc_v[low:high, :] += d_v
        hidden[0:SLOTS, pl.ds(pl.multiple_of(pair * 384 + 128, 128), 128)] = acc_k[...].astype(BF16)
        hidden[0:SLOTS, pl.ds(pl.multiple_of(pair * 384 + 256, 128), 128)] = acc_v[...].astype(BF16)
        d_qkv = hidden[0:SLOTS, pl.ds(pl.multiple_of(pair * 384, 128), 384)]
        sums = jnp.sum(d_qkv.astype(F32), axis=0, keepdims=True)
        pack[2:3, aligned(pair, TILE)] = sums[:, 0:128]
        pack[3:4, aligned(pair, TILE)] = sums[:, 256:384]
        d_w = tn(normed[...], d_qkv)
        for c in range(3):
            dense(4 * pair + c)[...] = d_w[:, c * TILE : (c + 1) * TILE].astype(BF16)

        @pl.when(lax.rem(pair, pairs_in_unit) == pairs_in_unit - 1)
        def _():
            unit = lax.div(pair, pairs_in_unit)
            for age, hop in enumerate(hops):

                @pl.when(unit >= age)
                def _(age=age, hop=hop):
                    hop(unit - age)

        e_spread(pair)

    acc_k, acc_v = bias.at[0:SLOTS, 0:TILE], bias.at[0:SLOTS, TILE : 2 * TILE]
    loop(0, PAIRS, attend_back)

    def later(step):
        for age, hop in enumerate(hops):
            if 0 <= step - age < units:
                hop(step - age)

    later(units)

    def first_back(i):
        block = aligned(i, ROWBLK)
        grad = nt(hidden[block, 0 : 3 * WIDTH], wfull[:, 0 : 3 * WIDTH])
        value, inv_std = normalize(tok[block, :].astype(F32))
        pack[0:1, :] += jnp.sum(grad * value, axis=0, keepdims=True)
        pack[1:2, :] += jnp.sum(grad, axis=0, keepdims=True)
        d_middle[block, :] += norm_back(grad, value, inv_std, vecs[0:1, :])

    loop(0, SLOTS // ROWBLK, first_back)
    save_tokens = pltpu.make_async_copy(d_middle.at[0:SLOTS, :], o_tokens, s_own.at[2 + n_mine])
    save_tokens.start()

    def p_dp(i):
        return remote(pack, pack_dp.at[i], s_p.at[i], r_p.at[i], at.dp_peer(i))

    for i in range(1, n_d):
        p_dp(i).start()
    later(units + 1)
    loop(0, n_mine, e_forward)

    def vec_lane(owner):
        return aligned(lax.div(owner * shard, TILE), TILE)

    def qv_lane(owner):
        return aligned(lax.div(lax.rem(owner * 2 * shard, WIDTH), TILE), TILE)

    def p_vec(k):
        src = pack_dp.at[0, 0:bias_at, vec_lane(at.ahead(k))]
        return remote(src, vec_f.at[k], s_vf.at[k], r_vf.at[k], at.fsdp_peer(k))

    def p_qv(k):
        src = pack_dp.at[0, 0:8, qv_lane(at.ahead(k))]
        return remote(src, qv_f.at[k], s_qf.at[k], r_qf.at[k], at.fsdp_peer(k))

    pack_dp[0] = pack[...]
    for i in range(1, n_d):
        p_dp(i).wait_recv()
        pack_dp[0] += pack_dp[i]
    loop(1, n_f, lambda k: [p_vec(k).start(), p_qv(k).start()])
    save_bias = pltpu.make_async_copy(
        pack_dp.at[0, bias_at : bias_at + 8, :], o_bias, s_own.at[3 + n_mine]
    )
    save_bias.start()
    later(units + 2)

    loop(1, n_f, lambda r: returned(ret_o, table_o, s_o, r_o, r).wait_recv())

    def combine(i):
        block = aligned(i, ROWBLK)
        total = middle[block, :] + nn(gather_rows(block), table_o[...])
        routed[block, :] = total.astype(BF16)

    loop(0, SLOTS // ROWBLK, combine)
    save_out = pltpu.make_async_copy(routed, o_out, s_own.at[4 + n_mine])
    save_out.start()

    loop(1, n_f, lambda k: [p_vec(k).wait_recv(), p_qv(k).wait_recv()])
    vec_f[0] = pack_dp[0, 0:bias_at, vec_lane(at.me)]
    qv_f[0] = pack_dp[0, 0:8, qv_lane(at.me)]

    def add_lanes(k):
        vec_f[0] += vec_f[k]
        qv_f[0] += qv_f[k]

    loop(1, n_f, add_lanes)
    save_vec = pltpu.make_async_copy(vec_f.at[0], o_vec, s_own.at[5 + n_mine])
    save_qv = pltpu.make_async_copy(qv_f.at[0], o_qv, s_own.at[6 + n_mine])
    save_vec.start()
    save_qv.start()
    loop(0, units, lambda u: [g_d_from(u, i).wait_recv() for i in range(1, n_d)])
    save_dense = pltpu.make_async_copy(final, o_dense, s_own.at[7 + n_mine])
    save_dense.start()

    def ended_f(k):
        send_v(k).wait_send()
        send_w(k).wait_send()
        for i in range(1, n_x):
            share_x(i, k).wait_send()
        for i in range(n_x):
            share_core(i, k).wait_send()
        give_back(ret_o, table_o, s_o, r_o, k).wait_send()
        p_vec(k).wait_send()
        p_qv(k).wait_send()

    loop(1, n_f, ended_f)

    def ended_e(j):
        to_partner(j).wait_send()
        for i in range(1, n_x):
            to_x(i, j).wait_send()
            all_x(i, j).wait_send()
        for i in range(n_x):
            to_core(i, j, at.core).wait_send()
            to_core(i, j, other).wait_recv()
        to_self(j).wait()

    loop(0, n_mine, ended_e)

    def ended_u(u):
        for x in range(n_x):
            g_core(u, x).wait_send()
        for i in range(1, n_x):
            g_x(u, i).wait_send()
        loop(1, n_f, lambda k: g_f(u, k).wait_send())
        for i in range(1, n_d):
            g_d(u, i).wait_send()

    loop(0, units, ended_u)
    for i in range(1, n_d):
        p_dp(i).wait_send()
    for copy in (save_tokens, save_bias, save_out, save_vec, save_qv, save_dense):
        copy.wait()


def block(n_f, n_d, experts, cap, cap_rows, small, w_in, w_out, b_in, b_out):
    vmem = pl.BlockSpec(memory_space=pltpu.VMEM)
    hbm = pl.BlockSpec(memory_space=pl.ANY)
    n_x = n_d // 2
    more_x = max(n_x - 1, 1)
    vec_rows = -(-(8 + experts) // 16) * 16
    shard = WIDTH // n_f
    table = n_f * cap_rows
    hid = w_in.shape[1]
    units = 16 // n_d
    n_mine = hid // FTILE
    pack_rows = 8 + experts + 8
    sds = jax.ShapeDtypeStruct
    vm = pltpu.VMEM
    dma = pltpu.SemaphoreType.DMA
    chunk_rows = table // CHUNKS
    pairs_of = lambda *shape: [dma(shape), dma(shape)]
    return pl.pallas_call(
        functools.partial(block_kernel, n_f, n_d, experts, cap, cap_rows),
        out_shape=(
            sds((SLOTS, WIDTH), BF16),
            sds((SLOTS, WIDTH), F32),
            sds((2 * n_mine, FTILE, WIDTH), BF16),
            sds((16, shard, TILE), BF16),
            sds((8 + experts, TILE), F32),
            sds((8, TILE), F32),
            sds((8, WIDTH), F32),
        ),
        in_specs=[vmem] * len(small) + [hbm] * 2 + [vmem] * 2,
        out_specs=[hbm] * 7,
        scratch_shapes=[
            vm((WIDTH, 4 * WIDTH), BF16),
            vm((vec_rows, WIDTH), BF16),
            vm((vec_rows, WIDTH), F32),
            vm((KEYS, 2 * TILE), F32),
            vm((2, KEYS, QBLK), F32),
            vm((2 * PAIRS, KEYS, QBLK), BF16),
            vm((3 * PAIRS, SLOTS, TILE), BF16),
            vm((SLOTS, WIDTH), BF16),
            vm((SLOTS, WIDTH), BF16),
            vm((SLOTS, WIDTH), F32),
            vm((SLOTS, WIDTH), BF16),
            vm((SLOTS, 8), F32),
        ]
        + [vm((table, WIDTH), BF16)] * 4
        + [
            vm((WIDTH, hid), BF16),
            vm((hid, WIDTH), BF16),
            vm((table, hid), BF16),
            vm((table, hid), BF16),
        ]
        + [vm((table, WIDTH), BF16)] * 3
        + [
            vm((2 * n_mine, FTILE, WIDTH), BF16),
            vm((n_mine, FTILE, WIDTH), BF16),
            vm((more_x, n_mine, FTILE // n_x, WIDTH), BF16),
            vm((units, n_x, WIDTH, TILE), BF16),
            vm((units, more_x, WIDTH, TILE), BF16),
            vm((units, n_f, shard, TILE), BF16),
            vm((16, shard, TILE), BF16),
            vm((pack_rows, WIDTH), F32),
            vm((n_d, pack_rows, WIDTH), F32),
            vm((n_f, 8 + experts, TILE), F32),
            vm((n_f, 8, TILE), F32),
            vm((max(2 * chunk_rows, SLOTS), WIDTH), F32),
        ]
        + pairs_of(n_f)
        + pairs_of(n_f)
        + pairs_of(more_x, n_f)
        + pairs_of(n_x, n_f)
        + pairs_of(n_f)
        + pairs_of(n_f)
        + pairs_of(n_f)
        + pairs_of(n_f)
        + pairs_of(n_mine)
        + pairs_of(more_x, n_mine)
        + pairs_of(more_x, n_mine)
        + pairs_of(n_x, n_mine)
        + pairs_of(units, n_x)
        + pairs_of(units, more_x)
        + pairs_of(units, n_f)
        + pairs_of(units, n_d)
        + pairs_of(n_d)
        + pairs_of(n_f)
        + pairs_of(n_f)
        + [dma((8 + n_mine,)), pltpu.SemaphoreType.REGULAR],
        compiler_params=pltpu.CompilerParams(
            collective_id=0, has_side_effects=True, vmem_limit_bytes=63 << 20
        ),
        name="block",
    )(*small, w_in, w_out, b_in, b_out)


def finish_kernel(
    n_f,
    experts,
    in_out,
    in_tokens,
    in_expert,
    dense,
    vec,
    qv,
    biases,
    o_out,
    o_tokens,
    o_g1,
    o_s1,
    o_qkv,
    o_bqv,
    o_wo,
    o_bo,
    o_g2,
    o_s2,
    o_router,
    o_w_in,
    o_b_in,
    o_w_out,
    o_b_out,
    low,
    wide,
    s_load,
    s_save,
):
    me = lax.axis_index("fsdp")
    shard = WIDTH // n_f
    tiles = in_expert.shape[0]
    loads = [pltpu.make_async_copy(in_expert.at[t], low.at[t], s_load.at[t]) for t in range(tiles)]
    for load in loads:
        load.start()
    saves = [
        pltpu.make_async_copy(in_out, o_out, s_save.at[tiles]),
        pltpu.make_async_copy(in_tokens, o_tokens, s_save.at[tiles + 1]),
    ]
    for save in saves:
        save.start()

    def my_lanes(value, size):
        place = lax.rem(me * size, TILE)
        total = jnp.zeros((value.shape[0], size), F32)
        for low_lane in range(0, TILE, size):
            total = total + jnp.where(place == low_lane, value[:, low_lane : low_lane + size], 0.0)
        return total

    own = my_lanes(vec[...], shard)
    for row, ref in ((0, o_g1), (1, o_s1), (4, o_bo), (5, o_g2), (6, o_s2)):
        ref[...] = own[row : row + 1, :]
    o_router[...] = jnp.transpose(own[8 : 8 + experts, :])
    lines = my_lanes(qv[...], 2 * shard)
    o_bqv[...] = jnp.where(me * 2 * shard < WIDTH, lines[2:3, :], lines[3:4, :])
    for pair in range(PAIRS):
        for c in range(3):
            at = c * WIDTH + pair * TILE
            o_qkv[:, at : at + TILE] = dense[4 * pair + c].astype(F32)
        o_wo[:, pair * TILE : (pair + 1) * TILE] = dense[4 * pair + 3].astype(F32)
    for f in range(tiles // 2):
        o_b_in[:, f * FTILE : (f + 1) * FTILE] = biases[f : f + 1, :]
    o_b_out[...] = biases[4:5, :]
    for t in range(tiles):
        loads[t].wait()
        wide[t] = low[t].astype(F32)
        piece = pl.ds(t // 2 * FTILE, FTILE)
        dst = o_w_out.at[0, piece, :] if t % 2 else o_w_in.at[0, :, piece]
        saves.append(pltpu.make_async_copy(wide.at[t], dst, s_save.at[t]))
        saves[-1].start()
    for save in saves:
        save.wait()


def finish(n_f, experts, hid, parts):
    vmem = pl.BlockSpec(memory_space=pltpu.VMEM)
    hbm = pl.BlockSpec(memory_space=pl.ANY)
    shard = WIDTH // n_f
    tiles = parts[2].shape[0]
    line = lambda *shape: jax.ShapeDtypeStruct(shape, F32)
    return pl.pallas_call(
        functools.partial(finish_kernel, n_f, experts),
        out_shape=(
            jax.ShapeDtypeStruct((SLOTS, WIDTH), BF16),
            line(SLOTS, WIDTH),
            line(1, shard),
            line(1, shard),
            line(shard, 3 * WIDTH),
            line(1, 2 * shard),
            line(shard, WIDTH),
            line(1, shard),
            line(1, shard),
            line(1, shard),
            line(shard, experts),
            line(1, WIDTH, hid),
            line(1, hid),
            line(1, hid, WIDTH),
            line(1, WIDTH),
        ),
        in_specs=[hbm] * 3 + [vmem] * 4,
        out_specs=[hbm] * 2 + [vmem] * 9 + [hbm, vmem, hbm, vmem],
        scratch_shapes=[
            pltpu.VMEM((tiles, FTILE, WIDTH), BF16),
            pltpu.VMEM((tiles, FTILE, WIDTH), F32),
            pltpu.SemaphoreType.DMA((tiles,)),
            pltpu.SemaphoreType.DMA((tiles + 2,)),
        ],
        compiler_params=pltpu.CompilerParams(vmem_limit_bytes=62 << 20),
        name="finish",
    )(*parts)


def shards(
    tokens,
    cotangent,
    segment_ids,
    pad_mask,
    expert_ids,
    priority,
    ln1_gain,
    ln1_shift,
    w_qkv,
    b_qv,
    w_o,
    b_o,
    ln2_gain,
    ln2_shift,
    w_router,
    w_in,
    b_in,
    w_out,
    b_out,
    n_f,
    n_d,
):
    experts = w_router.shape[1]
    cap = (21 * tokens.shape[0] + 10 * experts - 1) // (10 * experts)
    cap_rows = -(-cap // 16) * 16
    line = lambda vector: vector.reshape(1, -1)
    small = (
        tokens,
        cotangent,
        line(segment_ids),
        line(pad_mask),
        expert_ids.T,
        priority,
        w_qkv,
        w_o,
        line(ln1_gain),
        line(ln1_shift),
        line(b_qv),
        line(b_o),
        line(ln2_gain),
        line(ln2_shift),
        w_router,
    )
    parts = block(n_f, n_d, experts, cap, cap_rows, small, w_in[0], w_out[0], b_in, b_out)
    done = finish(n_f, experts, w_in.shape[2], parts)
    flat = (2, 3, 5, 7, 8, 9)
    return tuple(value.reshape(-1) if i in flat else value for i, value in enumerate(done))


def solution(mesh):
    both, one = P(("dp", "fsdp")), P("fsdp")
    n_f, n_d = mesh.shape["fsdp"], mesh.shape["dp"]
    return jax.shard_map(
        functools.partial(shards, n_f=n_f, n_d=n_d),
        mesh=mesh,
        in_specs=(both,) * 6 + (one,) * 13,
        out_specs=(both,) * 2 + (one,) * 13,
        check_vma=False,
    )
```

```python
import functools

import jax
import jax.numpy as jnp
from jax import lax
from jax.experimental import pallas as pl
from jax.experimental.pallas import tpu as pltpu
from jax.sharding import PartitionSpec as P

MESH = pl.DeviceIdType.MESH
BF16 = jnp.bfloat16
F32 = jnp.float32
SLOTS = 720
WIDTH = 512
PAIRS = 4
EPS = 1e-06
WINDOWS = ((0, 384, 0), (96, 624, 384), (336, 720, 912))
KEYS = 1296
QBLK = 240
ROWBLK = 240
TILE = 128
FTILE = 512
CHUNKS = 4
LOTS = 7


def nt(left, right):
    return lax.dot_general(left, right, (((1,), (1,)), ((), ())), preferred_element_type=F32)


def tn(left, right):
    return lax.dot_general(left, right, (((0,), (0,)), ((), ())), preferred_element_type=F32)


def nn(left, right):
    return jnp.dot(left, right, preferred_element_type=F32)


def normalize(value):
    centred = value - jnp.mean(value, axis=-1, keepdims=True)
    inv_std = lax.rsqrt(jnp.mean(centred * centred, axis=-1, keepdims=True) + EPS)
    return centred * inv_std, inv_std


def aligned(index, size):
    return pl.ds(pl.multiple_of(index * size, size), size)


class Place:
    def __init__(self, n_f, n_d):
        self.n_f, self.n_d, self.n_x = n_f, n_d, n_d // 2
        self.me = lax.axis_index("fsdp")
        self.d = lax.axis_index("dp")
        self.x = lax.div(self.d, 2)
        self.core = lax.rem(self.d, 2)

    def ahead(self, k):
        return lax.rem(self.me + k, self.n_f)

    def fsdp_peer(self, k):
        return (self.d, self.ahead(k))

    def x_index(self, i):
        return lax.rem(self.x + i, self.n_x)

    def x_peer(self, i):
        return (self.x_index(i) * 2 + self.core, self.me)

    def partner(self):
        return (self.x * 2 + 1 - self.core, self.me)

    def dp_peer(self, i):
        return (lax.rem(self.d + i, self.n_d), self.me)

    def enter(self):
        bar = pltpu.get_barrier_semaphore()

        def greet(k, _):
            pl.semaphore_signal(bar, inc=1, device_id=self.fsdp_peer(k), device_id_type=MESH)
            return 0

        lax.fori_loop(1, self.n_f, greet, 0)
        for i in range(1, self.n_d):
            pl.semaphore_signal(bar, inc=1, device_id=self.dp_peer(i), device_id_type=MESH)
        pl.semaphore_wait(bar, self.n_f - 1 + self.n_d - 1)


def remote(src, dst, send_sem, recv_sem, device):
    return pltpu.make_async_remote_copy(
        src_ref=src,
        dst_ref=dst,
        send_sem=send_sem,
        recv_sem=recv_sem,
        device_id=device,
        device_id_type=MESH,
    )


def loop(low, high, body):
    def step(k, carry):
        body(k)
        return carry

    lax.fori_loop(low, high, step, 0)


def block_kernel(
    n_f,
    n_d,
    experts,
    cap,
    cap_rows,
    tok,
    cot,
    segment,
    pad,
    chosen_ids,
    priority,
    w_qkv,
    w_o,
    gain_one,
    shift_one,
    b_qv,
    b_o,
    gain_two,
    shift_two,
    w_router,
    w_in_hbm,
    w_out_hbm,
    b_in,
    b_out,
    o_out,
    o_tokens,
    o_expert,
    o_dense,
    o_vec,
    o_qv,
    o_bias,
    wfull,
    vsh,
    vecs,
    bias,
    scores,
    probs,
    qkv,
    normed,
    mixed,
    middle,
    routed,
    place,
    send_x,
    send_g,
    x_in,
    g_in,
    w_in,
    w_out,
    hidden,
    d_pre,
    ret_d,
    ret_o,
    table_d,
    ew,
    ew_core,
    ew_x,
    dense_core,
    dense_x,
    dense_f,
    final,
    pack,
    pack_dp,
    vec_f,
    qv_f,
    d_middle,
    s_w,
    r_w,
    s_v,
    r_v,
    s_dx,
    r_dx,
    s_dc,
    r_dc,
    s_g,
    r_g,
    s_x,
    r_x,
    s_d,
    r_d,
    s_o,
    r_o,
    s_ec,
    r_ec,
    s_ex,
    r_ex,
    s_ea,
    r_ea,
    s_eb,
    r_eb,
    s_gc,
    r_gc,
    s_gx,
    r_gx,
    s_gf,
    r_gf,
    s_gd,
    r_gd,
    s_p,
    r_p,
    s_vf,
    r_vf,
    s_qf,
    r_qf,
    s_own,
    s_self,
    ready,
):
    at = Place(n_f, n_d)
    n_x = at.n_x
    shard = WIDTH // n_f
    colw = 4 * WIDTH // n_d
    other = 1 - at.core

    def cols_of(d):
        return aligned(d, colw)

    def w_piece(owner, d):
        return wfull.at[aligned(owner, shard), cols_of(d)]

    def x_back(i):
        return at.x_index(n_x - i)

    load_in = pltpu.make_async_copy(w_in_hbm, w_in, s_own.at[0])
    load_out = pltpu.make_async_copy(w_out_hbm, w_out, s_own.at[1])
    load_in.start()
    load_out.start()
    at.enter()

    n_y = 1 << ((n_f.bit_length() - 1) // 2)
    n_z = n_f // n_y
    my_z, my_y = lax.div(at.me, n_y), lax.rem(at.me, n_y)

    def member(z, y):
        return lax.rem(my_z + z, n_z) * n_y + lax.rem(my_y + y, n_y)

    def owner(k):
        return member(n_z - lax.rem(k, n_z), n_y - lax.div(k, n_z))

    def along_z(k):
        piece = w_piece(at.me, at.d)
        return remote(piece, piece, s_w.at[k], r_w.at[k], (at.d, member(k, 0)))

    def along_y(j, i):
        piece, k = w_piece(member(n_z - i, 0), at.d), j * n_z + i
        return remote(piece, piece, s_w.at[k], r_w.at[k], (at.d, member(0, j)))

    def got_w(k):
        piece = w_piece(owner(k), at.d)
        return remote(piece, piece, s_w.at[k], r_w.at[k], (at.d, at.me))

    vec_rows = vsh.shape[0]

    def vec_piece(owner):
        return hidden.at[aligned(owner, vec_rows), 0:WIDTH]

    def send_v(k):
        return remote(vsh, vec_piece(at.me), s_v.at[k], r_v.at[k], at.fsdp_peer(k))

    def share_x(i, k):
        piece = w_piece(owner(k), at.d)
        return remote(piece, piece, s_dx.at[i - 1, k], r_dx.at[i - 1, k], at.x_peer(i))

    def share_core(i, k):
        piece = w_piece(owner(k), x_back(i) * 2 + at.core)
        return remote(piece, piece, s_dc.at[i, k], r_dc.at[i, k], at.partner())

    own = aligned(at.me, shard)
    for pair in range(PAIRS):
        for c in range(3):
            low = (3 * pair + c) * TILE
            src = c * WIDTH + pair * TILE
            wfull[own, low : low + TILE] = w_qkv[:, src : src + TILE]
    wfull[own, 3 * WIDTH : 4 * WIDTH] = w_o[...]
    loop(1, n_z, lambda k: along_z(k).start())
    loop(1, n_y, lambda j: along_y(j, 0).start())

    def placing(size, low):
        shape = (size, WIDTH)
        target = lax.broadcasted_iota(jnp.int32, shape, 1) + low
        source = lax.broadcasted_iota(jnp.int32, shape, 0) + at.me * size
        return jnp.where(target == source, 1.0, 0.0).astype(BF16)

    blank = jnp.zeros((1, shard), F32)
    stack = [
        blank if ref is None else ref[...].astype(F32)
        for ref in (gain_one, shift_one, None, None, b_o, gain_two, shift_two, None)
    ]
    spread = nn(jnp.concatenate(stack, axis=0).astype(BF16), placing(shard, 0))
    row_iota = lax.broadcasted_iota(jnp.int32, (8, WIDTH), 0)
    for r in range(2):
        line = nn(b_qv[...], placing(2 * shard, r * WIDTH))
        spread = spread + jnp.where(row_iota == 2 + r, line, 0.0)
    router_rows = nn(w_router[...], placing(shard, 0))
    rest = jnp.zeros((vec_rows - 8 - experts, WIDTH), F32)
    parts = [spread, router_rows] + ([rest] if vec_rows > 8 + experts else [])
    vsh[...] = jnp.concatenate(parts, axis=0).astype(BF16)
    vec_piece(at.me)[...] = vsh[...]
    loop(1, n_f, lambda k: send_v(k).start())

    seg_r, pad_r, pri_r = (ref[...].astype(F32) for ref in (segment, pad, priority))
    lines = jnp.concatenate([seg_r, pad_r, pri_r, jnp.zeros((5, SLOTS), F32)], axis=0)
    columns = jnp.transpose(lines)
    seg_c, pad_c, pri_c = (columns[:, j : j + 1] for j in range(3))
    expert_iota = lax.broadcasted_iota(jnp.int32, (experts, SLOTS), 0)
    live = pad_r > 0
    before = jnp.where(pri_c < pri_r, 1.0, 0.0).astype(BF16)
    chose = [jnp.where((chosen_ids[k : k + 1, :] == expert_iota) & live, 1.0, 0.0) for k in range(2)]
    rank = [nn(one.astype(BF16), before) for one in chose]
    rank[1] = rank[1] + jnp.sum(chose[0], axis=1, keepdims=True)
    spot_r = []
    for k in range(2):
        slot = jnp.sum(chose[k] * rank[k], axis=0, keepdims=True)
        spot = chosen_ids[k : k + 1, :].astype(F32) * cap_rows + slot
        spot_r.append(jnp.where(live & (slot < cap), spot, -1.0))
    place[...] = jnp.transpose(jnp.concatenate(spot_r + [jnp.zeros((6, SLOTS), F32)], axis=0))
    slot_iota = lax.broadcasted_iota(jnp.int32, (cap_rows, SLOTS), 0)

    def pick(expert):
        mine = (slot_iota + expert * cap_rows).astype(F32)
        return jnp.where((mine == spot_r[0]) | (mine == spot_r[1]), 1.0, 0.0).astype(BF16)

    for b, (low, high, row) in enumerate(WINDOWS):
        queries = slice(b * QBLK, (b + 1) * QBLK)
        shape = (high - low, QBLK)
        same = seg_c[low:high, :] == seg_r[:, queries]
        itself = (lax.broadcasted_iota(jnp.int32, shape, 0) + low) == (
            lax.broadcasted_iota(jnp.int32, shape, 1) + b * QBLK
        )
        allowed = same & ((pad_c[low:high, :] > 0) | itself)
        bias[row : row + high - low, 0:QBLK] = jnp.where(allowed, 0.0, -1e30)

    chunk_rows = n_f * cap_rows // CHUNKS
    sources = n_f // CHUNKS

    def position(step):
        return lax.rem(2 * step, 3) + 3 * lax.div(step, 3)

    def send_rows(buffer, into, send, recv, k):
        return remote(
            buffer.at[aligned(at.ahead(k), cap_rows), :],
            into.at[aligned(n_f - k, cap_rows), :],
            send.at[k],
            recv.at[n_f - k],
            at.fsdp_peer(k),
        )

    def dispatch(source, buffer, into, send, recv):
        into[0:cap_rows, :] = nn(pick(at.me), source[...]).astype(BF16)

        def stage(step):
            first = position(step) * sources

            def one(r):
                @pl.when(r > 0)
                def _():
                    k = n_f - r
                    expert = at.ahead(k)
                    rows = nn(pick(expert), source[...]).astype(BF16)
                    buffer[aligned(expert, cap_rows), :] = rows
                    send_rows(buffer, into, send, recv, k).start()

            loop(first, first + sources, one)

        loop(0, CHUNKS, stage)

    def pass_on(k):
        for i in range(1, n_x):
            share_x(i, k).start()
        share_core(0, k).start()

    def from_z(k):
        got_w(k).wait_recv()
        loop(1, n_y, lambda j: along_y(j, k).start())
        pass_on(k)

    def from_y(k):
        got_w(k).wait_recv()
        pass_on(k)

    loop(1, n_z, from_z)
    dispatch(cot, send_g, g_in, s_g, r_g)
    loop(n_z, n_f, from_y)

    loop(1, n_f, lambda k: send_v(k).wait_recv())
    vecs[...] = vec_piece(0)[...].astype(F32)

    def add_vectors(owner):
        vecs[...] += vec_piece(owner)[...].astype(F32)

    loop(1, n_f, add_vectors)

    def first_norm(i):
        block = aligned(i, ROWBLK)
        value, _ = normalize(tok[block, :].astype(F32))
        normed[block, :] = (value * vecs[0:1, :] + vecs[1:2, :]).astype(BF16)

    loop(0, SLOTS // ROWBLK, first_norm)

    for i in range(1, n_x):

        def cross(k, i=i):
            piece = w_piece(owner(k), x_back(i) * 2 + at.core)
            remote(piece, piece, s_dx.at[i - 1, k], r_dx.at[i - 1, k], at.x_peer(i)).wait_recv()
            share_core(i, k).start()

        loop(1, n_f, cross)
    for i in range(n_x):

        def arrive(k, i=i):
            piece = w_piece(owner(k), x_back(i) * 2 + other)
            remote(piece, piece, s_dc.at[i, k], r_dc.at[i, k], at.partner()).wait_recv()

        loop(1, n_f, arrive)

    def project(pair):
        out = nn(normed[...], wfull[:, pl.ds(pl.multiple_of(pair * 384, 128), 384)])
        lanes = aligned(pair, TILE)
        qkv[pair] = ((out[:, 0:128] + vecs[2:3, lanes]) * 0.125).astype(BF16)
        qkv[PAIRS + pair] = out[:, 128:256].astype(BF16)
        qkv[2 * PAIRS + pair] = (out[:, 256:384] + vecs[3:4, lanes]).astype(BF16)

    loop(0, PAIRS, project)

    lane = lax.broadcasted_iota(jnp.int32, (1, TILE), 1)
    halves = (lane < 64, lane >= 64)

    def attend(pair):
        for b, (low, high, row) in enumerate(WINDOWS):
            window = slice(row, row + high - low)
            query = qkv[pair, b * QBLK : (b + 1) * QBLK, :]
            keys = qkv[PAIRS + pair, low:high, :]
            for h in range(2):
                one = jnp.where(halves[h], query, jnp.zeros_like(query))
                scores[h, window, :] = nt(keys, one) + bias[window, 0:QBLK]
        for b, (low, high, row) in enumerate(WINDOWS):
            window = slice(row, row + high - low)
            for h in range(2):
                value = scores[h, window, :]
                power = jnp.exp(value - jnp.max(value, axis=0, keepdims=True))
                share = 1.0 / jnp.sum(power, axis=0, keepdims=True)
                probs[2 * pair + h, window, :] = (power * share).astype(BF16)
        for b, (low, high, row) in enumerate(WINDOWS):
            window = slice(row, row + high - low)
            values = qkv[2 * PAIRS + pair, low:high, :]
            both = [tn(probs[2 * pair + h, window, :], values) for h in range(2)]
            mixed[b * QBLK : (b + 1) * QBLK, aligned(pair, TILE)] = jnp.where(
                halves[0], both[0], both[1]
            ).astype(BF16)

    loop(0, PAIRS, attend)

    def second_norm(i):
        block = aligned(i, ROWBLK)
        total = nn(mixed[block, :], wfull[:, 3 * WIDTH : 4 * WIDTH])
        total = tok[block, :].astype(F32) + total + vecs[4:5, :]
        middle[block, :] = total
        value, _ = normalize(total)
        routed[block, :] = (value * vecs[5:6, :] + vecs[6:7, :]).astype(BF16)

    loop(0, SLOTS // ROWBLK, second_norm)
    dispatch(routed, send_x, x_in, s_x, r_x)

    load_in.wait()
    load_out.wait()
    pack[...] = jnp.zeros_like(pack)
    router = vecs[8 : 8 + experts, :].astype(BF16)
    f_tiles = w_in.shape[1] // FTILE
    bias_at = 8 + experts
    hot = jnp.where(lax.broadcasted_iota(jnp.int32, (1, experts), 1) == at.me, 1.0, 0.0)

    def give_back(buffer, into, send, recv, r):
        return remote(
            buffer.at[aligned(r, cap_rows), :],
            into.at[aligned(at.me, cap_rows), :],
            send.at[r],
            recv.at[r],
            at.fsdp_peer(r),
        )

    acc_o, acc_d = d_middle.at[0:chunk_rows, :], d_middle.at[chunk_rows : 2 * chunk_rows, :]

    def expert_chunk(step):
        pos = position(step)
        block = aligned(pos, chunk_rows)
        first = pos * sources

        def arrive(r):
            @pl.when(r > 0)
            def _():
                send_rows(send_g, g_in, s_g, r_g, n_f - r).wait_recv()
                send_rows(send_x, x_in, s_x, r_x, n_f - r).wait_recv()

        loop(first, first + sources, arrive)
        x_rows = x_in[block, :]
        logits = nt(x_rows, router)
        gates = jnp.exp(logits - jnp.max(logits, axis=-1, keepdims=True))
        gates = gates / jnp.sum(gates, axis=-1, keepdims=True)
        chosen = jnp.sum(gates * hot, axis=-1, keepdims=True)
        g_rows = (chosen * g_in[block, :].astype(F32)).astype(BF16)
        g_in[block, :] = g_rows
        pack[bias_at + 4 : bias_at + 5, :] += jnp.sum(g_rows.astype(F32), axis=0, keepdims=True)
        acc_o[...] = jnp.broadcast_to(b_out[...].astype(F32), acc_o.shape)
        acc_d[...] = jnp.zeros_like(acc_d)
        def tile(f):
            lanes = aligned(f, FTILE)
            pre = nn(x_in[block, :], w_in[:, lanes]) + b_in[:, lanes].astype(F32)
            d_act = nt(g_in[block, :], w_out[lanes, :])
            cdf = 0.5 + 0.5 * lax.erf(pre * 0.7071067811865476)
            act = (pre * cdf).astype(BF16)
            slope = cdf + pre * jnp.exp(-0.5 * pre * pre) * 0.3989422804014327
            d_row = (d_act * slope).astype(BF16)
            hidden[block, lanes] = act
            d_pre[block, lanes] = d_row
            pack[pl.ds(bias_at + f, 1), :] += jnp.sum(
                d_row.astype(F32), axis=0, keepdims=True
            )
            acc_o[...] += nn(act, w_out[lanes, :])
            acc_d[...] += nt(d_row, w_in[:, lanes])

        loop(0, f_tiles, tile)
        result = acc_o[...]
        weight = jnp.sum(g_in[block, :].astype(F32) * result, axis=-1, keepdims=True)
        d_logits = (weight * (hot - gates)).astype(BF16)
        pack[8:bias_at, :] += tn(d_logits, x_in[block, :])
        ret_d[block, :] = (acc_d[...] + nn(d_logits, router)).astype(BF16)
        ret_o[block, :] = (chosen * result).astype(BF16)

        def back(r):
            @pl.when(r > 0)
            def _():
                give_back(ret_d, table_d, s_d, r_d, r).start()

        loop(first, first + sources, back)

    loop(0, CHUNKS, expert_chunk)
    mine = aligned(at.me, cap_rows)
    table_d[mine, :] = ret_d[0:cap_rows, :]

    part = FTILE // n_x
    per_core = f_tiles // 2

    def e_tile(core, j):
        return (core * per_core + j // 2) * 2 + j % 2

    def to_partner(j):
        return remote(ew.at[e_tile(other, j)], ew_core.at[j], s_ec.at[j], r_ec.at[j], at.partner())

    def to_x(i, j):
        src = ew.at[e_tile(at.core, j), aligned(at.x_index(i), part), :]
        return remote(src, ew_x.at[i - 1, j], s_ex.at[i - 1, j], r_ex.at[i - 1, j], at.x_peer(i))

    def e_part(core, j, x):
        return e_tile(core, j), aligned(x, part)

    def all_x(i, j):
        src = ew.at[e_tile(at.core, j), aligned(at.x, part), :]
        dst = ew_core.at[j, aligned(at.x, part), :]
        return remote(src, dst, s_ea.at[i - 1, j], r_ea.at[i - 1, j], at.x_peer(i))

    def from_x(i, j):
        dst = ew_core.at[j, aligned(x_back(i), part), :]
        return remote(dst, dst, s_ea.at[i - 1, j], r_ea.at[i - 1, j], at.x_peer(i))

    def e_result(i, j):
        piece = aligned(x_back(i), part)
        return ew.at[e_tile(at.core, j), piece, :] if i == 0 else ew_core.at[j, piece, :]

    def to_core(i, j, core):
        dst = o_expert.at[e_tile(core, j), aligned(x_back(i), part), :]
        return remote(e_result(i, j), dst, s_eb.at[i, j], r_eb.at[i, j], at.partner())

    def to_self(i, j):
        dst = o_expert.at[e_tile(at.core, j), aligned(x_back(i), part), :]
        return pltpu.make_async_copy(e_result(i, j), dst, s_self.at[i, j])

    n_mine = 2 * per_core

    def grad_tiles(core, f):
        tile = core * per_core + f
        lanes = aligned(tile, FTILE)
        ew[2 * tile] = tn(x_in[...], d_pre[:, lanes]).astype(BF16)
        ew[2 * tile + 1] = tn(hidden[:, lanes], g_in[...]).astype(BF16)

    def theirs(f):
        grad_tiles(other, f)
        to_partner(2 * f).start()
        to_partner(2 * f + 1).start()

    def sum_cores(j):
        to_partner(j).wait_recv()
        tile = e_tile(at.core, j)
        ew[tile] = (ew[tile].astype(F32) + ew_core[j].astype(F32)).astype(BF16)
        for i in range(1, n_x):
            to_x(i, j).start()

    def tile_row(f):
        theirs(f)
        grad_tiles(at.core, f)
        sum_cores(2 * f)
        sum_cores(2 * f + 1)

    loop(0, per_core, tile_row)

    table_o = send_x

    def left(k):
        send_rows(send_x, x_in, s_x, r_x, k).wait_send()

    loop(1, n_f, left)
    table_o[mine, :] = ret_o[0:cap_rows, :]

    def tell(k):
        pl.semaphore_signal(ready, inc=1, device_id=at.fsdp_peer(k), device_id_type=MESH)

    loop(1, n_f, tell)
    pl.semaphore_wait(ready, n_f - 1)

    def send_lot(lot):
        def one(step):
            r = 1 + lax.rem(n_f // 2 - 1 + step, n_f - 1)
            give_back(ret_o, table_o, s_o, r_o, r).start()

        loop(lax.div((n_f - 1) * lot, LOTS), lax.div((n_f - 1) * (lot + 1), LOTS), one)

    loop(0, 2, send_lot)

    def returned(buffer, into, send, recv, r):
        home = at.ahead(n_f - r)
        return remote(
            buffer.at[aligned(r, cap_rows), :],
            into.at[aligned(home, cap_rows), :],
            send.at[r],
            recv.at[r],
            at.fsdp_peer(r),
        )

    def e_spread(j):
        for i in range(1, n_x):
            to_x(i, j).wait_recv()
        tile = e_tile(at.core, j)
        own = aligned(at.x, part)
        total = ew[tile, own, :].astype(F32)
        for i in range(1, n_x):
            total = total + ew_x[i - 1, j].astype(F32)
        ew[tile, own, :] = total.astype(BF16)
        for i in range(1, n_x):
            all_x(i, j).start()
        to_core(0, j, at.core).start()
        to_self(0, j).start()

    def e_forward(j):
        for i in range(1, n_x):
            from_x(i, j).wait_recv()
            to_core(i, j, at.core).start()
            to_self(i, j).start()

    loop(0, n_mine // 2, e_spread)
    loop(1, n_f, lambda r: returned(ret_d, table_d, s_d, r_d, r).wait_recv())

    loop(1, n_f, lambda k: send_rows(send_g, g_in, s_g, r_g, k).wait_send())
    d_mixed = send_g

    table_iota = lax.broadcasted_iota(jnp.int32, (ROWBLK, n_f * cap_rows), 1).astype(F32)

    def gather_rows(block):
        hit = (table_iota == place[block, 0:1]) | (table_iota == place[block, 1:2])
        return jnp.where(hit, 1.0, 0.0).astype(BF16)

    def norm_back(grad, value, inv_std, gain):
        scaled = grad * gain
        return inv_std * (
            scaled
            - jnp.mean(scaled, axis=-1, keepdims=True)
            - value * jnp.mean(scaled * value, axis=-1, keepdims=True)
        )

    def second_back(i):
        block = aligned(i, ROWBLK)
        grad = nn(gather_rows(block), table_d[...])
        value, inv_std = normalize(middle[block, :])
        pack[5:6, :] += jnp.sum(grad * value, axis=0, keepdims=True)
        pack[6:7, :] += jnp.sum(grad, axis=0, keepdims=True)
        total = cot[block, :].astype(F32) + norm_back(grad, value, inv_std, vecs[5:6, :])
        d_middle[block, :] = total
        low = total.astype(BF16)
        routed[block, :] = low
        pack[4:5, :] += jnp.sum(low.astype(F32), axis=0, keepdims=True)
        d_mixed[block, :] = nt(low, wfull[:, 3 * WIDTH : 4 * WIDTH]).astype(BF16)

    loop(0, SLOTS // ROWBLK, second_back)

    d_wo = tn(mixed[...], routed[...])
    for pair in range(PAIRS):
        hidden[WIDTH * 2 : WIDTH * 3, (4 * pair + 3) * TILE : (4 * pair + 4) * TILE] = d_wo[:, pair * TILE : (pair + 1) * TILE].astype(BF16)

    units = 16 // n_d
    pairs_in_unit = PAIRS // units

    def own_rows(owner):
        return pl.ds(pl.multiple_of(WIDTH * 2 + owner * shard, shard), shard)

    def dense(tile):
        return hidden.at[WIDTH * 2 : WIDTH * 3, aligned(tile, TILE)]

    def g_core(u, x):
        src = dense(u * n_d + x * 2 + other)
        return remote(src, dense_core.at[u, x], s_gc.at[u, x], r_gc.at[u, x], at.partner())

    def g_x(u, i):
        src = dense(u * n_d + at.x_index(i) * 2 + at.core)
        return remote(
            src, dense_x.at[u, i - 1], s_gx.at[u, i - 1], r_gx.at[u, i - 1], at.x_peer(i)
        )

    def g_f(u, k):
        src = hidden.at[own_rows(at.ahead(k)), aligned(u * n_d + at.d, TILE)]
        return remote(src, dense_f.at[u, k], s_gf.at[u, k], r_gf.at[u, k], at.fsdp_peer(k))

    def g_d(u, i):
        src = final.at[u * n_d + at.d]
        return remote(src, src, s_gd.at[u, i], r_gd.at[u, i], at.dp_peer(i))

    def g_d_from(u, i):
        dst = final.at[u * n_d + lax.rem(at.d + n_d - i, n_d)]
        return remote(dst, dst, s_gd.at[u, i], r_gd.at[u, i], at.dp_peer(i))

    def first_hop(u):
        for x in range(n_x):
            g_core(u, x).start()

    def second_hop(u):
        for x in range(n_x):
            g_core(u, x).wait_recv()
            tile = dense(u * n_d + x * 2 + at.core)
            tile[...] = (tile[...].astype(F32) + dense_core[u, x].astype(F32)).astype(BF16)
        for i in range(1, n_x):
            g_x(u, i).start()

    def third_hop(u):
        tile = dense(u * n_d + at.d)
        total = tile[...].astype(F32)
        for i in range(1, n_x):
            g_x(u, i).wait_recv()
            total = total + dense_x[u, i - 1].astype(F32)
        tile[...] = total.astype(BF16)
        loop(1, n_f, lambda k: g_f(u, k).start())

    def fourth_hop(u):
        tile = u * n_d + at.d
        dense_f[u, 0] = hidden[own_rows(at.me), aligned(tile, TILE)]
        loop(1, n_f, lambda k: g_f(u, k).wait_recv())
        total = dense_f[u, 0].astype(F32)
        for k in range(1, n_f):
            total = total + dense_f[u, k].astype(F32)
        final[tile] = total.astype(BF16)
        for i in range(1, n_d):
            g_d(u, i).start()

    hops = (first_hop, second_hop, third_hop, fourth_hop)

    def attend_back(pair):
        for b, (low, high, row) in enumerate(WINDOWS):
            window = slice(row, row + high - low)
            grad = d_mixed[b * QBLK : (b + 1) * QBLK, aligned(pair, TILE)]
            values = qkv[2 * PAIRS + pair, low:high, :]
            for h in range(2):
                one = jnp.where(halves[h], grad, jnp.zeros_like(grad))
                scores[h, window, :] = nt(values, one)
        for b, (low, high, row) in enumerate(WINDOWS):
            window = slice(row, row + high - low)
            for h in range(2):
                share = probs[2 * pair + h, window, :].astype(F32)
                moved = share * scores[h, window, :]
                moved = moved - share * jnp.sum(moved, axis=0, keepdims=True)
                d_pre[window, h * 256 : h * 256 + QBLK] = moved.astype(BF16)
        for array in (acc_k, acc_v):
            array[...] = jnp.zeros_like(array)
        for b, (low, high, row) in enumerate(WINDOWS):
            window = slice(row, row + high - low)
            block = slice(b * QBLK, (b + 1) * QBLK)
            keys = qkv[PAIRS + pair, low:high, :]
            query = qkv[pair, block, :]
            grad = d_mixed[block, aligned(pair, TILE)]
            both = [
                [
                    tn(d_pre[window, h * 256 : h * 256 + QBLK], keys),
                    nn(d_pre[window, h * 256 : h * 256 + QBLK], query),
                    nn(probs[2 * pair + h, window, :], grad),
                ]
                for h in range(2)
            ]
            d_q, d_k, d_v = [jnp.where(halves[0], one, two) for one, two in zip(*both)]
            hidden[block, pl.ds(pl.multiple_of(pair * 384, 128), 128)] = (d_q * 0.125).astype(BF16)
            acc_k[low:high, :] += d_k
            acc_v[low:high, :] += d_v
        hidden[0:SLOTS, pl.ds(pl.multiple_of(pair * 384 + 128, 128), 128)] = acc_k[...].astype(BF16)
        hidden[0:SLOTS, pl.ds(pl.multiple_of(pair * 384 + 256, 128), 128)] = acc_v[...].astype(BF16)
        d_qkv = hidden[0:SLOTS, pl.ds(pl.multiple_of(pair * 384, 128), 384)]
        sums = jnp.sum(d_qkv.astype(F32), axis=0, keepdims=True)
        pack[2:3, aligned(pair, TILE)] = sums[:, 0:128]
        pack[3:4, aligned(pair, TILE)] = sums[:, 256:384]
        d_w = tn(normed[...], d_qkv)
        for c in range(3):
            dense(4 * pair + c)[...] = d_w[:, c * TILE : (c + 1) * TILE].astype(BF16)

        @pl.when(lax.rem(pair, pairs_in_unit) == pairs_in_unit - 1)
        def _():
            unit = lax.div(pair, pairs_in_unit)
            for age, hop in enumerate(hops):

                @pl.when(unit >= age)
                def _(age=age, hop=hop):
                    hop(unit - age)

        send_lot(pair + 2)

        @pl.when(pair == 1)
        def _():
            loop(n_mine // 2, n_mine - 1, e_spread)


    acc_k, acc_v = bias.at[0:SLOTS, 0:TILE], bias.at[0:SLOTS, TILE : 2 * TILE]
    loop(0, PAIRS, attend_back)

    def later(step):
        for age, hop in enumerate(hops):
            if 0 <= step - age < units:
                hop(step - age)

    later(units)
    send_lot(PAIRS + 2)

    def first_back(i):
        block = aligned(i, ROWBLK)
        grad = nt(hidden[block, 0 : 3 * WIDTH], wfull[:, 0 : 3 * WIDTH])
        value, inv_std = normalize(tok[block, :].astype(F32))
        pack[0:1, :] += jnp.sum(grad * value, axis=0, keepdims=True)
        pack[1:2, :] += jnp.sum(grad, axis=0, keepdims=True)
        d_middle[block, :] += norm_back(grad, value, inv_std, vecs[0:1, :])

    loop(0, SLOTS // ROWBLK, first_back)
    save_tokens = pltpu.make_async_copy(d_middle.at[0:SLOTS, :], o_tokens, s_own.at[2 + n_mine])
    save_tokens.start()

    def p_dp(i):
        return remote(pack, pack_dp.at[i], s_p.at[i], r_p.at[i], at.dp_peer(i))

    for i in range(1, n_d):
        p_dp(i).start()
    later(units + 1)
    e_spread(n_mine - 1)
    loop(0, n_mine - 1, e_forward)

    def vec_lane(owner):
        return aligned(lax.div(owner * shard, TILE), TILE)

    def qv_lane(owner):
        return aligned(lax.div(lax.rem(owner * 2 * shard, WIDTH), TILE), TILE)

    def p_vec(k):
        src = pack_dp.at[0, 0:bias_at, vec_lane(at.ahead(k))]
        return remote(src, vec_f.at[k], s_vf.at[k], r_vf.at[k], at.fsdp_peer(k))

    def p_qv(k):
        src = pack_dp.at[0, 0:8, qv_lane(at.ahead(k))]
        return remote(src, qv_f.at[k], s_qf.at[k], r_qf.at[k], at.fsdp_peer(k))

    pack_dp[0] = pack[...]
    for i in range(1, n_d):
        p_dp(i).wait_recv()
        pack_dp[0] += pack_dp[i]
    loop(1, n_f, lambda k: [p_vec(k).start(), p_qv(k).start()])
    save_bias = pltpu.make_async_copy(
        pack_dp.at[0, bias_at : bias_at + 8, :], o_bias, s_own.at[3 + n_mine]
    )
    save_bias.start()
    later(units + 2)
    e_forward(n_mine - 1)

    loop(1, n_f, lambda r: returned(ret_o, table_o, s_o, r_o, r).wait_recv())

    def combine(i):
        block = aligned(i, ROWBLK)
        total = middle[block, :] + nn(gather_rows(block), table_o[...])
        routed[block, :] = total.astype(BF16)

    loop(0, SLOTS // ROWBLK, combine)
    save_out = pltpu.make_async_copy(routed, o_out, s_own.at[4 + n_mine])
    save_out.start()

    loop(1, n_f, lambda k: [p_vec(k).wait_recv(), p_qv(k).wait_recv()])
    vec_f[0] = pack_dp[0, 0:bias_at, vec_lane(at.me)]
    qv_f[0] = pack_dp[0, 0:8, qv_lane(at.me)]

    def add_lanes(k):
        vec_f[0] += vec_f[k]
        qv_f[0] += qv_f[k]

    loop(1, n_f, add_lanes)
    save_vec = pltpu.make_async_copy(vec_f.at[0], o_vec, s_own.at[5 + n_mine])
    save_qv = pltpu.make_async_copy(qv_f.at[0], o_qv, s_own.at[6 + n_mine])
    save_vec.start()
    save_qv.start()
    loop(0, units, lambda u: [g_d_from(u, i).wait_recv() for i in range(1, n_d)])
    save_dense = pltpu.make_async_copy(final, o_dense, s_own.at[7 + n_mine])
    save_dense.start()

    def ended_f(k):
        send_v(k).wait_send()
        got_w(k).wait_send()
        for i in range(1, n_x):
            share_x(i, k).wait_send()
        for i in range(n_x):
            share_core(i, k).wait_send()
        give_back(ret_d, table_d, s_d, r_d, k).wait_send()
        give_back(ret_o, table_o, s_o, r_o, k).wait_send()
        p_vec(k).wait_send()
        p_qv(k).wait_send()

    loop(1, n_f, ended_f)

    def ended_e(j):
        to_partner(j).wait_send()
        for i in range(1, n_x):
            to_x(i, j).wait_send()
            all_x(i, j).wait_send()
        for i in range(n_x):
            to_core(i, j, at.core).wait_send()
            to_core(i, j, other).wait_recv()
            to_self(i, j).wait()

    loop(0, n_mine, ended_e)

    def ended_u(u):
        for x in range(n_x):
            g_core(u, x).wait_send()
        for i in range(1, n_x):
            g_x(u, i).wait_send()
        loop(1, n_f, lambda k: g_f(u, k).wait_send())
        for i in range(1, n_d):
            g_d(u, i).wait_send()

    loop(0, units, ended_u)
    for i in range(1, n_d):
        p_dp(i).wait_send()
    for copy in (save_tokens, save_bias, save_out, save_vec, save_qv, save_dense):
        copy.wait()


def block(n_f, n_d, experts, cap, cap_rows, small, w_in, w_out, b_in, b_out):
    vmem = pl.BlockSpec(memory_space=pltpu.VMEM)
    hbm = pl.BlockSpec(memory_space=pl.ANY)
    n_x = n_d // 2
    more_x = max(n_x - 1, 1)
    vec_rows = -(-(8 + experts) // 16) * 16
    shard = WIDTH // n_f
    table = n_f * cap_rows
    hid = w_in.shape[1]
    units = 16 // n_d
    n_mine = hid // FTILE
    pack_rows = 8 + experts + 8
    sds = jax.ShapeDtypeStruct
    vm = pltpu.VMEM
    dma = pltpu.SemaphoreType.DMA
    chunk_rows = table // CHUNKS
    pairs_of = lambda *shape: [dma(shape), dma(shape)]
    return pl.pallas_call(
        functools.partial(block_kernel, n_f, n_d, experts, cap, cap_rows),
        out_shape=(
            sds((SLOTS, WIDTH), BF16),
            sds((SLOTS, WIDTH), F32),
            sds((2 * n_mine, FTILE, WIDTH), BF16),
            sds((16, shard, TILE), BF16),
            sds((8 + experts, TILE), F32),
            sds((8, TILE), F32),
            sds((8, WIDTH), F32),
        ),
        in_specs=[vmem] * len(small) + [hbm] * 2 + [vmem] * 2,
        out_specs=[hbm] * 7,
        scratch_shapes=[
            vm((WIDTH, 4 * WIDTH), BF16),
            vm((vec_rows, WIDTH), BF16),
            vm((vec_rows, WIDTH), F32),
            vm((KEYS, 2 * TILE), F32),
            vm((2, KEYS, QBLK), F32),
            vm((2 * PAIRS, KEYS, QBLK), BF16),
            vm((3 * PAIRS, SLOTS, TILE), BF16),
            vm((SLOTS, WIDTH), BF16),
            vm((SLOTS, WIDTH), BF16),
            vm((SLOTS, WIDTH), F32),
            vm((SLOTS, WIDTH), BF16),
            vm((SLOTS, 8), F32),
        ]
        + [vm((table, WIDTH), BF16)] * 4
        + [
            vm((WIDTH, hid), BF16),
            vm((hid, WIDTH), BF16),
            vm((table, hid), BF16),
            vm((table, hid), BF16),
        ]
        + [vm((table, WIDTH), BF16)] * 3
        + [
            vm((2 * n_mine, FTILE, WIDTH), BF16),
            vm((n_mine, FTILE, WIDTH), BF16),
            vm((more_x, n_mine, FTILE // n_x, WIDTH), BF16),
            vm((units, n_x, WIDTH, TILE), BF16),
            vm((units, more_x, WIDTH, TILE), BF16),
            vm((units, n_f, shard, TILE), BF16),
            vm((16, shard, TILE), BF16),
            vm((pack_rows, WIDTH), F32),
            vm((n_d, pack_rows, WIDTH), F32),
            vm((n_f, 8 + experts, TILE), F32),
            vm((n_f, 8, TILE), F32),
            vm((max(2 * chunk_rows, SLOTS), WIDTH), F32),
        ]
        + pairs_of(n_f)
        + pairs_of(n_f)
        + pairs_of(more_x, n_f)
        + pairs_of(n_x, n_f)
        + pairs_of(n_f)
        + pairs_of(n_f)
        + pairs_of(n_f)
        + pairs_of(n_f)
        + pairs_of(n_mine)
        + pairs_of(more_x, n_mine)
        + pairs_of(more_x, n_mine)
        + pairs_of(n_x, n_mine)
        + pairs_of(units, n_x)
        + pairs_of(units, more_x)
        + pairs_of(units, n_f)
        + pairs_of(units, n_d)
        + pairs_of(n_d)
        + pairs_of(n_f)
        + pairs_of(n_f)
        + [dma((8 + n_mine,)), dma((n_x, n_mine)), pltpu.SemaphoreType.REGULAR],
        compiler_params=pltpu.CompilerParams(
            collective_id=0, has_side_effects=True, vmem_limit_bytes=63 << 20
        ),
        name="block",
    )(*small, w_in, w_out, b_in, b_out)


def finish_kernel(
    n_f,
    experts,
    in_out,
    in_tokens,
    in_expert,
    dense,
    vec,
    qv,
    biases,
    o_out,
    o_tokens,
    o_g1,
    o_s1,
    o_qkv,
    o_bqv,
    o_wo,
    o_bo,
    o_g2,
    o_s2,
    o_router,
    o_w_in,
    o_b_in,
    o_w_out,
    o_b_out,
    low,
    wide,
    rows_low,
    rows_wide,
    s_load,
    s_save,
):
    me = lax.axis_index("fsdp")
    shard = WIDTH // n_f
    tiles = in_expert.shape[0]
    loads = [pltpu.make_async_copy(in_expert.at[t], low.at[t], s_load.at[t]) for t in range(tiles)]
    for load in loads:
        load.start()
    rows_in = [
        pltpu.make_async_copy(in_out, rows_low, s_load.at[tiles]),
        pltpu.make_async_copy(in_tokens, rows_wide, s_load.at[tiles + 1]),
    ]
    for load in rows_in:
        load.start()

    def my_lanes(value, size):
        place = lax.rem(me * size, TILE)
        total = jnp.zeros((value.shape[0], size), F32)
        for low_lane in range(0, TILE, size):
            total = total + jnp.where(place == low_lane, value[:, low_lane : low_lane + size], 0.0)
        return total

    own = my_lanes(vec[...], shard)
    for row, ref in ((0, o_g1), (1, o_s1), (4, o_bo), (5, o_g2), (6, o_s2)):
        ref[...] = own[row : row + 1, :]
    o_router[...] = own[8 : 8 + experts, :]
    lines = my_lanes(qv[...], 2 * shard)
    o_bqv[...] = jnp.where(me * 2 * shard < WIDTH, lines[2:3, :], lines[3:4, :])
    for pair in range(PAIRS):
        for c in range(3):
            at = c * WIDTH + pair * TILE
            o_qkv[:, at : at + TILE] = dense[4 * pair + c].astype(F32)
        o_wo[:, pair * TILE : (pair + 1) * TILE] = dense[4 * pair + 3].astype(F32)
    for f in range(tiles // 2):
        o_b_in[:, f * FTILE : (f + 1) * FTILE] = biases[f : f + 1, :]
    o_b_out[...] = biases[4:5, :]
    saves = []
    for t in range(tiles):
        loads[t].wait()
        wide[t] = low[t].astype(F32)
        piece = pl.ds(t // 2 * FTILE, FTILE)
        dst = o_w_out.at[0, piece, :] if t % 2 else o_w_in.at[0, :, piece]
        saves.append(pltpu.make_async_copy(wide.at[t], dst, s_save.at[t]))
        saves[-1].start()
    rows_out = [
        pltpu.make_async_copy(rows_low, o_out, s_save.at[tiles]),
        pltpu.make_async_copy(rows_wide, o_tokens, s_save.at[tiles + 1]),
    ]
    for load, save in zip(rows_in, rows_out):
        load.wait()
        save.start()
    for save in saves + rows_out:
        save.wait()


def finish(n_f, experts, hid, parts):
    vmem = pl.BlockSpec(memory_space=pltpu.VMEM)
    hbm = pl.BlockSpec(memory_space=pl.ANY)
    shard = WIDTH // n_f
    tiles = parts[2].shape[0]
    line = lambda *shape: jax.ShapeDtypeStruct(shape, F32)
    return pl.pallas_call(
        functools.partial(finish_kernel, n_f, experts),
        out_shape=(
            jax.ShapeDtypeStruct((SLOTS, WIDTH), BF16),
            line(SLOTS, WIDTH),
            line(1, shard),
            line(1, shard),
            line(shard, 3 * WIDTH),
            line(1, 2 * shard),
            line(shard, WIDTH),
            line(1, shard),
            line(1, shard),
            line(1, shard),
            line(experts, shard),
            line(1, WIDTH, hid),
            line(1, hid),
            line(1, hid, WIDTH),
            line(1, WIDTH),
        ),
        in_specs=[hbm] * 3 + [vmem] * 4,
        out_specs=[hbm] * 2 + [vmem] * 9 + [hbm, vmem, hbm, vmem],
        scratch_shapes=[
            pltpu.VMEM((tiles, FTILE, WIDTH), BF16),
            pltpu.VMEM((tiles, FTILE, WIDTH), F32),
            pltpu.VMEM((SLOTS, WIDTH), BF16),
            pltpu.VMEM((SLOTS, WIDTH), F32),
            pltpu.SemaphoreType.DMA((tiles + 2,)),
            pltpu.SemaphoreType.DMA((tiles + 2,)),
        ],
        compiler_params=pltpu.CompilerParams(vmem_limit_bytes=62 << 20),
        name="finish",
    )(*parts)


def shards(
    tokens,
    cotangent,
    segment_ids,
    pad_mask,
    expert_ids,
    priority,
    ln1_gain,
    ln1_shift,
    w_qkv,
    b_qv,
    w_o,
    b_o,
    ln2_gain,
    ln2_shift,
    w_router,
    w_in,
    b_in,
    w_out,
    b_out,
    n_f,
    n_d,
):
    experts = w_router.shape[1]
    cap = (21 * tokens.shape[0] + 10 * experts - 1) // (10 * experts)
    cap_rows = -(-cap // 16) * 16
    line = lambda vector: vector.reshape(1, -1)
    small = (
        tokens,
        cotangent,
        line(segment_ids),
        line(pad_mask),
        expert_ids.T,
        priority,
        w_qkv,
        w_o,
        line(ln1_gain),
        line(ln1_shift),
        line(b_qv),
        line(b_o),
        line(ln2_gain),
        line(ln2_shift),
        w_router.T,
    )
    parts = block(n_f, n_d, experts, cap, cap_rows, small, w_in[0], w_out[0], b_in, b_out)
    done = finish(n_f, experts, w_in.shape[2], parts)
    flat = (2, 3, 5, 7, 8, 9)
    done = [value.reshape(-1) if i in flat else value for i, value in enumerate(done)]
    done[10] = done[10].T
    return tuple(done)


def solution(mesh):
    both, one = P(("dp", "fsdp")), P("fsdp")
    n_f, n_d = mesh.shape["fsdp"], mesh.shape["dp"]
    return jax.shard_map(
        functools.partial(shards, n_f=n_f, n_d=n_d),
        mesh=mesh,
        in_specs=(both,) * 6 + (one,) * 13,
        out_specs=(both,) * 2 + (one,) * 13,
        check_vma=False,
    )
```

```python
import functools

import jax
import jax.numpy as jnp
from jax import lax
from jax.experimental import pallas as pl
from jax.experimental.pallas import tpu as pltpu
from jax.sharding import PartitionSpec as P

MESH = pl.DeviceIdType.MESH
BF16 = jnp.bfloat16
F32 = jnp.float32
SLOTS = 720
WIDTH = 512
PAIRS = 4
EPS = 1e-06
WINDOWS = ((0, 384, 0), (96, 624, 384), (336, 720, 912))
KEYS = 1296
QBLK = 240
ROWBLK = 240
TILE = 128
FTILE = 512
CHUNKS = 4
LOTS = 7


def nt(left, right):
    return lax.dot_general(left, right, (((1,), (1,)), ((), ())), preferred_element_type=F32)


def tn(left, right):
    return lax.dot_general(left, right, (((0,), (0,)), ((), ())), preferred_element_type=F32)


def nn(left, right):
    return jnp.dot(left, right, preferred_element_type=F32)


def normalize(value):
    centred = value - jnp.mean(value, axis=-1, keepdims=True)
    inv_std = lax.rsqrt(jnp.mean(centred * centred, axis=-1, keepdims=True) + EPS)
    return centred * inv_std, inv_std


def aligned(index, size):
    return pl.ds(pl.multiple_of(index * size, size), size)


class Place:
    def __init__(self, n_f, n_d):
        self.n_f, self.n_d, self.n_x = n_f, n_d, n_d // 2
        self.me = lax.axis_index("fsdp")
        self.d = lax.axis_index("dp")
        self.x = lax.div(self.d, 2)
        self.core = lax.rem(self.d, 2)

    def ahead(self, k):
        return lax.rem(self.me + k, self.n_f)

    def fsdp_peer(self, k):
        return (self.d, self.ahead(k))

    def x_index(self, i):
        return lax.rem(self.x + i, self.n_x)

    def x_peer(self, i):
        return (self.x_index(i) * 2 + self.core, self.me)

    def partner(self):
        return (self.x * 2 + 1 - self.core, self.me)

    def dp_peer(self, i):
        return (lax.rem(self.d + i, self.n_d), self.me)

    def enter(self):
        bar = pltpu.get_barrier_semaphore()

        def greet(k, _):
            pl.semaphore_signal(bar, inc=1, device_id=self.fsdp_peer(k), device_id_type=MESH)
            return 0

        lax.fori_loop(1, self.n_f, greet, 0)
        for i in range(1, self.n_d):
            pl.semaphore_signal(bar, inc=1, device_id=self.dp_peer(i), device_id_type=MESH)
        pl.semaphore_wait(bar, self.n_f - 1 + self.n_d - 1)


def remote(src, dst, send_sem, recv_sem, device):
    return pltpu.make_async_remote_copy(
        src_ref=src,
        dst_ref=dst,
        send_sem=send_sem,
        recv_sem=recv_sem,
        device_id=device,
        device_id_type=MESH,
    )


def loop(low, high, body):
    def step(k, carry):
        body(k)
        return carry

    lax.fori_loop(low, high, step, 0)


def y_members(n_f):
    return 1 << ((n_f.bit_length() - 1) // 2)


def block_kernel(
    n_f,
    n_d,
    experts,
    cap,
    cap_rows,
    tok,
    cot,
    segment,
    pad,
    chosen_ids,
    priority,
    w_qkv,
    w_o,
    gain_one,
    shift_one,
    b_qv,
    b_o,
    gain_two,
    shift_two,
    w_router,
    w_in_hbm,
    w_out_hbm,
    b_in,
    b_out,
    o_out,
    o_tokens,
    o_expert,
    o_dense,
    o_vec,
    o_qv,
    o_bias,
    wfull,
    vsh,
    vecs,
    bias,
    scores,
    probs,
    qkv,
    normed,
    mixed,
    middle,
    routed,
    place,
    send_x,
    send_g,
    x_in,
    g_in,
    w_in,
    w_out,
    hidden,
    d_pre,
    ret_d,
    ret_o,
    table_d,
    ew,
    ew_core,
    ew_x,
    dense_core,
    dense_y,
    dense_z,
    dense_s,
    dense_x,
    final,
    pack,
    pack_dp,
    vec_f,
    qv_f,
    d_middle,
    s_w,
    r_w,
    s_v,
    r_v,
    s_dx,
    r_dx,
    s_dc,
    r_dc,
    s_g,
    r_g,
    s_x,
    r_x,
    s_d,
    r_d,
    s_o,
    r_o,
    s_ec,
    r_ec,
    s_ex,
    r_ex,
    s_ea,
    r_ea,
    s_eb,
    r_eb,
    s_gc,
    r_gc,
    s_gy,
    r_gy,
    s_gz,
    r_gz,
    s_gx,
    r_gx,
    s_gd,
    r_gd,
    s_p,
    r_p,
    s_vf,
    r_vf,
    s_qf,
    r_qf,
    s_own,
    s_self,
    ready,
):
    at = Place(n_f, n_d)
    n_x = at.n_x
    shard = WIDTH // n_f
    colw = 4 * WIDTH // n_d
    other = 1 - at.core

    def cols_of(d):
        return aligned(d, colw)

    def w_piece(owner, d):
        return wfull.at[aligned(owner, shard), cols_of(d)]

    def x_back(i):
        return at.x_index(n_x - i)

    load_in = pltpu.make_async_copy(w_in_hbm, w_in, s_own.at[0])
    load_out = pltpu.make_async_copy(w_out_hbm, w_out, s_own.at[1])
    load_in.start()
    load_out.start()
    at.enter()

    n_y = y_members(n_f)
    n_z = n_f // n_y
    my_z, my_y = lax.div(at.me, n_y), lax.rem(at.me, n_y)

    def member(z, y):
        return lax.rem(my_z + z, n_z) * n_y + lax.rem(my_y + y, n_y)

    def owner(k):
        return member(n_z - lax.rem(k, n_z), n_y - lax.div(k, n_z))

    def along_z(k):
        piece = w_piece(at.me, at.d)
        return remote(piece, piece, s_w.at[k], r_w.at[k], (at.d, member(k, 0)))

    def along_y(j, i):
        piece, k = w_piece(member(n_z - i, 0), at.d), j * n_z + i
        return remote(piece, piece, s_w.at[k], r_w.at[k], (at.d, member(0, j)))

    def got_w(k):
        piece = w_piece(owner(k), at.d)
        return remote(piece, piece, s_w.at[k], r_w.at[k], (at.d, at.me))

    vec_rows = vsh.shape[0]

    def vec_piece(owner):
        return hidden.at[aligned(owner, vec_rows), 0:WIDTH]

    def send_v(k):
        return remote(vsh, vec_piece(at.me), s_v.at[k], r_v.at[k], at.fsdp_peer(k))

    def share_x(i, k):
        piece = w_piece(owner(k), at.d)
        return remote(piece, piece, s_dx.at[i - 1, k], r_dx.at[i - 1, k], at.x_peer(i))

    def share_core(i, k):
        piece = w_piece(owner(k), x_back(i) * 2 + at.core)
        return remote(piece, piece, s_dc.at[i, k], r_dc.at[i, k], at.partner())

    own = aligned(at.me, shard)
    for pair in range(PAIRS):
        for c in range(3):
            low = (3 * pair + c) * TILE
            src = c * WIDTH + pair * TILE
            wfull[own, low : low + TILE] = w_qkv[:, src : src + TILE]
    wfull[own, 3 * WIDTH : 4 * WIDTH] = w_o[...]
    loop(1, n_z, lambda k: along_z(k).start())
    loop(1, n_y, lambda j: along_y(j, 0).start())

    def placing(size, low):
        shape = (size, WIDTH)
        target = lax.broadcasted_iota(jnp.int32, shape, 1) + low
        source = lax.broadcasted_iota(jnp.int32, shape, 0) + at.me * size
        return jnp.where(target == source, 1.0, 0.0).astype(BF16)

    blank = jnp.zeros((1, shard), F32)
    stack = [
        blank if ref is None else ref[...].astype(F32)
        for ref in (gain_one, shift_one, None, None, b_o, gain_two, shift_two, None)
    ]
    spread = nn(jnp.concatenate(stack, axis=0).astype(BF16), placing(shard, 0))
    row_iota = lax.broadcasted_iota(jnp.int32, (8, WIDTH), 0)
    for r in range(2):
        line = nn(b_qv[...], placing(2 * shard, r * WIDTH))
        spread = spread + jnp.where(row_iota == 2 + r, line, 0.0)
    router_rows = nn(w_router[...], placing(shard, 0))
    rest = jnp.zeros((vec_rows - 8 - experts, WIDTH), F32)
    parts = [spread, router_rows] + ([rest] if vec_rows > 8 + experts else [])
    vsh[...] = jnp.concatenate(parts, axis=0).astype(BF16)
    vec_piece(at.me)[...] = vsh[...]
    loop(1, n_f, lambda k: send_v(k).start())

    seg_r, pad_r, pri_r = (
        ref[...].reshape(1, SLOTS).astype(F32) for ref in (segment, pad, priority)
    )
    lines = jnp.concatenate([seg_r, pad_r, pri_r, jnp.zeros((5, SLOTS), F32)], axis=0)
    columns = jnp.transpose(lines)
    seg_c, pad_c, pri_c = (columns[:, j : j + 1] for j in range(3))
    expert_iota = lax.broadcasted_iota(jnp.int32, (experts, SLOTS), 0)
    live = pad_r > 0
    before = jnp.where(pri_c < pri_r, 1.0, 0.0).astype(BF16)
    chose = [jnp.where((chosen_ids[k : k + 1, :] == expert_iota) & live, 1.0, 0.0) for k in range(2)]
    rank = [nn(one.astype(BF16), before) for one in chose]
    rank[1] = rank[1] + jnp.sum(chose[0], axis=1, keepdims=True)
    spot_r = []
    for k in range(2):
        slot = jnp.sum(chose[k] * rank[k], axis=0, keepdims=True)
        spot = chosen_ids[k : k + 1, :].astype(F32) * cap_rows + slot
        spot_r.append(jnp.where(live & (slot < cap), spot, -1.0))
    place[...] = jnp.transpose(jnp.concatenate(spot_r + [jnp.zeros((6, SLOTS), F32)], axis=0))
    slot_iota = lax.broadcasted_iota(jnp.int32, (cap_rows, SLOTS), 0)

    def pick(expert):
        mine = (slot_iota + expert * cap_rows).astype(F32)
        return jnp.where((mine == spot_r[0]) | (mine == spot_r[1]), 1.0, 0.0).astype(BF16)

    for b, (low, high, row) in enumerate(WINDOWS):
        queries = slice(b * QBLK, (b + 1) * QBLK)
        shape = (high - low, QBLK)
        same = seg_c[low:high, :] == seg_r[:, queries]
        itself = (lax.broadcasted_iota(jnp.int32, shape, 0) + low) == (
            lax.broadcasted_iota(jnp.int32, shape, 1) + b * QBLK
        )
        allowed = same & ((pad_c[low:high, :] > 0) | itself)
        bias[row : row + high - low, 0:QBLK] = jnp.where(allowed, 0.0, -1e30)

    chunk_rows = n_f * cap_rows // CHUNKS
    sources = n_f // CHUNKS

    def position(step, side):
        inner = lax.rem(lax.div(step + 1, 2), 2)
        near = 1 + 2 * lax.rem(step + 1 + side, 2)
        return inner * near + (1 - inner) * 2 * lax.div(step, 3)

    z_side = lax.rem(my_z, 2)

    def send_rows(buffer, into, send, recv, k):
        return remote(
            buffer.at[aligned(at.ahead(k), cap_rows), :],
            into.at[aligned(n_f - k, cap_rows), :],
            send.at[k],
            recv.at[n_f - k],
            at.fsdp_peer(k),
        )

    def dispatch(source, buffer, into, send, recv):
        into[0:cap_rows, :] = nn(pick(at.me), source[...]).astype(BF16)

        def stage(step):
            first = position(step, 1 - z_side) * sources

            def one(r):
                @pl.when(r > 0)
                def _():
                    k = n_f - r
                    expert = at.ahead(k)
                    rows = nn(pick(expert), source[...]).astype(BF16)
                    buffer[aligned(expert, cap_rows), :] = rows
                    send_rows(buffer, into, send, recv, k).start()

            loop(first, first + sources, one)

        loop(0, CHUNKS, stage)

    def pass_on(k):
        for i in range(1, n_x):
            share_x(i, k).start()
        share_core(0, k).start()

    def from_z(k):
        got_w(k).wait_recv()
        loop(1, n_y, lambda j: along_y(j, k).start())
        pass_on(k)

    def from_y(k):
        got_w(k).wait_recv()
        pass_on(k)

    loop(1, n_z, from_z)
    dispatch(cot, send_g, g_in, s_g, r_g)
    loop(n_z, n_f, from_y)

    loop(1, n_f, lambda k: send_v(k).wait_recv())
    vecs[...] = vec_piece(0)[...].astype(F32)

    def add_vectors(owner):
        vecs[...] += vec_piece(owner)[...].astype(F32)

    loop(1, n_f, add_vectors)

    def first_norm(i):
        block = aligned(i, ROWBLK)
        value, _ = normalize(tok[block, :].astype(F32))
        normed[block, :] = (value * vecs[0:1, :] + vecs[1:2, :]).astype(BF16)

    loop(0, SLOTS // ROWBLK, first_norm)

    for i in range(1, n_x):

        def cross(k, i=i):
            piece = w_piece(owner(k), x_back(i) * 2 + at.core)
            remote(piece, piece, s_dx.at[i - 1, k], r_dx.at[i - 1, k], at.x_peer(i)).wait_recv()
            share_core(i, k).start()

        loop(1, n_f, cross)
    for i in range(n_x):

        def arrive(k, i=i):
            piece = w_piece(owner(k), x_back(i) * 2 + other)
            remote(piece, piece, s_dc.at[i, k], r_dc.at[i, k], at.partner()).wait_recv()

        loop(1, n_f, arrive)

    def project(pair):
        out = nn(normed[...], wfull[:, pl.ds(pl.multiple_of(pair * 384, 128), 384)])
        lanes = aligned(pair, TILE)
        qkv[pair] = ((out[:, 0:128] + vecs[2:3, lanes]) * 0.125).astype(BF16)
        qkv[PAIRS + pair] = out[:, 128:256].astype(BF16)
        qkv[2 * PAIRS + pair] = (out[:, 256:384] + vecs[3:4, lanes]).astype(BF16)

    loop(0, PAIRS, project)

    lane = lax.broadcasted_iota(jnp.int32, (1, TILE), 1)
    halves = (lane < 64, lane >= 64)

    def attend(pair):
        for b, (low, high, row) in enumerate(WINDOWS):
            window = slice(row, row + high - low)
            query = qkv[pair, b * QBLK : (b + 1) * QBLK, :]
            keys = qkv[PAIRS + pair, low:high, :]
            for h in range(2):
                one = jnp.where(halves[h], query, jnp.zeros_like(query))
                scores[h, window, :] = nt(keys, one) + bias[window, 0:QBLK]
        for b, (low, high, row) in enumerate(WINDOWS):
            window = slice(row, row + high - low)
            for h in range(2):
                value = scores[h, window, :]
                power = jnp.exp(value - jnp.max(value, axis=0, keepdims=True))
                share = 1.0 / jnp.sum(power, axis=0, keepdims=True)
                probs[2 * pair + h, window, :] = (power * share).astype(BF16)
        for b, (low, high, row) in enumerate(WINDOWS):
            window = slice(row, row + high - low)
            values = qkv[2 * PAIRS + pair, low:high, :]
            both = [tn(probs[2 * pair + h, window, :], values) for h in range(2)]
            mixed[b * QBLK : (b + 1) * QBLK, aligned(pair, TILE)] = jnp.where(
                halves[0], both[0], both[1]
            ).astype(BF16)

    loop(0, PAIRS, attend)

    def second_norm(i):
        block = aligned(i, ROWBLK)
        total = nn(mixed[block, :], wfull[:, 3 * WIDTH : 4 * WIDTH])
        total = tok[block, :].astype(F32) + total + vecs[4:5, :]
        middle[block, :] = total
        value, _ = normalize(total)
        routed[block, :] = (value * vecs[5:6, :] + vecs[6:7, :]).astype(BF16)

    loop(0, SLOTS // ROWBLK, second_norm)
    dispatch(routed, send_x, x_in, s_x, r_x)

    load_in.wait()
    load_out.wait()
    pack[...] = jnp.zeros_like(pack)

    def clear(t):
        ew[t] = jnp.zeros((FTILE, WIDTH), BF16)

    loop(0, ew.shape[0], clear)
    router = vecs[8 : 8 + experts, :].astype(BF16)
    f_tiles = w_in.shape[1] // FTILE
    bias_at = 8 + experts
    hot = jnp.where(lax.broadcasted_iota(jnp.int32, (1, experts), 1) == at.me, 1.0, 0.0)

    def give_back(buffer, into, send, recv, r):
        return remote(
            buffer.at[aligned(r, cap_rows), :],
            into.at[aligned(at.me, cap_rows), :],
            send.at[r],
            recv.at[r],
            at.fsdp_peer(r),
        )

    acc_o, acc_d = d_middle.at[0:chunk_rows, :], d_middle.at[chunk_rows : 2 * chunk_rows, :]

    def expert_chunk(step):
        pos = position(step, z_side)
        block = aligned(pos, chunk_rows)
        first = pos * sources

        def arrive(r):
            @pl.when(r > 0)
            def _():
                send_rows(send_g, g_in, s_g, r_g, n_f - r).wait_recv()
                send_rows(send_x, x_in, s_x, r_x, n_f - r).wait_recv()

        loop(first, first + sources, arrive)
        x_rows = x_in[block, :]
        logits = nt(x_rows, router)
        gates = jnp.exp(logits - jnp.max(logits, axis=-1, keepdims=True))
        gates = gates / jnp.sum(gates, axis=-1, keepdims=True)
        chosen = jnp.sum(gates * hot, axis=-1, keepdims=True)
        g_rows = (chosen * g_in[block, :].astype(F32)).astype(BF16)
        g_in[block, :] = g_rows
        pack[bias_at + 4 : bias_at + 5, :] += jnp.sum(g_rows.astype(F32), axis=0, keepdims=True)
        acc_o[...] = jnp.broadcast_to(b_out[...].astype(F32), acc_o.shape)
        acc_d[...] = jnp.zeros_like(acc_d)
        def tile(f):
            lanes = aligned(f, FTILE)
            pre = nn(x_in[block, :], w_in[:, lanes]) + b_in[:, lanes].astype(F32)
            d_act = nt(g_in[block, :], w_out[lanes, :])
            cdf = 0.5 + 0.5 * lax.erf(pre * 0.7071067811865476)
            act = (pre * cdf).astype(BF16)
            slope = cdf + pre * jnp.exp(-0.5 * pre * pre) * 0.3989422804014327
            d_row = (d_act * slope).astype(BF16)
            hidden[block, lanes] = act
            d_pre[block, lanes] = d_row
            pack[pl.ds(bias_at + f, 1), :] += jnp.sum(
                d_row.astype(F32), axis=0, keepdims=True
            )
            acc_o[...] += nn(act, w_out[lanes, :])
            acc_d[...] += nt(d_row, w_in[:, lanes])

        loop(0, f_tiles, tile)
        result = acc_o[...]
        weight = jnp.sum(g_in[block, :].astype(F32) * result, axis=-1, keepdims=True)
        d_logits = (weight * (hot - gates)).astype(BF16)
        pack[8:bias_at, :] += tn(d_logits, x_in[block, :])
        ret_d[block, :] = (acc_d[...] + nn(d_logits, router)).astype(BF16)
        ret_o[block, :] = (chosen * result).astype(BF16)

        def back(r):
            @pl.when(r > 0)
            def _():
                give_back(ret_d, table_d, s_d, r_d, r).start()

        loop(first, first + sources, back)

        @pl.when(step < CHUNKS - 1)
        def _():
            loop(0, f_tiles, lambda f: add_tiles(f, block))

    def add_tiles(f, block):
        lanes = aligned(f, FTILE)
        product = tn(x_in[block, :], d_pre[block, lanes])
        ew[2 * f] = (ew[2 * f].astype(F32) + product).astype(BF16)
        product = tn(hidden[block, lanes], g_in[block, :])
        ew[2 * f + 1] = (ew[2 * f + 1].astype(F32) + product).astype(BF16)

    loop(0, CHUNKS, expert_chunk)
    last = pl.ds(2 * chunk_rows, chunk_rows)
    mine = aligned(at.me, cap_rows)
    table_d[mine, :] = ret_d[0:cap_rows, :]

    part = FTILE // n_x
    per_core = f_tiles // 2

    def e_tile(core, j):
        return (core * per_core + j // 2) * 2 + j % 2

    def to_partner(j):
        return remote(ew.at[e_tile(other, j)], ew_core.at[j], s_ec.at[j], r_ec.at[j], at.partner())

    def to_x(i, j):
        src = ew.at[e_tile(at.core, j), aligned(at.x_index(i), part), :]
        return remote(src, ew_x.at[i - 1, j], s_ex.at[i - 1, j], r_ex.at[i - 1, j], at.x_peer(i))

    def e_part(core, j, x):
        return e_tile(core, j), aligned(x, part)

    def all_x(i, j):
        src = ew.at[e_tile(at.core, j), aligned(at.x, part), :]
        dst = ew_core.at[j, aligned(at.x, part), :]
        return remote(src, dst, s_ea.at[i - 1, j], r_ea.at[i - 1, j], at.x_peer(i))

    def from_x(i, j):
        dst = ew_core.at[j, aligned(x_back(i), part), :]
        return remote(dst, dst, s_ea.at[i - 1, j], r_ea.at[i - 1, j], at.x_peer(i))

    def e_result(i, j):
        piece = aligned(x_back(i), part)
        return ew.at[e_tile(at.core, j), piece, :] if i == 0 else ew_core.at[j, piece, :]

    def to_core(i, j, core):
        dst = o_expert.at[e_tile(core, j), aligned(x_back(i), part), :]
        return remote(e_result(i, j), dst, s_eb.at[i, j], r_eb.at[i, j], at.partner())

    def to_self(i, j):
        dst = o_expert.at[e_tile(at.core, j), aligned(x_back(i), part), :]
        return pltpu.make_async_copy(e_result(i, j), dst, s_self.at[i, j])

    n_mine = 2 * per_core

    def theirs(f):
        add_tiles(other * per_core + f, last)
        to_partner(2 * f).start()
        to_partner(2 * f + 1).start()

    def sum_cores(j):
        to_partner(j).wait_recv()
        tile = e_tile(at.core, j)
        ew[tile] = (ew[tile].astype(F32) + ew_core[j].astype(F32)).astype(BF16)
        for i in range(1, n_x):
            to_x(i, j).start()

    def tile_row(f):
        theirs(f)
        add_tiles(at.core * per_core + f, last)
        sum_cores(2 * f)
        sum_cores(2 * f + 1)

    loop(0, per_core, tile_row)

    table_o = send_x

    def left(k):
        send_rows(send_x, x_in, s_x, r_x, k).wait_send()

    loop(1, n_f, left)
    table_o[mine, :] = ret_o[0:cap_rows, :]

    def tell(k):
        pl.semaphore_signal(ready, inc=1, device_id=at.fsdp_peer(k), device_id_type=MESH)

    loop(1, n_f, tell)
    pl.semaphore_wait(ready, n_f - 1)

    def send_lot(lot):
        def one(step):
            r = 1 + lax.rem(n_f // 2 - 1 + step, n_f - 1)
            give_back(ret_o, table_o, s_o, r_o, r).start()

        loop(lax.div((n_f - 1) * lot, LOTS), lax.div((n_f - 1) * (lot + 1), LOTS), one)

    loop(0, 2, send_lot)

    def returned(buffer, into, send, recv, r):
        home = at.ahead(n_f - r)
        return remote(
            buffer.at[aligned(r, cap_rows), :],
            into.at[aligned(home, cap_rows), :],
            send.at[r],
            recv.at[r],
            at.fsdp_peer(r),
        )

    def e_spread(j):
        for i in range(1, n_x):
            to_x(i, j).wait_recv()
        tile = e_tile(at.core, j)
        own = aligned(at.x, part)
        total = ew[tile, own, :].astype(F32)
        for i in range(1, n_x):
            total = total + ew_x[i - 1, j].astype(F32)
        ew[tile, own, :] = total.astype(BF16)
        for i in range(1, n_x):
            all_x(i, j).start()
        to_core(0, j, at.core).start()
        to_self(0, j).start()

    def e_forward(j):
        for i in range(1, n_x):
            from_x(i, j).wait_recv()
            to_core(i, j, at.core).start()
            to_self(i, j).start()

    loop(0, n_mine - 1, e_spread)
    loop(1, n_f, lambda r: returned(ret_d, table_d, s_d, r_d, r).wait_recv())

    loop(1, n_f, lambda k: send_rows(send_g, g_in, s_g, r_g, k).wait_send())
    d_mixed = send_g

    table_iota = lax.broadcasted_iota(jnp.int32, (ROWBLK, n_f * cap_rows), 1).astype(F32)

    def gather_rows(block):
        hit = (table_iota == place[block, 0:1]) | (table_iota == place[block, 1:2])
        return jnp.where(hit, 1.0, 0.0).astype(BF16)

    def norm_back(grad, value, inv_std, gain):
        scaled = grad * gain
        return inv_std * (
            scaled
            - jnp.mean(scaled, axis=-1, keepdims=True)
            - value * jnp.mean(scaled * value, axis=-1, keepdims=True)
        )

    def second_back(i):
        block = aligned(i, ROWBLK)
        grad = nn(gather_rows(block), table_d[...])
        value, inv_std = normalize(middle[block, :])
        pack[5:6, :] += jnp.sum(grad * value, axis=0, keepdims=True)
        pack[6:7, :] += jnp.sum(grad, axis=0, keepdims=True)
        total = cot[block, :].astype(F32) + norm_back(grad, value, inv_std, vecs[5:6, :])
        d_middle[block, :] = total
        low = total.astype(BF16)
        routed[block, :] = low
        pack[4:5, :] += jnp.sum(low.astype(F32), axis=0, keepdims=True)
        d_mixed[block, :] = nt(low, wfull[:, 3 * WIDTH : 4 * WIDTH]).astype(BF16)

    loop(0, SLOTS // ROWBLK, second_back)

    units = 16 // n_d
    pairs_in_unit = PAIRS // units

    y_rows = n_z * shard

    def dense(tile):
        return hidden.at[WIDTH * 2 : WIDTH * 3, aligned(tile, TILE)]

    def put_dense(tile, value):
        value = value.astype(BF16)
        for z in range(n_z):
            for y in range(n_y):
                low = (z * n_y + y) * shard
                row = WIDTH * 2 + (y * n_z + z) * shard
                hidden[row : row + shard, aligned(tile, TILE)] = value[low : low + shard, :]

    def y_block(tile, y):
        rows = pl.ds(pl.multiple_of(WIDTH * 2 + y * y_rows, shard), y_rows)
        return hidden.at[rows, aligned(tile, TILE)]

    def z_piece(tile, z):
        rows = pl.ds(pl.multiple_of(WIDTH * 2 + (my_y * n_z + z) * shard, shard), shard)
        return hidden.at[rows, aligned(tile, TILE)]

    def own_tile(u, x):
        return u * n_d + x * 2 + at.core

    def g_core(u, x):
        src = dense(u * n_d + x * 2 + other)
        return remote(src, dense_core.at[u, x], s_gc.at[u, x], r_gc.at[u, x], at.partner())

    def g_y(u, x, j):
        src = y_block(own_tile(u, x), lax.rem(my_y + j, n_y))
        sems = s_gy.at[u, x, j - 1], r_gy.at[u, x, j - 1]
        return remote(src, dense_y.at[u, x, j - 1], *sems, (at.d, member(0, j)))

    def g_z(u, x, i):
        src = z_piece(own_tile(u, x), lax.rem(my_z + i, n_z))
        sems = s_gz.at[u, x, i], r_gz.at[u, x, i]
        return remote(src, dense_z.at[u, x, i], *sems, (at.d, member(i, 0)))

    def g_x(u, i):
        sems = s_gx.at[u, i - 1], r_gx.at[u, i - 1]
        return remote(dense_s.at[u], dense_x.at[u, i - 1], *sems, at.x_peer(i))

    def g_d(u, core):
        src = final.at[u, core]
        return remote(src, src, s_gd.at[u], r_gd.at[u], at.partner())

    def first_hop(u):
        for x in range(n_x):
            g_core(u, x).start()

    def second_hop(u):
        for x in range(n_x):
            g_core(u, x).wait_recv()
            tile = dense(own_tile(u, x))
            tile[...] = (tile[...].astype(F32) + dense_core[u, x].astype(F32)).astype(BF16)
            for j in range(1, n_y):
                g_y(u, x, j).start()

    def third_hop(u):
        for x in range(n_x):
            mine = y_block(own_tile(u, x), my_y)
            total = mine[...].astype(F32)
            for j in range(1, n_y):
                g_y(u, x, j).wait_recv()
                total = total + dense_y[u, x, j - 1].astype(F32)
            mine[...] = total.astype(BF16)
            for i in range(1, n_z):
                g_z(u, x, i).start()

    def fourth_hop(u):
        for x in range(n_x):
            total = z_piece(own_tile(u, x), my_z)[...].astype(F32)
            for i in range(1, n_z):
                g_z(u, x, i).wait_recv()
                total = total + dense_z[u, x, i].astype(F32)
            dense_s[u, x] = total.astype(BF16)
        for i in range(1, n_x):
            g_x(u, i).start()

    def fifth_hop(u):
        total = dense_s[u].astype(F32)
        for i in range(1, n_x):
            g_x(u, i).wait_recv()
            total = total + dense_x[u, i - 1].astype(F32)
        final[u, at.core] = total.astype(BF16)
        g_d(u, at.core).start()

    hops = (first_hop, second_hop, third_hop, fourth_hop, fifth_hop)

    d_wo = tn(mixed[...], routed[...])
    for pair in range(PAIRS):
        put_dense(4 * pair + 3, d_wo[:, pair * TILE : (pair + 1) * TILE])

    def attend_back(pair):
        for b, (low, high, row) in enumerate(WINDOWS):
            window = slice(row, row + high - low)
            grad = d_mixed[b * QBLK : (b + 1) * QBLK, aligned(pair, TILE)]
            values = qkv[2 * PAIRS + pair, low:high, :]
            for h in range(2):
                one = jnp.where(halves[h], grad, jnp.zeros_like(grad))
                scores[h, window, :] = nt(values, one)
        for b, (low, high, row) in enumerate(WINDOWS):
            window = slice(row, row + high - low)
            for h in range(2):
                share = probs[2 * pair + h, window, :].astype(F32)
                moved = share * scores[h, window, :]
                moved = moved - share * jnp.sum(moved, axis=0, keepdims=True)
                d_pre[window, h * 256 : h * 256 + QBLK] = moved.astype(BF16)
        for array in (acc_k, acc_v):
            array[...] = jnp.zeros_like(array)
        for b, (low, high, row) in enumerate(WINDOWS):
            window = slice(row, row + high - low)
            block = slice(b * QBLK, (b + 1) * QBLK)
            keys = qkv[PAIRS + pair, low:high, :]
            query = qkv[pair, block, :]
            grad = d_mixed[block, aligned(pair, TILE)]
            both = [
                [
                    tn(d_pre[window, h * 256 : h * 256 + QBLK], keys),
                    nn(d_pre[window, h * 256 : h * 256 + QBLK], query),
                    nn(probs[2 * pair + h, window, :], grad),
                ]
                for h in range(2)
            ]
            d_q, d_k, d_v = [jnp.where(halves[0], one, two) for one, two in zip(*both)]
            hidden[block, pl.ds(pl.multiple_of(pair * 384, 128), 128)] = (d_q * 0.125).astype(BF16)
            acc_k[low:high, :] += d_k
            acc_v[low:high, :] += d_v
        hidden[0:SLOTS, pl.ds(pl.multiple_of(pair * 384 + 128, 128), 128)] = acc_k[...].astype(BF16)
        hidden[0:SLOTS, pl.ds(pl.multiple_of(pair * 384 + 256, 128), 128)] = acc_v[...].astype(BF16)
        d_qkv = hidden[0:SLOTS, pl.ds(pl.multiple_of(pair * 384, 128), 384)]
        sums = jnp.sum(d_qkv.astype(F32), axis=0, keepdims=True)
        pack[2:3, aligned(pair, TILE)] = sums[:, 0:128]
        pack[3:4, aligned(pair, TILE)] = sums[:, 256:384]
        d_w = tn(normed[...], d_qkv)
        for c in range(3):
            put_dense(4 * pair + c, d_w[:, c * TILE : (c + 1) * TILE])

        @pl.when(lax.rem(pair, pairs_in_unit) == pairs_in_unit - 1)
        def _():
            unit = lax.div(pair, pairs_in_unit)
            for age, hop in enumerate(hops):

                @pl.when(unit >= age)
                def _(age=age, hop=hop):
                    hop(unit - age)

        send_lot(pair + 2)


    acc_k, acc_v = bias.at[0:SLOTS, 0:TILE], bias.at[0:SLOTS, TILE : 2 * TILE]
    loop(0, PAIRS, attend_back)

    def later(step):
        for age, hop in enumerate(hops):
            if 0 <= step - age < units:
                hop(step - age)

    later(units)
    send_lot(PAIRS + 2)

    def first_back(i):
        block = aligned(i, ROWBLK)
        grad = nt(hidden[block, 0 : 3 * WIDTH], wfull[:, 0 : 3 * WIDTH])
        value, inv_std = normalize(tok[block, :].astype(F32))
        pack[0:1, :] += jnp.sum(grad * value, axis=0, keepdims=True)
        pack[1:2, :] += jnp.sum(grad, axis=0, keepdims=True)
        d_middle[block, :] += norm_back(grad, value, inv_std, vecs[0:1, :])

    loop(0, SLOTS // ROWBLK, first_back)
    save_tokens = pltpu.make_async_copy(d_middle.at[0:SLOTS, :], o_tokens, s_own.at[2 + n_mine])
    save_tokens.start()

    def p_dp(i):
        return remote(pack, pack_dp.at[i], s_p.at[i], r_p.at[i], at.dp_peer(i))

    for i in range(1, n_d):
        p_dp(i).start()
    later(units + 1)
    e_spread(n_mine - 1)
    loop(0, n_mine - 1, e_forward)

    def vec_lane(owner):
        return aligned(lax.div(owner * shard, TILE), TILE)

    def qv_lane(owner):
        return aligned(lax.div(lax.rem(owner * 2 * shard, WIDTH), TILE), TILE)

    def p_vec(k):
        src = pack_dp.at[0, 0:bias_at, vec_lane(at.ahead(k))]
        return remote(src, vec_f.at[k], s_vf.at[k], r_vf.at[k], at.fsdp_peer(k))

    def p_qv(k):
        src = pack_dp.at[0, 0:8, qv_lane(at.ahead(k))]
        return remote(src, qv_f.at[k], s_qf.at[k], r_qf.at[k], at.fsdp_peer(k))

    pack_dp[0] = pack[...]
    for i in range(1, n_d):
        p_dp(i).wait_recv()
        pack_dp[0] += pack_dp[i]
    loop(1, n_f, lambda k: [p_vec(k).start(), p_qv(k).start()])
    save_bias = pltpu.make_async_copy(
        pack_dp.at[0, bias_at : bias_at + 8, :], o_bias, s_own.at[3 + n_mine]
    )
    save_bias.start()
    later(units + 2)
    e_forward(n_mine - 1)

    loop(1, n_f, lambda r: returned(ret_o, table_o, s_o, r_o, r).wait_recv())

    def combine(i):
        block = aligned(i, ROWBLK)
        total = middle[block, :] + nn(gather_rows(block), table_o[...])
        routed[block, :] = total.astype(BF16)

    loop(0, SLOTS // ROWBLK, combine)
    save_out = pltpu.make_async_copy(routed, o_out, s_own.at[4 + n_mine])
    save_out.start()
    later(units + 3)

    loop(1, n_f, lambda k: [p_vec(k).wait_recv(), p_qv(k).wait_recv()])
    vec_f[0] = pack_dp[0, 0:bias_at, vec_lane(at.me)]
    qv_f[0] = pack_dp[0, 0:8, qv_lane(at.me)]

    def add_lanes(k):
        vec_f[0] += vec_f[k]
        qv_f[0] += qv_f[k]

    loop(1, n_f, add_lanes)
    save_vec = pltpu.make_async_copy(vec_f.at[0], o_vec, s_own.at[5 + n_mine])
    save_qv = pltpu.make_async_copy(qv_f.at[0], o_qv, s_own.at[6 + n_mine])
    save_vec.start()
    save_qv.start()
    loop(0, units, lambda u: g_d(u, other).wait_recv())
    save_dense = pltpu.make_async_copy(final, o_dense, s_own.at[7 + n_mine])
    save_dense.start()

    def ended_f(k):
        send_v(k).wait_send()
        got_w(k).wait_send()
        for i in range(1, n_x):
            share_x(i, k).wait_send()
        for i in range(n_x):
            share_core(i, k).wait_send()
        give_back(ret_d, table_d, s_d, r_d, k).wait_send()
        give_back(ret_o, table_o, s_o, r_o, k).wait_send()
        p_vec(k).wait_send()
        p_qv(k).wait_send()

    loop(1, n_f, ended_f)

    def ended_e(j):
        to_partner(j).wait_send()
        for i in range(1, n_x):
            to_x(i, j).wait_send()
            all_x(i, j).wait_send()
        for i in range(n_x):
            to_core(i, j, at.core).wait_send()
            to_core(i, j, other).wait_recv()
            to_self(i, j).wait()

    loop(0, n_mine, ended_e)

    def ended_u(u):
        for x in range(n_x):
            g_core(u, x).wait_send()
            for j in range(1, n_y):
                g_y(u, x, j).wait_send()
            for i in range(1, n_z):
                g_z(u, x, i).wait_send()
        for i in range(1, n_x):
            g_x(u, i).wait_send()
        g_d(u, at.core).wait_send()

    loop(0, units, ended_u)
    for i in range(1, n_d):
        p_dp(i).wait_send()
    for copy in (save_tokens, save_bias, save_out, save_vec, save_qv, save_dense):
        copy.wait()


def block(n_f, n_d, experts, cap, cap_rows, small, w_in, w_out, b_in, b_out):
    vmem = pl.BlockSpec(memory_space=pltpu.VMEM)
    hbm = pl.BlockSpec(memory_space=pl.ANY)
    n_x = n_d // 2
    more_x = max(n_x - 1, 1)
    vec_rows = -(-(8 + experts) // 16) * 16
    shard = WIDTH // n_f
    table = n_f * cap_rows
    hid = w_in.shape[1]
    units = 16 // n_d
    n_mine = hid // FTILE
    n_y = y_members(n_f)
    more_y = max(n_y - 1, 1)
    pack_rows = 8 + experts + 8
    sds = jax.ShapeDtypeStruct
    vm = pltpu.VMEM
    dma = pltpu.SemaphoreType.DMA
    chunk_rows = table // CHUNKS
    pairs_of = lambda *shape: [dma(shape), dma(shape)]
    return pl.pallas_call(
        functools.partial(block_kernel, n_f, n_d, experts, cap, cap_rows),
        out_shape=(
            sds((SLOTS, WIDTH), BF16),
            sds((SLOTS, WIDTH), F32),
            sds((2 * n_mine, FTILE, WIDTH), BF16),
            sds((units, 2, n_x, shard, TILE), BF16),
            sds((8 + experts, TILE), F32),
            sds((8, TILE), F32),
            sds((8, WIDTH), F32),
        ),
        in_specs=[vmem] * len(small) + [hbm] * 2 + [vmem] * 2,
        out_specs=[hbm] * 7,
        scratch_shapes=[
            vm((WIDTH, 4 * WIDTH), BF16),
            vm((vec_rows, WIDTH), BF16),
            vm((vec_rows, WIDTH), F32),
            vm((KEYS, 2 * TILE), F32),
            vm((2, KEYS, QBLK), F32),
            vm((2 * PAIRS, KEYS, QBLK), BF16),
            vm((3 * PAIRS, SLOTS, TILE), BF16),
            vm((SLOTS, WIDTH), BF16),
            vm((SLOTS, WIDTH), BF16),
            vm((SLOTS, WIDTH), F32),
            vm((SLOTS, WIDTH), BF16),
            vm((SLOTS, 8), F32),
        ]
        + [vm((table, WIDTH), BF16)] * 4
        + [
            vm((WIDTH, hid), BF16),
            vm((hid, WIDTH), BF16),
            vm((table, hid), BF16),
            vm((table, hid), BF16),
        ]
        + [vm((table, WIDTH), BF16)] * 3
        + [
            vm((2 * n_mine, FTILE, WIDTH), BF16),
            vm((n_mine, FTILE, WIDTH), BF16),
            vm((more_x, n_mine, FTILE // n_x, WIDTH), BF16),
            vm((units, n_x, WIDTH, TILE), BF16),
            vm((units, n_x, more_y, n_f // n_y * shard, TILE), BF16),
            vm((units, n_x, n_f // n_y, shard, TILE), BF16),
            vm((units, n_x, shard, TILE), BF16),
            vm((units, more_x, n_x, shard, TILE), BF16),
            vm((units, 2, n_x, shard, TILE), BF16),
            vm((pack_rows, WIDTH), F32),
            vm((n_d, pack_rows, WIDTH), F32),
            vm((n_f, 8 + experts, TILE), F32),
            vm((n_f, 8, TILE), F32),
            vm((max(2 * chunk_rows, SLOTS), WIDTH), F32),
        ]
        + pairs_of(n_f)
        + pairs_of(n_f)
        + pairs_of(more_x, n_f)
        + pairs_of(n_x, n_f)
        + pairs_of(n_f)
        + pairs_of(n_f)
        + pairs_of(n_f)
        + pairs_of(n_f)
        + pairs_of(n_mine)
        + pairs_of(more_x, n_mine)
        + pairs_of(more_x, n_mine)
        + pairs_of(n_x, n_mine)
        + pairs_of(units, n_x)
        + pairs_of(units, n_x, more_y)
        + pairs_of(units, n_x, n_f // n_y)
        + pairs_of(units, more_x)
        + pairs_of(units)
        + pairs_of(n_d)
        + pairs_of(n_f)
        + pairs_of(n_f)
        + [dma((8 + n_mine,)), dma((n_x, n_mine)), pltpu.SemaphoreType.REGULAR],
        compiler_params=pltpu.CompilerParams(
            collective_id=0, has_side_effects=True, vmem_limit_bytes=63 << 20
        ),
        name="block",
    )(*small, w_in, w_out, b_in, b_out)


def finish_kernel(
    n_f,
    experts,
    in_out,
    in_tokens,
    in_expert,
    dense,
    vec,
    qv,
    biases,
    o_out,
    o_tokens,
    o_g1,
    o_s1,
    o_qkv,
    o_bqv,
    o_wo,
    o_bo,
    o_g2,
    o_s2,
    o_router,
    o_w_in,
    o_b_in,
    o_w_out,
    o_b_out,
    low,
    wide,
    rows_low,
    rows_wide,
    s_load,
    s_save,
):
    me = lax.axis_index("fsdp")
    shard = WIDTH // n_f
    tiles = in_expert.shape[0]
    loads = [pltpu.make_async_copy(in_expert.at[t], low.at[t], s_load.at[t]) for t in range(tiles)]
    for load in loads:
        load.start()
    rows_in = [
        pltpu.make_async_copy(in_out, rows_low, s_load.at[tiles]),
        pltpu.make_async_copy(in_tokens, rows_wide, s_load.at[tiles + 1]),
    ]
    for load in rows_in:
        load.start()

    def my_lanes(value, size):
        place = lax.rem(me * size, TILE)
        total = jnp.zeros((value.shape[0], size), F32)
        for low_lane in range(0, TILE, size):
            total = total + jnp.where(place == low_lane, value[:, low_lane : low_lane + size], 0.0)
        return total

    own = my_lanes(vec[...], shard)
    for row, ref in ((0, o_g1), (1, o_s1), (4, o_bo), (5, o_g2), (6, o_s2)):
        ref[...] = own[row : row + 1, :]
    o_router[...] = own[8 : 8 + experts, :]
    lines = my_lanes(qv[...], 2 * shard)
    o_bqv[...] = jnp.where(me * 2 * shard < WIDTH, lines[2:3, :], lines[3:4, :])
    n_d = 2 * dense.shape[2]

    def tile(t):
        return dense[t // n_d, t % 2, t % n_d // 2].astype(F32)

    for pair in range(PAIRS):
        for c in range(3):
            at = c * WIDTH + pair * TILE
            o_qkv[:, at : at + TILE] = tile(4 * pair + c)
        o_wo[:, pair * TILE : (pair + 1) * TILE] = tile(4 * pair + 3)
    for f in range(tiles // 2):
        o_b_in[:, f * FTILE : (f + 1) * FTILE] = biases[f : f + 1, :]
    o_b_out[...] = biases[4:5, :]
    saves = []
    for t in range(tiles):
        loads[t].wait()
        wide[t] = low[t].astype(F32)
        piece = pl.ds(t // 2 * FTILE, FTILE)
        dst = o_w_out.at[0, piece, :] if t % 2 else o_w_in.at[0, :, piece]
        saves.append(pltpu.make_async_copy(wide.at[t], dst, s_save.at[t]))
        saves[-1].start()
    rows_out = [
        pltpu.make_async_copy(rows_low, o_out, s_save.at[tiles]),
        pltpu.make_async_copy(rows_wide, o_tokens, s_save.at[tiles + 1]),
    ]
    for load, save in zip(rows_in, rows_out):
        load.wait()
        save.start()
    for save in saves + rows_out:
        save.wait()


def finish(n_f, experts, hid, parts):
    vmem = pl.BlockSpec(memory_space=pltpu.VMEM)
    hbm = pl.BlockSpec(memory_space=pl.ANY)
    shard = WIDTH // n_f
    tiles = parts[2].shape[0]
    line = lambda *shape: jax.ShapeDtypeStruct(shape, F32)
    return pl.pallas_call(
        functools.partial(finish_kernel, n_f, experts),
        out_shape=(
            jax.ShapeDtypeStruct((SLOTS, WIDTH), BF16),
            line(SLOTS, WIDTH),
            line(1, shard),
            line(1, shard),
            line(shard, 3 * WIDTH),
            line(1, 2 * shard),
            line(shard, WIDTH),
            line(1, shard),
            line(1, shard),
            line(1, shard),
            line(experts, shard),
            line(1, WIDTH, hid),
            line(1, hid),
            line(1, hid, WIDTH),
            line(1, WIDTH),
        ),
        in_specs=[hbm] * 3 + [vmem] * 4,
        out_specs=[hbm] * 2 + [vmem] * 9 + [hbm, vmem, hbm, vmem],
        scratch_shapes=[
            pltpu.VMEM((tiles, FTILE, WIDTH), BF16),
            pltpu.VMEM((tiles, FTILE, WIDTH), F32),
            pltpu.VMEM((SLOTS, WIDTH), BF16),
            pltpu.VMEM((SLOTS, WIDTH), F32),
            pltpu.SemaphoreType.DMA((tiles + 2,)),
            pltpu.SemaphoreType.DMA((tiles + 2,)),
        ],
        compiler_params=pltpu.CompilerParams(vmem_limit_bytes=62 << 20),
        name="finish",
    )(*parts)


def shards(
    tokens,
    cotangent,
    segment_ids,
    pad_mask,
    expert_ids,
    priority,
    ln1_gain,
    ln1_shift,
    w_qkv,
    b_qv,
    w_o,
    b_o,
    ln2_gain,
    ln2_shift,
    w_router,
    w_in,
    b_in,
    w_out,
    b_out,
    n_f,
    n_d,
):
    experts = w_router.shape[1]
    cap = (21 * tokens.shape[0] + 10 * experts - 1) // (10 * experts)
    cap_rows = -(-cap // 16) * 16
    line = lambda vector: vector.reshape(1, -1)
    small = (
        tokens,
        cotangent,
        segment_ids,
        pad_mask,
        expert_ids.T,
        priority,
        w_qkv,
        w_o,
        line(ln1_gain),
        line(ln1_shift),
        line(b_qv),
        line(b_o),
        line(ln2_gain),
        line(ln2_shift),
        w_router.T,
    )
    parts = block(n_f, n_d, experts, cap, cap_rows, small, w_in[0], w_out[0], b_in, b_out)
    done = finish(n_f, experts, w_in.shape[2], parts)
    flat = (2, 3, 5, 7, 8, 9)
    done = [value.reshape(-1) if i in flat else value for i, value in enumerate(done)]
    done[10] = done[10].T
    return tuple(done)


def solution(mesh):
    both, one = P(("dp", "fsdp")), P("fsdp")
    n_f, n_d = mesh.shape["fsdp"], mesh.shape["dp"]
    return jax.shard_map(
        functools.partial(shards, n_f=n_f, n_d=n_d),
        mesh=mesh,
        in_specs=(both,) * 6 + (one,) * 13,
        out_specs=(both,) * 2 + (one,) * 13,
        check_vma=False,
    )
```

```python
import functools

import jax
import jax.numpy as jnp
from jax import lax
from jax.experimental import pallas as pl
from jax.experimental.pallas import tpu as pltpu
from jax.sharding import PartitionSpec as P

MESH = pl.DeviceIdType.MESH
BF16 = jnp.bfloat16
F32 = jnp.float32
SLOTS = 720
WIDTH = 512
PAIRS = 4
EPS = 1e-06
WINDOWS = ((0, 384, 0), (96, 624, 384), (336, 720, 912))
KEYS = 1296
QBLK = 240
ROWBLK = 240
TILE = 128
FTILE = 512
CHUNKS = 4
LOTS = 7


def nt(left, right):
    return lax.dot_general(left, right, (((1,), (1,)), ((), ())), preferred_element_type=F32)


def tn(left, right):
    return lax.dot_general(left, right, (((0,), (0,)), ((), ())), preferred_element_type=F32)


def nn(left, right):
    return jnp.dot(left, right, preferred_element_type=F32)


def normalize(value):
    centred = value - jnp.mean(value, axis=-1, keepdims=True)
    inv_std = lax.rsqrt(jnp.mean(centred * centred, axis=-1, keepdims=True) + EPS)
    return centred * inv_std, inv_std


def aligned(index, size):
    return pl.ds(pl.multiple_of(index * size, size), size)


class Place:
    def __init__(self, n_f, n_d):
        self.n_f, self.n_d, self.n_x = n_f, n_d, n_d // 2
        self.me = lax.axis_index("fsdp")
        self.d = lax.axis_index("dp")
        self.x = lax.div(self.d, 2)
        self.core = lax.rem(self.d, 2)

    def ahead(self, k):
        return lax.rem(self.me + k, self.n_f)

    def fsdp_peer(self, k):
        return (self.d, self.ahead(k))

    def x_index(self, i):
        return lax.rem(self.x + i, self.n_x)

    def x_peer(self, i):
        return (self.x_index(i) * 2 + self.core, self.me)

    def partner(self):
        return (self.x * 2 + 1 - self.core, self.me)

    def dp_peer(self, i):
        return (lax.rem(self.d + i, self.n_d), self.me)

    def enter(self):
        bar = pltpu.get_barrier_semaphore()

        def greet(k, _):
            pl.semaphore_signal(bar, inc=1, device_id=self.fsdp_peer(k), device_id_type=MESH)
            return 0

        lax.fori_loop(1, self.n_f, greet, 0)
        for i in range(1, self.n_d):
            pl.semaphore_signal(bar, inc=1, device_id=self.dp_peer(i), device_id_type=MESH)
        pl.semaphore_wait(bar, self.n_f - 1 + self.n_d - 1)


def remote(src, dst, send_sem, recv_sem, device):
    return pltpu.make_async_remote_copy(
        src_ref=src,
        dst_ref=dst,
        send_sem=send_sem,
        recv_sem=recv_sem,
        device_id=device,
        device_id_type=MESH,
    )


def loop(low, high, body):
    def step(k, carry):
        body(k)
        return carry

    lax.fori_loop(low, high, step, 0)


def y_members(n_f):
    return 1 << ((n_f.bit_length() - 1) // 2)


def block_kernel(
    n_f,
    n_d,
    experts,
    cap,
    cap_rows,
    tok_hbm,
    cot_hbm,
    segment,
    pad,
    chosen_ids,
    priority,
    w_qkv,
    w_o,
    gain_one,
    shift_one,
    b_qv,
    b_o,
    gain_two,
    shift_two,
    w_router,
    w_in_hbm,
    w_out_hbm,
    b_in,
    b_out,
    o_out,
    o_tokens,
    o_expert,
    o_dense,
    o_vec,
    o_qv,
    o_bias,
    tok,
    cot,
    wfull,
    vsh,
    vecs,
    bias,
    scores,
    probs,
    qkv,
    normed,
    mixed,
    middle,
    routed,
    place,
    send_x,
    send_g,
    x_in,
    g_in,
    w_in,
    w_out,
    hidden,
    d_pre,
    ret_d,
    ret_o,
    table_d,
    ew,
    ew_core,
    ew_x,
    dense_core,
    dense_y,
    dense_z,
    dense_s,
    dense_x,
    final,
    pack,
    pack_dp,
    vec_f,
    qv_f,
    d_middle,
    s_w,
    r_w,
    s_v,
    r_v,
    s_dx,
    r_dx,
    s_dc,
    r_dc,
    s_g,
    r_g,
    s_x,
    r_x,
    s_d,
    r_d,
    s_o,
    r_o,
    s_ec,
    r_ec,
    s_ex,
    r_ex,
    s_ea,
    r_ea,
    s_eb,
    r_eb,
    s_gc,
    r_gc,
    s_gy,
    r_gy,
    s_gz,
    r_gz,
    s_gx,
    r_gx,
    s_gd,
    r_gd,
    s_p,
    r_p,
    s_vf,
    r_vf,
    s_qf,
    r_qf,
    s_own,
    s_self,
    ready,
):
    at = Place(n_f, n_d)
    n_x = at.n_x
    shard = WIDTH // n_f
    colw = 4 * WIDTH // n_d
    other = 1 - at.core

    def cols_of(d):
        return aligned(d, colw)

    def w_piece(owner, d):
        return wfull.at[aligned(owner, shard), cols_of(d)]

    def x_back(i):
        return at.x_index(n_x - i)

    load_in = pltpu.make_async_copy(w_in_hbm, w_in, s_own.at[0])
    load_out = pltpu.make_async_copy(w_out_hbm, w_out, s_own.at[1])
    load_tok = pltpu.make_async_copy(tok_hbm, tok, s_own.at[2])
    load_cot = pltpu.make_async_copy(cot_hbm, cot, s_own.at[3])
    for load in (load_cot, load_tok, load_in, load_out):
        load.start()
    at.enter()

    n_y = y_members(n_f)
    n_z = n_f // n_y
    my_z, my_y = lax.div(at.me, n_y), lax.rem(at.me, n_y)

    def member(z, y):
        return lax.rem(my_z + z, n_z) * n_y + lax.rem(my_y + y, n_y)

    def owner(k):
        return member(n_z - lax.rem(k, n_z), n_y - lax.div(k, n_z))

    def along_z(k):
        piece = w_piece(at.me, at.d)
        return remote(piece, piece, s_w.at[k], r_w.at[k], (at.d, member(k, 0)))

    def along_y(j, i):
        piece, k = w_piece(member(n_z - i, 0), at.d), j * n_z + i
        return remote(piece, piece, s_w.at[k], r_w.at[k], (at.d, member(0, j)))

    def got_w(k):
        piece = w_piece(owner(k), at.d)
        return remote(piece, piece, s_w.at[k], r_w.at[k], (at.d, at.me))

    vec_rows = vsh.shape[0]

    def vec_piece(owner):
        return hidden.at[aligned(owner, vec_rows), 0:WIDTH]

    def send_v(k):
        return remote(vsh, vec_piece(at.me), s_v.at[k], r_v.at[k], at.fsdp_peer(k))

    def share_x(i, k):
        piece = w_piece(owner(k), at.d)
        return remote(piece, piece, s_dx.at[i - 1, k], r_dx.at[i - 1, k], at.x_peer(i))

    def share_core(i, k):
        piece = w_piece(owner(k), x_back(i) * 2 + at.core)
        return remote(piece, piece, s_dc.at[i, k], r_dc.at[i, k], at.partner())

    own = aligned(at.me, shard)
    for pair in range(PAIRS):
        for c in range(3):
            low = (3 * pair + c) * TILE
            src = c * WIDTH + pair * TILE
            wfull[own, low : low + TILE] = w_qkv[:, src : src + TILE]
    wfull[own, 3 * WIDTH : 4 * WIDTH] = w_o[...]
    loop(1, n_z, lambda k: along_z(k).start())
    loop(1, n_y, lambda j: along_y(j, 0).start())

    def placing(size, low):
        shape = (size, WIDTH)
        target = lax.broadcasted_iota(jnp.int32, shape, 1) + low
        source = lax.broadcasted_iota(jnp.int32, shape, 0) + at.me * size
        return jnp.where(target == source, 1.0, 0.0).astype(BF16)

    blank = jnp.zeros((1, shard), F32)
    stack = [
        blank if ref is None else ref[...].astype(F32)
        for ref in (gain_one, shift_one, None, None, b_o, gain_two, shift_two, None)
    ]
    spread = nn(jnp.concatenate(stack, axis=0).astype(BF16), placing(shard, 0))
    row_iota = lax.broadcasted_iota(jnp.int32, (8, WIDTH), 0)
    for r in range(2):
        line = nn(b_qv[...], placing(2 * shard, r * WIDTH))
        spread = spread + jnp.where(row_iota == 2 + r, line, 0.0)
    router_rows = nn(w_router[...], placing(shard, 0))
    rest = jnp.zeros((vec_rows - 8 - experts, WIDTH), F32)
    parts = [spread, router_rows] + ([rest] if vec_rows > 8 + experts else [])
    vsh[...] = jnp.concatenate(parts, axis=0).astype(BF16)
    vec_piece(at.me)[...] = vsh[...]
    loop(1, n_f, lambda k: send_v(k).start())

    seg_r, pad_r, pri_r = (
        ref[...].reshape(1, SLOTS).astype(F32) for ref in (segment, pad, priority)
    )
    lines = jnp.concatenate([seg_r, pad_r, pri_r, jnp.zeros((5, SLOTS), F32)], axis=0)
    columns = jnp.transpose(lines)
    seg_c, pad_c, pri_c = (columns[:, j : j + 1] for j in range(3))
    expert_iota = lax.broadcasted_iota(jnp.int32, (experts, SLOTS), 0)
    live = pad_r > 0
    before = jnp.where(pri_c < pri_r, 1.0, 0.0).astype(BF16)
    chose = [jnp.where((chosen_ids[k : k + 1, :] == expert_iota) & live, 1.0, 0.0) for k in range(2)]
    rank = [nn(one.astype(BF16), before) for one in chose]
    rank[1] = rank[1] + jnp.sum(chose[0], axis=1, keepdims=True)
    spot_r = []
    for k in range(2):
        slot = jnp.sum(chose[k] * rank[k], axis=0, keepdims=True)
        spot = chosen_ids[k : k + 1, :].astype(F32) * cap_rows + slot
        spot_r.append(jnp.where(live & (slot < cap), spot, -1.0))
    place[...] = jnp.transpose(jnp.concatenate(spot_r + [jnp.zeros((6, SLOTS), F32)], axis=0))
    slot_iota = lax.broadcasted_iota(jnp.int32, (cap_rows, SLOTS), 0)

    def pick(expert):
        mine = (slot_iota + expert * cap_rows).astype(F32)
        return jnp.where((mine == spot_r[0]) | (mine == spot_r[1]), 1.0, 0.0).astype(BF16)

    for b, (low, high, row) in enumerate(WINDOWS):
        queries = slice(b * QBLK, (b + 1) * QBLK)
        shape = (high - low, QBLK)
        same = seg_c[low:high, :] == seg_r[:, queries]
        itself = (lax.broadcasted_iota(jnp.int32, shape, 0) + low) == (
            lax.broadcasted_iota(jnp.int32, shape, 1) + b * QBLK
        )
        allowed = same & ((pad_c[low:high, :] > 0) | itself)
        bias[row : row + high - low, 0:QBLK] = jnp.where(allowed, 0.0, -1e30)

    chunk_rows = n_f * cap_rows // CHUNKS
    sources = n_f // CHUNKS

    def position(step, side):
        inner = lax.rem(lax.div(step + 1, 2), 2)
        near = 1 + 2 * lax.rem(step + 1 + side, 2)
        return inner * near + (1 - inner) * 2 * lax.div(step, 3)

    z_side = lax.rem(my_z, 2)

    def send_rows(buffer, into, send, recv, k):
        return remote(
            buffer.at[aligned(at.ahead(k), cap_rows), :],
            into.at[aligned(n_f - k, cap_rows), :],
            send.at[k],
            recv.at[n_f - k],
            at.fsdp_peer(k),
        )

    def dispatch(source, buffer, into, send, recv):
        into[0:cap_rows, :] = nn(pick(at.me), source[...]).astype(BF16)

        def stage(step):
            first = position(step, 1 - z_side) * sources

            def one(r):
                @pl.when(r > 0)
                def _():
                    k = n_f - r
                    expert = at.ahead(k)
                    rows = nn(pick(expert), source[...]).astype(BF16)
                    buffer[aligned(expert, cap_rows), :] = rows
                    send_rows(buffer, into, send, recv, k).start()

            loop(first, first + sources, one)

        loop(0, CHUNKS, stage)

    def pass_on(k):
        for i in range(1, n_x):
            share_x(i, k).start()
        share_core(0, k).start()

    def from_z(k):
        got_w(k).wait_recv()
        loop(1, n_y, lambda j: along_y(j, k).start())
        pass_on(k)

    def from_y(k):
        got_w(k).wait_recv()
        pass_on(k)

    loop(1, n_z, from_z)
    load_cot.wait()
    dispatch(cot, send_g, g_in, s_g, r_g)
    loop(n_z, n_f, from_y)

    loop(1, n_f, lambda k: send_v(k).wait_recv())
    vecs[...] = vec_piece(0)[...].astype(F32)

    def add_vectors(owner):
        vecs[...] += vec_piece(owner)[...].astype(F32)

    loop(1, n_f, add_vectors)

    load_tok.wait()

    def first_norm(i):
        block = aligned(i, ROWBLK)
        value, _ = normalize(tok[block, :].astype(F32))
        normed[block, :] = (value * vecs[0:1, :] + vecs[1:2, :]).astype(BF16)

    loop(0, SLOTS // ROWBLK, first_norm)

    for i in range(1, n_x):

        def cross(k, i=i):
            piece = w_piece(owner(k), x_back(i) * 2 + at.core)
            remote(piece, piece, s_dx.at[i - 1, k], r_dx.at[i - 1, k], at.x_peer(i)).wait_recv()
            share_core(i, k).start()

        loop(1, n_f, cross)
    for i in range(n_x):

        def arrive(k, i=i):
            piece = w_piece(owner(k), x_back(i) * 2 + other)
            remote(piece, piece, s_dc.at[i, k], r_dc.at[i, k], at.partner()).wait_recv()

        loop(1, n_f, arrive)

    def project(pair):
        out = nn(normed[...], wfull[:, pl.ds(pl.multiple_of(pair * 384, 128), 384)])
        lanes = aligned(pair, TILE)
        qkv[pair] = ((out[:, 0:128] + vecs[2:3, lanes]) * 0.125).astype(BF16)
        qkv[PAIRS + pair] = out[:, 128:256].astype(BF16)
        qkv[2 * PAIRS + pair] = (out[:, 256:384] + vecs[3:4, lanes]).astype(BF16)

    loop(0, PAIRS, project)

    lane = lax.broadcasted_iota(jnp.int32, (1, TILE), 1)
    halves = (lane < 64, lane >= 64)

    def attend(pair):
        for b, (low, high, row) in enumerate(WINDOWS):
            window = slice(row, row + high - low)
            query = qkv[pair, b * QBLK : (b + 1) * QBLK, :]
            keys = qkv[PAIRS + pair, low:high, :]
            for h in range(2):
                one = jnp.where(halves[h], query, jnp.zeros_like(query))
                scores[h, window, :] = nt(keys, one) + bias[window, 0:QBLK]
        for b, (low, high, row) in enumerate(WINDOWS):
            window = slice(row, row + high - low)
            for h in range(2):
                value = scores[h, window, :]
                power = jnp.exp(value - jnp.max(value, axis=0, keepdims=True))
                share = 1.0 / jnp.sum(power, axis=0, keepdims=True)
                probs[2 * pair + h, window, :] = (power * share).astype(BF16)
        for b, (low, high, row) in enumerate(WINDOWS):
            window = slice(row, row + high - low)
            values = qkv[2 * PAIRS + pair, low:high, :]
            both = [tn(probs[2 * pair + h, window, :], values) for h in range(2)]
            mixed[b * QBLK : (b + 1) * QBLK, aligned(pair, TILE)] = jnp.where(
                halves[0], both[0], both[1]
            ).astype(BF16)

    loop(0, PAIRS, attend)

    def second_norm(i):
        block = aligned(i, ROWBLK)
        total = nn(mixed[block, :], wfull[:, 3 * WIDTH : 4 * WIDTH])
        total = tok[block, :].astype(F32) + total + vecs[4:5, :]
        middle[block, :] = total
        value, _ = normalize(total)
        routed[block, :] = (value * vecs[5:6, :] + vecs[6:7, :]).astype(BF16)

    loop(0, SLOTS // ROWBLK, second_norm)
    dispatch(routed, send_x, x_in, s_x, r_x)

    load_in.wait()
    load_out.wait()
    pack[...] = jnp.zeros_like(pack)

    def clear(t):
        ew[t] = jnp.zeros((FTILE, WIDTH), BF16)

    loop(0, ew.shape[0], clear)
    router = vecs[8 : 8 + experts, :].astype(BF16)
    f_tiles = w_in.shape[1] // FTILE
    bias_at = 8 + experts
    hot = jnp.where(lax.broadcasted_iota(jnp.int32, (1, experts), 1) == at.me, 1.0, 0.0)

    def give_back(buffer, into, send, recv, r):
        return remote(
            buffer.at[aligned(r, cap_rows), :],
            into.at[aligned(at.me, cap_rows), :],
            send.at[r],
            recv.at[r],
            at.fsdp_peer(r),
        )

    acc_o, acc_d = d_middle.at[0:chunk_rows, :], d_middle.at[chunk_rows : 2 * chunk_rows, :]

    def expert_chunk(step):
        pos = position(step, z_side)
        block = aligned(pos, chunk_rows)
        first = pos * sources

        def arrive(r):
            @pl.when(r > 0)
            def _():
                send_rows(send_g, g_in, s_g, r_g, n_f - r).wait_recv()
                send_rows(send_x, x_in, s_x, r_x, n_f - r).wait_recv()

        loop(first, first + sources, arrive)
        x_rows = x_in[block, :]
        logits = nt(x_rows, router)
        gates = jnp.exp(logits - jnp.max(logits, axis=-1, keepdims=True))
        gates = gates / jnp.sum(gates, axis=-1, keepdims=True)
        chosen = jnp.sum(gates * hot, axis=-1, keepdims=True)
        g_rows = (chosen * g_in[block, :].astype(F32)).astype(BF16)
        g_in[block, :] = g_rows
        pack[bias_at + 4 : bias_at + 5, :] += jnp.sum(g_rows.astype(F32), axis=0, keepdims=True)
        acc_o[...] = jnp.broadcast_to(b_out[...].astype(F32), acc_o.shape)
        acc_d[...] = jnp.zeros_like(acc_d)
        def tile(f):
            lanes = aligned(f, FTILE)
            pre = nn(x_in[block, :], w_in[:, lanes]) + b_in[:, lanes].astype(F32)
            d_act = nt(g_in[block, :], w_out[lanes, :])
            cdf = 0.5 + 0.5 * lax.erf(pre * 0.7071067811865476)
            act = (pre * cdf).astype(BF16)
            slope = cdf + pre * jnp.exp(-0.5 * pre * pre) * 0.3989422804014327
            d_row = (d_act * slope).astype(BF16)
            hidden[block, lanes] = act
            d_pre[block, lanes] = d_row
            pack[pl.ds(bias_at + f, 1), :] += jnp.sum(
                d_row.astype(F32), axis=0, keepdims=True
            )
            acc_o[...] += nn(act, w_out[lanes, :])
            acc_d[...] += nt(d_row, w_in[:, lanes])

        loop(0, f_tiles, tile)
        result = acc_o[...]
        weight = jnp.sum(g_in[block, :].astype(F32) * result, axis=-1, keepdims=True)
        d_logits = (weight * (hot - gates)).astype(BF16)
        pack[8:bias_at, :] += tn(d_logits, x_in[block, :])
        ret_d[block, :] = (acc_d[...] + nn(d_logits, router)).astype(BF16)
        ret_o[block, :] = (chosen * result).astype(BF16)

        def back(r):
            @pl.when(r > 0)
            def _():
                give_back(ret_d, table_d, s_d, r_d, r).start()

        loop(first, first + sources, back)

        @pl.when(step < CHUNKS - 1)
        def _():
            loop(0, f_tiles, lambda f: add_tiles(f, block))

    def add_tiles(f, block):
        lanes = aligned(f, FTILE)
        product = tn(x_in[block, :], d_pre[block, lanes])
        ew[2 * f] = (ew[2 * f].astype(F32) + product).astype(BF16)
        product = tn(hidden[block, lanes], g_in[block, :])
        ew[2 * f + 1] = (ew[2 * f + 1].astype(F32) + product).astype(BF16)

    loop(0, CHUNKS, expert_chunk)
    last = pl.ds(2 * chunk_rows, chunk_rows)
    mine = aligned(at.me, cap_rows)
    table_d[mine, :] = ret_d[0:cap_rows, :]

    part = FTILE // n_x
    per_core = f_tiles // 2

    def e_tile(core, j):
        return (core * per_core + j // 2) * 2 + j % 2

    def to_partner(j):
        return remote(ew.at[e_tile(other, j)], ew_core.at[j], s_ec.at[j], r_ec.at[j], at.partner())

    def to_x(i, j):
        src = ew.at[e_tile(at.core, j), aligned(at.x_index(i), part), :]
        return remote(src, ew_x.at[i - 1, j], s_ex.at[i - 1, j], r_ex.at[i - 1, j], at.x_peer(i))

    def e_part(core, j, x):
        return e_tile(core, j), aligned(x, part)

    def all_x(i, j):
        src = ew.at[e_tile(at.core, j), aligned(at.x, part), :]
        dst = ew_core.at[j, aligned(at.x, part), :]
        return remote(src, dst, s_ea.at[i - 1, j], r_ea.at[i - 1, j], at.x_peer(i))

    def from_x(i, j):
        dst = ew_core.at[j, aligned(x_back(i), part), :]
        return remote(dst, dst, s_ea.at[i - 1, j], r_ea.at[i - 1, j], at.x_peer(i))

    def e_result(i, j):
        piece = aligned(x_back(i), part)
        return ew.at[e_tile(at.core, j), piece, :] if i == 0 else ew_core.at[j, piece, :]

    def to_core(i, j, core):
        dst = o_expert.at[e_tile(core, j), aligned(x_back(i), part), :]
        return remote(e_result(i, j), dst, s_eb.at[i, j], r_eb.at[i, j], at.partner())

    def to_self(i, j):
        dst = o_expert.at[e_tile(at.core, j), aligned(x_back(i), part), :]
        return pltpu.make_async_copy(e_result(i, j), dst, s_self.at[i, j])

    n_mine = 2 * per_core

    def theirs(f):
        add_tiles(other * per_core + f, last)
        to_partner(2 * f).start()
        to_partner(2 * f + 1).start()

    def sum_cores(j):
        to_partner(j).wait_recv()
        tile = e_tile(at.core, j)
        ew[tile] = (ew[tile].astype(F32) + ew_core[j].astype(F32)).astype(BF16)
        for i in range(1, n_x):
            to_x(i, j).start()

    def tile_row(f):
        theirs(f)
        add_tiles(at.core * per_core + f, last)
        sum_cores(2 * f)
        sum_cores(2 * f + 1)

    loop(0, per_core, tile_row)

    table_o = send_x

    def left(k):
        send_rows(send_x, x_in, s_x, r_x, k).wait_send()

    loop(1, n_f, left)
    table_o[mine, :] = ret_o[0:cap_rows, :]

    def tell(k):
        pl.semaphore_signal(ready, inc=1, device_id=at.fsdp_peer(k), device_id_type=MESH)

    loop(1, n_f, tell)
    pl.semaphore_wait(ready, n_f - 1)

    def send_lot(lot):
        def one(step):
            r = 1 + lax.rem(1 + step, n_f - 1)
            give_back(ret_o, table_o, s_o, r_o, r).start()

        loop(lax.div((n_f - 1) * lot, LOTS), lax.div((n_f - 1) * (lot + 1), LOTS), one)

    loop(0, 3, send_lot)

    def returned(buffer, into, send, recv, r):
        home = at.ahead(n_f - r)
        return remote(
            buffer.at[aligned(r, cap_rows), :],
            into.at[aligned(home, cap_rows), :],
            send.at[r],
            recv.at[r],
            at.fsdp_peer(r),
        )

    def e_spread(j):
        for i in range(1, n_x):
            to_x(i, j).wait_recv()
        tile = e_tile(at.core, j)
        own = aligned(at.x, part)
        total = ew[tile, own, :].astype(F32)
        for i in range(1, n_x):
            total = total + ew_x[i - 1, j].astype(F32)
        ew[tile, own, :] = total.astype(BF16)
        for i in range(1, n_x):
            all_x(i, j).start()
        to_core(0, j, at.core).start()
        to_self(0, j).start()

    def e_forward(j):
        for i in range(1, n_x):
            from_x(i, j).wait_recv()
            to_core(i, j, at.core).start()
            to_self(i, j).start()

    loop(0, n_mine - 1, e_spread)
    loop(1, n_f, lambda r: returned(ret_d, table_d, s_d, r_d, r).wait_recv())

    loop(1, n_f, lambda k: send_rows(send_g, g_in, s_g, r_g, k).wait_send())
    d_mixed = send_g

    table_iota = lax.broadcasted_iota(jnp.int32, (ROWBLK, n_f * cap_rows), 1).astype(F32)

    def gather_rows(block):
        hit = (table_iota == place[block, 0:1]) | (table_iota == place[block, 1:2])
        return jnp.where(hit, 1.0, 0.0).astype(BF16)

    def norm_back(grad, value, inv_std, gain):
        scaled = grad * gain
        return inv_std * (
            scaled
            - jnp.mean(scaled, axis=-1, keepdims=True)
            - value * jnp.mean(scaled * value, axis=-1, keepdims=True)
        )

    def second_back(i):
        block = aligned(i, ROWBLK)
        grad = nn(gather_rows(block), table_d[...])
        value, inv_std = normalize(middle[block, :])
        pack[5:6, :] += jnp.sum(grad * value, axis=0, keepdims=True)
        pack[6:7, :] += jnp.sum(grad, axis=0, keepdims=True)
        total = cot[block, :].astype(F32) + norm_back(grad, value, inv_std, vecs[5:6, :])
        d_middle[block, :] = total
        low = total.astype(BF16)
        routed[block, :] = low
        pack[4:5, :] += jnp.sum(low.astype(F32), axis=0, keepdims=True)
        d_mixed[block, :] = nt(low, wfull[:, 3 * WIDTH : 4 * WIDTH]).astype(BF16)

    loop(0, SLOTS // ROWBLK, second_back)

    units = 16 // n_d
    pairs_in_unit = PAIRS // units

    y_rows = n_z * shard

    def dense(tile):
        return hidden.at[WIDTH * 2 : WIDTH * 3, aligned(tile, TILE)]

    def put_dense(tile, value):
        value = value.astype(BF16)
        for z in range(n_z):
            for y in range(n_y):
                low = (z * n_y + y) * shard
                row = WIDTH * 2 + (y * n_z + z) * shard
                hidden[row : row + shard, aligned(tile, TILE)] = value[low : low + shard, :]

    def y_block(tile, y):
        rows = pl.ds(pl.multiple_of(WIDTH * 2 + y * y_rows, shard), y_rows)
        return hidden.at[rows, aligned(tile, TILE)]

    def z_piece(tile, z):
        rows = pl.ds(pl.multiple_of(WIDTH * 2 + (my_y * n_z + z) * shard, shard), shard)
        return hidden.at[rows, aligned(tile, TILE)]

    def own_tile(u, x):
        return u * n_d + x * 2 + at.core

    def g_core(u, x):
        src = dense(u * n_d + x * 2 + other)
        return remote(src, dense_core.at[u, x], s_gc.at[u, x], r_gc.at[u, x], at.partner())

    def g_y(u, x, j):
        src = y_block(own_tile(u, x), lax.rem(my_y + j, n_y))
        sems = s_gy.at[u, x, j - 1], r_gy.at[u, x, j - 1]
        return remote(src, dense_y.at[u, x, j - 1], *sems, (at.d, member(0, j)))

    def g_z(u, x, i):
        src = z_piece(own_tile(u, x), lax.rem(my_z + i, n_z))
        sems = s_gz.at[u, x, i], r_gz.at[u, x, i]
        return remote(src, dense_z.at[u, x, i], *sems, (at.d, member(i, 0)))

    def g_x(u, i):
        sems = s_gx.at[u, i - 1], r_gx.at[u, i - 1]
        return remote(dense_s.at[u], dense_x.at[u, i - 1], *sems, at.x_peer(i))

    def g_d(u, core):
        src = final.at[u, core]
        return remote(src, src, s_gd.at[u], r_gd.at[u], at.partner())

    def first_hop(u):
        for x in range(n_x):
            g_core(u, x).start()

    def second_hop(u):
        for x in range(n_x):
            g_core(u, x).wait_recv()
            tile = dense(own_tile(u, x))
            tile[...] = (tile[...].astype(F32) + dense_core[u, x].astype(F32)).astype(BF16)
            for j in range(1, n_y):
                g_y(u, x, j).start()

    def third_hop(u):
        for x in range(n_x):
            mine = y_block(own_tile(u, x), my_y)
            total = mine[...].astype(F32)
            for j in range(1, n_y):
                g_y(u, x, j).wait_recv()
                total = total + dense_y[u, x, j - 1].astype(F32)
            mine[...] = total.astype(BF16)
            for i in range(1, n_z):
                g_z(u, x, i).start()

    def fourth_hop(u):
        for x in range(n_x):
            total = z_piece(own_tile(u, x), my_z)[...].astype(F32)
            for i in range(1, n_z):
                g_z(u, x, i).wait_recv()
                total = total + dense_z[u, x, i].astype(F32)
            dense_s[u, x] = total.astype(BF16)
        for i in range(1, n_x):
            g_x(u, i).start()

    def fifth_hop(u):
        total = dense_s[u].astype(F32)
        for i in range(1, n_x):
            g_x(u, i).wait_recv()
            total = total + dense_x[u, i - 1].astype(F32)
        final[u, at.core] = total.astype(BF16)
        g_d(u, at.core).start()

    hops = (first_hop, second_hop, third_hop, fourth_hop, fifth_hop)

    d_wo = tn(mixed[...], routed[...])
    for pair in range(PAIRS):
        put_dense(4 * pair + 3, d_wo[:, pair * TILE : (pair + 1) * TILE])

    def attend_back(pair):
        for b, (low, high, row) in enumerate(WINDOWS):
            window = slice(row, row + high - low)
            grad = d_mixed[b * QBLK : (b + 1) * QBLK, aligned(pair, TILE)]
            values = qkv[2 * PAIRS + pair, low:high, :]
            for h in range(2):
                one = jnp.where(halves[h], grad, jnp.zeros_like(grad))
                scores[h, window, :] = nt(values, one)
        for b, (low, high, row) in enumerate(WINDOWS):
            window = slice(row, row + high - low)
            for h in range(2):
                share = probs[2 * pair + h, window, :].astype(F32)
                moved = share * scores[h, window, :]
                moved = moved - share * jnp.sum(moved, axis=0, keepdims=True)
                d_pre[window, h * 256 : h * 256 + QBLK] = moved.astype(BF16)
        for array in (acc_k, acc_v):
            array[...] = jnp.zeros_like(array)
        for b, (low, high, row) in enumerate(WINDOWS):
            window = slice(row, row + high - low)
            block = slice(b * QBLK, (b + 1) * QBLK)
            keys = qkv[PAIRS + pair, low:high, :]
            query = qkv[pair, block, :]
            grad = d_mixed[block, aligned(pair, TILE)]
            both = [
                [
                    tn(d_pre[window, h * 256 : h * 256 + QBLK], keys),
                    nn(d_pre[window, h * 256 : h * 256 + QBLK], query),
                    nn(probs[2 * pair + h, window, :], grad),
                ]
                for h in range(2)
            ]
            d_q, d_k, d_v = [jnp.where(halves[0], one, two) for one, two in zip(*both)]
            hidden[block, pl.ds(pl.multiple_of(pair * 384, 128), 128)] = (d_q * 0.125).astype(BF16)
            acc_k[low:high, :] += d_k
            acc_v[low:high, :] += d_v
        hidden[0:SLOTS, pl.ds(pl.multiple_of(pair * 384 + 128, 128), 128)] = acc_k[...].astype(BF16)
        hidden[0:SLOTS, pl.ds(pl.multiple_of(pair * 384 + 256, 128), 128)] = acc_v[...].astype(BF16)
        d_qkv = hidden[0:SLOTS, pl.ds(pl.multiple_of(pair * 384, 128), 384)]
        sums = jnp.sum(d_qkv.astype(F32), axis=0, keepdims=True)
        pack[2:3, aligned(pair, TILE)] = sums[:, 0:128]
        pack[3:4, aligned(pair, TILE)] = sums[:, 256:384]
        d_w = tn(normed[...], d_qkv)
        for c in range(3):
            put_dense(4 * pair + c, d_w[:, c * TILE : (c + 1) * TILE])

        @pl.when(lax.rem(pair, pairs_in_unit) == pairs_in_unit - 1)
        def _():
            unit = lax.div(pair, pairs_in_unit)
            for age, hop in enumerate(hops):

                @pl.when(unit >= age)
                def _(age=age, hop=hop):
                    hop(unit - age)

        @pl.when(pair == 0)
        def _():
            loop(3, LOTS, send_lot)


    acc_k, acc_v = bias.at[0:SLOTS, 0:TILE], bias.at[0:SLOTS, TILE : 2 * TILE]
    loop(0, PAIRS, attend_back)

    def later(step):
        for age, hop in enumerate(hops):
            if 0 <= step - age < units:
                hop(step - age)

    later(units)

    def first_back(i):
        block = aligned(i, ROWBLK)
        grad = nt(hidden[block, 0 : 3 * WIDTH], wfull[:, 0 : 3 * WIDTH])
        value, inv_std = normalize(tok[block, :].astype(F32))
        pack[0:1, :] += jnp.sum(grad * value, axis=0, keepdims=True)
        pack[1:2, :] += jnp.sum(grad, axis=0, keepdims=True)
        d_middle[block, :] += norm_back(grad, value, inv_std, vecs[0:1, :])

    loop(0, SLOTS // ROWBLK, first_back)
    save_tokens = pltpu.make_async_copy(d_middle.at[0:SLOTS, :], o_tokens, s_own.at[2 + n_mine])
    save_tokens.start()

    def p_dp(i):
        return remote(pack, pack_dp.at[i], s_p.at[i], r_p.at[i], at.dp_peer(i))

    for i in range(1, n_d):
        p_dp(i).start()
    later(units + 1)
    e_spread(n_mine - 1)
    loop(0, n_mine - 1, e_forward)

    def vec_lane(owner):
        return aligned(lax.div(owner * shard, TILE), TILE)

    def qv_lane(owner):
        return aligned(lax.div(lax.rem(owner * 2 * shard, WIDTH), TILE), TILE)

    def p_vec(k):
        src = pack_dp.at[0, 0:bias_at, vec_lane(at.ahead(k))]
        return remote(src, vec_f.at[k], s_vf.at[k], r_vf.at[k], at.fsdp_peer(k))

    def p_qv(k):
        src = pack_dp.at[0, 0:8, qv_lane(at.ahead(k))]
        return remote(src, qv_f.at[k], s_qf.at[k], r_qf.at[k], at.fsdp_peer(k))

    pack_dp[0] = pack[...]
    for i in range(1, n_d):
        p_dp(i).wait_recv()
        pack_dp[0] += pack_dp[i]
    loop(1, n_f, lambda k: [p_vec(k).start(), p_qv(k).start()])
    save_bias = pltpu.make_async_copy(
        pack_dp.at[0, bias_at : bias_at + 8, :], o_bias, s_own.at[3 + n_mine]
    )
    save_bias.start()
    later(units + 2)
    e_forward(n_mine - 1)

    loop(1, n_f, lambda r: returned(ret_o, table_o, s_o, r_o, r).wait_recv())

    def combine(i):
        block = aligned(i, ROWBLK)
        total = middle[block, :] + nn(gather_rows(block), table_o[...])
        routed[block, :] = total.astype(BF16)

    loop(0, SLOTS // ROWBLK, combine)
    save_out = pltpu.make_async_copy(routed, o_out, s_own.at[4 + n_mine])
    save_out.start()
    later(units + 3)

    loop(1, n_f, lambda k: [p_vec(k).wait_recv(), p_qv(k).wait_recv()])
    vec_f[0] = pack_dp[0, 0:bias_at, vec_lane(at.me)]
    qv_f[0] = pack_dp[0, 0:8, qv_lane(at.me)]

    def add_lanes(k):
        vec_f[0] += vec_f[k]
        qv_f[0] += qv_f[k]

    loop(1, n_f, add_lanes)
    save_vec = pltpu.make_async_copy(vec_f.at[0], o_vec, s_own.at[5 + n_mine])
    save_qv = pltpu.make_async_copy(qv_f.at[0], o_qv, s_own.at[6 + n_mine])
    save_vec.start()
    save_qv.start()
    loop(0, units, lambda u: g_d(u, other).wait_recv())
    save_dense = pltpu.make_async_copy(final, o_dense, s_own.at[7 + n_mine])
    save_dense.start()

    def ended_f(k):
        send_v(k).wait_send()
        got_w(k).wait_send()
        for i in range(1, n_x):
            share_x(i, k).wait_send()
        for i in range(n_x):
            share_core(i, k).wait_send()
        give_back(ret_d, table_d, s_d, r_d, k).wait_send()
        give_back(ret_o, table_o, s_o, r_o, k).wait_send()
        p_vec(k).wait_send()
        p_qv(k).wait_send()

    loop(1, n_f, ended_f)

    def ended_e(j):
        to_partner(j).wait_send()
        for i in range(1, n_x):
            to_x(i, j).wait_send()
            all_x(i, j).wait_send()
        for i in range(n_x):
            to_core(i, j, at.core).wait_send()
            to_core(i, j, other).wait_recv()
            to_self(i, j).wait()

    loop(0, n_mine, ended_e)

    def ended_u(u):
        for x in range(n_x):
            g_core(u, x).wait_send()
            for j in range(1, n_y):
                g_y(u, x, j).wait_send()
            for i in range(1, n_z):
                g_z(u, x, i).wait_send()
        for i in range(1, n_x):
            g_x(u, i).wait_send()
        g_d(u, at.core).wait_send()

    loop(0, units, ended_u)
    for i in range(1, n_d):
        p_dp(i).wait_send()
    for copy in (save_tokens, save_bias, save_out, save_vec, save_qv, save_dense):
        copy.wait()


def block(n_f, n_d, experts, cap, cap_rows, small, w_in, w_out, b_in, b_out):
    vmem = pl.BlockSpec(memory_space=pltpu.VMEM)
    hbm = pl.BlockSpec(memory_space=pl.ANY)
    n_x = n_d // 2
    more_x = max(n_x - 1, 1)
    vec_rows = -(-(8 + experts) // 16) * 16
    shard = WIDTH // n_f
    table = n_f * cap_rows
    hid = w_in.shape[1]
    units = 16 // n_d
    n_mine = hid // FTILE
    n_y = y_members(n_f)
    more_y = max(n_y - 1, 1)
    pack_rows = 8 + experts + 8
    sds = jax.ShapeDtypeStruct
    vm = pltpu.VMEM
    dma = pltpu.SemaphoreType.DMA
    chunk_rows = table // CHUNKS
    pairs_of = lambda *shape: [dma(shape), dma(shape)]
    return pl.pallas_call(
        functools.partial(block_kernel, n_f, n_d, experts, cap, cap_rows),
        out_shape=(
            sds((SLOTS, WIDTH), BF16),
            sds((SLOTS, WIDTH), F32),
            sds((2 * n_mine, FTILE, WIDTH), BF16),
            sds((units, 2, n_x, shard, TILE), BF16),
            sds((8 + experts, TILE), F32),
            sds((8, TILE), F32),
            sds((8, WIDTH), F32),
        ),
        in_specs=[hbm] * 2 + [vmem] * (len(small) - 2) + [hbm] * 2 + [vmem] * 2,
        out_specs=[hbm] * 7,
        scratch_shapes=[
            vm((SLOTS, WIDTH), BF16),
            vm((SLOTS, WIDTH), BF16),
            vm((WIDTH, 4 * WIDTH), BF16),
            vm((vec_rows, WIDTH), BF16),
            vm((vec_rows, WIDTH), F32),
            vm((KEYS, 2 * TILE), F32),
            vm((2, KEYS, QBLK), F32),
            vm((2 * PAIRS, KEYS, QBLK), BF16),
            vm((3 * PAIRS, SLOTS, TILE), BF16),
            vm((SLOTS, WIDTH), BF16),
            vm((SLOTS, WIDTH), BF16),
            vm((SLOTS, WIDTH), F32),
            vm((SLOTS, WIDTH), BF16),
            vm((SLOTS, 8), F32),
        ]
        + [vm((table, WIDTH), BF16)] * 4
        + [
            vm((WIDTH, hid), BF16),
            vm((hid, WIDTH), BF16),
            vm((table, hid), BF16),
            vm((table, hid), BF16),
        ]
        + [vm((table, WIDTH), BF16)] * 3
        + [
            vm((2 * n_mine, FTILE, WIDTH), BF16),
            vm((n_mine, FTILE, WIDTH), BF16),
            vm((more_x, n_mine, FTILE // n_x, WIDTH), BF16),
            vm((units, n_x, WIDTH, TILE), BF16),
            vm((units, n_x, more_y, n_f // n_y * shard, TILE), BF16),
            vm((units, n_x, n_f // n_y, shard, TILE), BF16),
            vm((units, n_x, shard, TILE), BF16),
            vm((units, more_x, n_x, shard, TILE), BF16),
            vm((units, 2, n_x, shard, TILE), BF16),
            vm((pack_rows, WIDTH), F32),
            vm((n_d, pack_rows, WIDTH), F32),
            vm((n_f, 8 + experts, TILE), F32),
            vm((n_f, 8, TILE), F32),
            vm((max(2 * chunk_rows, SLOTS), WIDTH), F32),
        ]
        + pairs_of(n_f)
        + pairs_of(n_f)
        + pairs_of(more_x, n_f)
        + pairs_of(n_x, n_f)
        + pairs_of(n_f)
        + pairs_of(n_f)
        + pairs_of(n_f)
        + pairs_of(n_f)
        + pairs_of(n_mine)
        + pairs_of(more_x, n_mine)
        + pairs_of(more_x, n_mine)
        + pairs_of(n_x, n_mine)
        + pairs_of(units, n_x)
        + pairs_of(units, n_x, more_y)
        + pairs_of(units, n_x, n_f // n_y)
        + pairs_of(units, more_x)
        + pairs_of(units)
        + pairs_of(n_d)
        + pairs_of(n_f)
        + pairs_of(n_f)
        + [dma((8 + n_mine,)), dma((n_x, n_mine)), pltpu.SemaphoreType.REGULAR],
        compiler_params=pltpu.CompilerParams(
            collective_id=0, has_side_effects=True, vmem_limit_bytes=63 << 20
        ),
        name="block",
    )(*small, w_in, w_out, b_in, b_out)


def finish_kernel(
    n_f,
    experts,
    in_out,
    in_tokens,
    in_expert,
    dense,
    vec,
    qv,
    biases,
    o_out,
    o_tokens,
    o_g1,
    o_s1,
    o_qkv,
    o_bqv,
    o_wo,
    o_bo,
    o_g2,
    o_s2,
    o_router,
    o_w_in,
    o_b_in,
    o_w_out,
    o_b_out,
    low,
    wide,
    rows_low,
    rows_wide,
    s_load,
    s_save,
):
    me = lax.axis_index("fsdp")
    shard = WIDTH // n_f
    tiles = in_expert.shape[0]
    loads = [pltpu.make_async_copy(in_expert.at[t], low.at[t], s_load.at[t]) for t in range(tiles)]
    for load in loads:
        load.start()
    rows_in = [
        pltpu.make_async_copy(in_out, rows_low, s_load.at[tiles]),
        pltpu.make_async_copy(in_tokens, rows_wide, s_load.at[tiles + 1]),
    ]
    for load in rows_in:
        load.start()

    def my_lanes(value, size):
        place = lax.rem(me * size, TILE)
        total = jnp.zeros((value.shape[0], size), F32)
        for low_lane in range(0, TILE, size):
            total = total + jnp.where(place == low_lane, value[:, low_lane : low_lane + size], 0.0)
        return total

    own = my_lanes(vec[...], shard)
    for row, ref in ((0, o_g1), (1, o_s1), (4, o_bo), (5, o_g2), (6, o_s2)):
        ref[...] = own[row : row + 1, :]
    o_router[...] = own[8 : 8 + experts, :]
    lines = my_lanes(qv[...], 2 * shard)
    o_bqv[...] = jnp.where(me * 2 * shard < WIDTH, lines[2:3, :], lines[3:4, :])
    n_d = 2 * dense.shape[2]

    def tile(t):
        return dense[t // n_d, t % 2, t % n_d // 2].astype(F32)

    for pair in range(PAIRS):
        for c in range(3):
            at = c * WIDTH + pair * TILE
            o_qkv[:, at : at + TILE] = tile(4 * pair + c)
        o_wo[:, pair * TILE : (pair + 1) * TILE] = tile(4 * pair + 3)
    for f in range(tiles // 2):
        o_b_in[:, f * FTILE : (f + 1) * FTILE] = biases[f : f + 1, :]
    o_b_out[...] = biases[4:5, :]
    saves = []
    for t in range(tiles):
        loads[t].wait()
        wide[t] = low[t].astype(F32)
        piece = pl.ds(t // 2 * FTILE, FTILE)
        dst = o_w_out.at[0, piece, :] if t % 2 else o_w_in.at[0, :, piece]
        saves.append(pltpu.make_async_copy(wide.at[t], dst, s_save.at[t]))
        saves[-1].start()
    rows_out = [
        pltpu.make_async_copy(rows_low, o_out, s_save.at[tiles]),
        pltpu.make_async_copy(rows_wide, o_tokens, s_save.at[tiles + 1]),
    ]
    for load, save in zip(rows_in, rows_out):
        load.wait()
        save.start()
    for save in saves + rows_out:
        save.wait()


def finish(n_f, experts, hid, parts):
    vmem = pl.BlockSpec(memory_space=pltpu.VMEM)
    hbm = pl.BlockSpec(memory_space=pl.ANY)
    shard = WIDTH // n_f
    tiles = parts[2].shape[0]
    line = lambda *shape: jax.ShapeDtypeStruct(shape, F32)
    return pl.pallas_call(
        functools.partial(finish_kernel, n_f, experts),
        out_shape=(
            jax.ShapeDtypeStruct((SLOTS, WIDTH), BF16),
            line(SLOTS, WIDTH),
            line(1, shard),
            line(1, shard),
            line(shard, 3 * WIDTH),
            line(1, 2 * shard),
            line(shard, WIDTH),
            line(1, shard),
            line(1, shard),
            line(1, shard),
            line(experts, shard),
            line(1, WIDTH, hid),
            line(1, hid),
            line(1, hid, WIDTH),
            line(1, WIDTH),
        ),
        in_specs=[hbm] * 3 + [vmem] * 4,
        out_specs=[hbm] * 2 + [vmem] * 9 + [hbm, vmem, hbm, vmem],
        scratch_shapes=[
            pltpu.VMEM((tiles, FTILE, WIDTH), BF16),
            pltpu.VMEM((tiles, FTILE, WIDTH), F32),
            pltpu.VMEM((SLOTS, WIDTH), BF16),
            pltpu.VMEM((SLOTS, WIDTH), F32),
            pltpu.SemaphoreType.DMA((tiles + 2,)),
            pltpu.SemaphoreType.DMA((tiles + 2,)),
        ],
        compiler_params=pltpu.CompilerParams(vmem_limit_bytes=62 << 20),
        name="finish",
    )(*parts)


def shards(
    tokens,
    cotangent,
    segment_ids,
    pad_mask,
    expert_ids,
    priority,
    ln1_gain,
    ln1_shift,
    w_qkv,
    b_qv,
    w_o,
    b_o,
    ln2_gain,
    ln2_shift,
    w_router,
    w_in,
    b_in,
    w_out,
    b_out,
    n_f,
    n_d,
):
    experts = w_router.shape[1]
    cap = (21 * tokens.shape[0] + 10 * experts - 1) // (10 * experts)
    cap_rows = -(-cap // 16) * 16
    line = lambda vector: vector.reshape(1, -1)
    small = (
        tokens,
        cotangent,
        segment_ids,
        pad_mask,
        expert_ids.T,
        priority,
        w_qkv,
        w_o,
        line(ln1_gain),
        line(ln1_shift),
        line(b_qv),
        line(b_o),
        line(ln2_gain),
        line(ln2_shift),
        w_router.T,
    )
    parts = block(n_f, n_d, experts, cap, cap_rows, small, w_in[0], w_out[0], b_in, b_out)
    done = finish(n_f, experts, w_in.shape[2], parts)
    flat = (2, 3, 5, 7, 8, 9)
    done = [value.reshape(-1) if i in flat else value for i, value in enumerate(done)]
    done[10] = done[10].T
    return tuple(done)


def solution(mesh):
    both, one = P(("dp", "fsdp")), P("fsdp")
    n_f, n_d = mesh.shape["fsdp"], mesh.shape["dp"]
    return jax.shard_map(
        functools.partial(shards, n_f=n_f, n_d=n_d),
        mesh=mesh,
        in_specs=(both,) * 6 + (one,) * 13,
        out_specs=(both,) * 2 + (one,) * 13,
        check_vma=False,
    )
```

```python
import functools

import jax
import jax.numpy as jnp
from jax import lax
from jax.experimental import pallas as pl
from jax.experimental.pallas import tpu as pltpu
from jax.sharding import PartitionSpec as P

MESH = pl.DeviceIdType.MESH
BF16 = jnp.bfloat16
F32 = jnp.float32
SLOTS = 720
WIDTH = 512
PAIRS = 4
EPS = 1e-06
WINDOWS = ((0, 384, 0), (96, 624, 384), (336, 720, 912))
KEYS = 1296
QBLK = 240
ROWBLK = 240
TILE = 128
FTILE = 512
CHUNKS = 4
LOTS = 7


def nt(left, right):
    return lax.dot_general(left, right, (((1,), (1,)), ((), ())), preferred_element_type=F32)


def tn(left, right):
    return lax.dot_general(left, right, (((0,), (0,)), ((), ())), preferred_element_type=F32)


def nn(left, right):
    return jnp.dot(left, right, preferred_element_type=F32)


def normalize(value):
    centred = value - jnp.mean(value, axis=-1, keepdims=True)
    inv_std = lax.rsqrt(jnp.mean(centred * centred, axis=-1, keepdims=True) + EPS)
    return centred * inv_std, inv_std


def aligned(index, size):
    return pl.ds(pl.multiple_of(index * size, size), size)


class Place:
    def __init__(self, n_f, n_d):
        self.n_f, self.n_d, self.n_x = n_f, n_d, n_d // 2
        self.me = lax.axis_index("fsdp")
        self.d = lax.axis_index("dp")
        self.x = lax.div(self.d, 2)
        self.core = lax.rem(self.d, 2)

    def ahead(self, k):
        return lax.rem(self.me + k, self.n_f)

    def fsdp_peer(self, k):
        return (self.d, self.ahead(k))

    def x_index(self, i):
        return lax.rem(self.x + i, self.n_x)

    def x_peer(self, i):
        return (self.x_index(i) * 2 + self.core, self.me)

    def partner(self):
        return (self.x * 2 + 1 - self.core, self.me)

    def dp_peer(self, i):
        return (lax.rem(self.d + i, self.n_d), self.me)

    def enter(self):
        bar = pltpu.get_barrier_semaphore()

        def greet(k, _):
            pl.semaphore_signal(bar, inc=1, device_id=self.fsdp_peer(k), device_id_type=MESH)
            return 0

        lax.fori_loop(1, self.n_f, greet, 0)
        for i in range(1, self.n_d):
            pl.semaphore_signal(bar, inc=1, device_id=self.dp_peer(i), device_id_type=MESH)
        pl.semaphore_wait(bar, self.n_f - 1 + self.n_d - 1)


def remote(src, dst, send_sem, recv_sem, device):
    return pltpu.make_async_remote_copy(
        src_ref=src,
        dst_ref=dst,
        send_sem=send_sem,
        recv_sem=recv_sem,
        device_id=device,
        device_id_type=MESH,
    )


def loop(low, high, body):
    def step(k, carry):
        body(k)
        return carry

    lax.fori_loop(low, high, step, 0)


def y_members(n_f):
    return 1 << ((n_f.bit_length() - 1) // 2)


def block_kernel(
    n_f,
    n_d,
    experts,
    cap,
    cap_rows,
    tok_hbm,
    cot_hbm,
    segment,
    pad,
    chosen_ids,
    priority,
    w_qkv,
    w_o,
    gain_one,
    shift_one,
    b_qv,
    b_o,
    gain_two,
    shift_two,
    w_router,
    w_in_hbm,
    w_out_hbm,
    b_in,
    b_out,
    o_out,
    o_tokens,
    o_expert,
    o_dense,
    o_vec,
    o_qv,
    o_bias,
    tok,
    cot,
    wfull,
    vsh,
    vecs,
    bias,
    scores,
    probs,
    qkv,
    normed,
    mixed,
    middle,
    routed,
    place,
    send_x,
    send_g,
    x_in,
    g_in,
    w_in,
    w_out,
    hidden,
    d_pre,
    ret_d,
    ret_o,
    table_d,
    ew,
    ew_core,
    ew_x,
    dense_core,
    dense_y,
    dense_z,
    dense_s,
    dense_x,
    final,
    pack,
    pack_dp,
    vec_f,
    qv_f,
    d_middle,
    s_w,
    r_w,
    s_v,
    r_v,
    s_dx,
    r_dx,
    s_dc,
    r_dc,
    s_g,
    r_g,
    s_x,
    r_x,
    s_d,
    r_d,
    s_o,
    r_o,
    s_ec,
    r_ec,
    s_ex,
    r_ex,
    s_ea,
    r_ea,
    s_eb,
    r_eb,
    s_gc,
    r_gc,
    s_gy,
    r_gy,
    s_gz,
    r_gz,
    s_gx,
    r_gx,
    s_gd,
    r_gd,
    s_p,
    r_p,
    s_vf,
    r_vf,
    s_qf,
    r_qf,
    s_own,
    s_self,
    ready,
):
    at = Place(n_f, n_d)
    n_x = at.n_x
    shard = WIDTH // n_f
    colw = 4 * WIDTH // n_d
    other = 1 - at.core

    def cols_of(d):
        return aligned(d, colw)

    def w_piece(owner, d):
        return wfull.at[aligned(owner, shard), cols_of(d)]

    def x_back(i):
        return at.x_index(n_x - i)

    load_in = pltpu.make_async_copy(w_in_hbm, w_in, s_own.at[0])
    load_out = pltpu.make_async_copy(w_out_hbm, w_out, s_own.at[1])
    load_tok = pltpu.make_async_copy(tok_hbm, tok, s_own.at[2])
    load_cot = pltpu.make_async_copy(cot_hbm, cot, s_own.at[3])
    for load in (load_cot, load_tok, load_in, load_out):
        load.start()
    at.enter()

    n_y = y_members(n_f)
    n_z = n_f // n_y
    my_z, my_y = lax.div(at.me, n_y), lax.rem(at.me, n_y)

    def member(z, y):
        return lax.rem(my_z + z, n_z) * n_y + lax.rem(my_y + y, n_y)

    def owner(k):
        return member(n_z - lax.rem(k, n_z), n_y - lax.div(k, n_z))

    def along_z(k):
        piece = w_piece(at.me, at.d)
        return remote(piece, piece, s_w.at[k], r_w.at[k], (at.d, member(k, 0)))

    def along_y(j, i):
        piece, k = w_piece(member(n_z - i, 0), at.d), j * n_z + i
        return remote(piece, piece, s_w.at[k], r_w.at[k], (at.d, member(0, j)))

    def got_w(k):
        piece = w_piece(owner(k), at.d)
        return remote(piece, piece, s_w.at[k], r_w.at[k], (at.d, at.me))

    vec_rows = vsh.shape[0]

    def vec_piece(owner):
        return hidden.at[aligned(owner, vec_rows), 0:WIDTH]

    def send_v(k):
        return remote(vsh, vec_piece(at.me), s_v.at[k], r_v.at[k], at.fsdp_peer(k))

    def share_x(i, k):
        piece = w_piece(owner(k), at.d)
        return remote(piece, piece, s_dx.at[i - 1, k], r_dx.at[i - 1, k], at.x_peer(i))

    def share_core(i, k):
        piece = w_piece(owner(k), x_back(i) * 2 + at.core)
        return remote(piece, piece, s_dc.at[i, k], r_dc.at[i, k], at.partner())

    own = aligned(at.me, shard)
    for pair in range(PAIRS):
        for c in range(3):
            low = (3 * pair + c) * TILE
            src = c * WIDTH + pair * TILE
            wfull[own, low : low + TILE] = w_qkv[:, src : src + TILE]
    wfull[own, 3 * WIDTH : 4 * WIDTH] = w_o[...]
    loop(1, n_z, lambda k: along_z(k).start())
    loop(1, n_y, lambda j: along_y(j, 0).start())

    def placing(size, low):
        shape = (size, WIDTH)
        target = lax.broadcasted_iota(jnp.int32, shape, 1) + low
        source = lax.broadcasted_iota(jnp.int32, shape, 0) + at.me * size
        return jnp.where(target == source, 1.0, 0.0).astype(BF16)

    blank = jnp.zeros((1, shard), F32)
    stack = [
        blank if ref is None else ref[...].astype(F32)
        for ref in (gain_one, shift_one, None, None, b_o, gain_two, shift_two, None)
    ]
    spread = nn(jnp.concatenate(stack, axis=0).astype(BF16), placing(shard, 0))
    row_iota = lax.broadcasted_iota(jnp.int32, (8, WIDTH), 0)
    for r in range(2):
        line = nn(b_qv[...], placing(2 * shard, r * WIDTH))
        spread = spread + jnp.where(row_iota == 2 + r, line, 0.0)
    router_rows = nn(w_router[...], placing(shard, 0))
    rest = jnp.zeros((vec_rows - 8 - experts, WIDTH), F32)
    parts = [spread, router_rows] + ([rest] if vec_rows > 8 + experts else [])
    vsh[...] = jnp.concatenate(parts, axis=0).astype(BF16)
    vec_piece(at.me)[...] = vsh[...]
    loop(1, n_f, lambda k: send_v(k).start())

    seg_r, pad_r, pri_r = (
        ref[...].reshape(1, SLOTS).astype(F32) for ref in (segment, pad, priority)
    )
    lines = jnp.concatenate([seg_r, pad_r, pri_r, jnp.zeros((5, SLOTS), F32)], axis=0)
    columns = jnp.transpose(lines)
    seg_c, pad_c, pri_c = (columns[:, j : j + 1] for j in range(3))
    expert_iota = lax.broadcasted_iota(jnp.int32, (experts, SLOTS), 0)
    live = pad_r > 0
    before = jnp.where(pri_c < pri_r, 1.0, 0.0).astype(BF16)
    chose = [jnp.where((chosen_ids[k : k + 1, :] == expert_iota) & live, 1.0, 0.0) for k in range(2)]
    rank = [nn(one.astype(BF16), before) for one in chose]
    rank[1] = rank[1] + jnp.sum(chose[0], axis=1, keepdims=True)
    spot_r = []
    for k in range(2):
        slot = jnp.sum(chose[k] * rank[k], axis=0, keepdims=True)
        spot = chosen_ids[k : k + 1, :].astype(F32) * cap_rows + slot
        spot_r.append(jnp.where(live & (slot < cap), spot, -1.0))
    place[...] = jnp.transpose(jnp.concatenate(spot_r + [jnp.zeros((6, SLOTS), F32)], axis=0))
    slot_iota = lax.broadcasted_iota(jnp.int32, (cap_rows, SLOTS), 0)

    def pick(expert):
        mine = (slot_iota + expert * cap_rows).astype(F32)
        return jnp.where((mine == spot_r[0]) | (mine == spot_r[1]), 1.0, 0.0).astype(BF16)

    for b, (low, high, row) in enumerate(WINDOWS):
        queries = slice(b * QBLK, (b + 1) * QBLK)
        shape = (high - low, QBLK)
        same = seg_c[low:high, :] == seg_r[:, queries]
        itself = (lax.broadcasted_iota(jnp.int32, shape, 0) + low) == (
            lax.broadcasted_iota(jnp.int32, shape, 1) + b * QBLK
        )
        allowed = same & ((pad_c[low:high, :] > 0) | itself)
        bias[row : row + high - low, 0:QBLK] = jnp.where(allowed, 0.0, -1e30)

    chunk_rows = n_f * cap_rows // CHUNKS
    sources = n_f // CHUNKS

    def position(step, side):
        inner = lax.rem(lax.div(step + 1, 2), 2)
        near = 1 + 2 * lax.rem(step + 1 + side, 2)
        return inner * near + (1 - inner) * 2 * lax.div(step, 3)

    z_side = lax.rem(my_z, 2)

    def send_rows(buffer, into, send, recv, k):
        return remote(
            buffer.at[aligned(at.ahead(k), cap_rows), :],
            into.at[aligned(n_f - k, cap_rows), :],
            send.at[k],
            recv.at[n_f - k],
            at.fsdp_peer(k),
        )

    def dispatch(source, buffer, into, send, recv):
        into[0:cap_rows, :] = nn(pick(at.me), source[...]).astype(BF16)

        def stage(step):
            first = position(step, 1 - z_side) * sources

            def one(r):
                @pl.when(r > 0)
                def _():
                    k = n_f - r
                    expert = at.ahead(k)
                    rows = nn(pick(expert), source[...]).astype(BF16)
                    buffer[aligned(expert, cap_rows), :] = rows
                    send_rows(buffer, into, send, recv, k).start()

            loop(first, first + sources, one)

        loop(0, CHUNKS, stage)

    def pass_on(k):
        for i in range(1, n_x):
            share_x(i, k).start()
        share_core(0, k).start()

    def from_z(k):
        got_w(k).wait_recv()
        loop(1, n_y, lambda j: along_y(j, k).start())
        pass_on(k)

    def from_y(k):
        got_w(k).wait_recv()
        pass_on(k)

    loop(1, n_z, from_z)
    load_cot.wait()
    dispatch(cot, send_g, g_in, s_g, r_g)
    loop(n_z, n_f, from_y)

    loop(1, n_f, lambda k: send_v(k).wait_recv())
    vecs[...] = vec_piece(0)[...].astype(F32)

    def add_vectors(owner):
        vecs[...] += vec_piece(owner)[...].astype(F32)

    loop(1, n_f, add_vectors)

    load_tok.wait()

    def first_norm(i):
        block = aligned(i, ROWBLK)
        value, _ = normalize(tok[block, :].astype(F32))
        normed[block, :] = (value * vecs[0:1, :] + vecs[1:2, :]).astype(BF16)

    loop(0, SLOTS // ROWBLK, first_norm)

    for i in range(1, n_x):

        def cross(k, i=i):
            piece = w_piece(owner(k), x_back(i) * 2 + at.core)
            remote(piece, piece, s_dx.at[i - 1, k], r_dx.at[i - 1, k], at.x_peer(i)).wait_recv()
            share_core(i, k).start()

        loop(1, n_f, cross)
    for i in range(n_x):

        def arrive(k, i=i):
            piece = w_piece(owner(k), x_back(i) * 2 + other)
            remote(piece, piece, s_dc.at[i, k], r_dc.at[i, k], at.partner()).wait_recv()

        loop(1, n_f, arrive)

    def project(pair):
        out = nn(normed[...], wfull[:, pl.ds(pl.multiple_of(pair * 384, 128), 384)])
        lanes = aligned(pair, TILE)
        qkv[pair] = ((out[:, 0:128] + vecs[2:3, lanes]) * 0.125).astype(BF16)
        qkv[PAIRS + pair] = out[:, 128:256].astype(BF16)
        qkv[2 * PAIRS + pair] = (out[:, 256:384] + vecs[3:4, lanes]).astype(BF16)

    loop(0, PAIRS, project)

    lane = lax.broadcasted_iota(jnp.int32, (1, TILE), 1)
    halves = (lane < 64, lane >= 64)

    def attend(pair):
        for b, (low, high, row) in enumerate(WINDOWS):
            window = slice(row, row + high - low)
            query = qkv[pair, b * QBLK : (b + 1) * QBLK, :]
            keys = qkv[PAIRS + pair, low:high, :]
            for h in range(2):
                one = jnp.where(halves[h], query, jnp.zeros_like(query))
                scores[h, window, :] = nt(keys, one) + bias[window, 0:QBLK]
        for b, (low, high, row) in enumerate(WINDOWS):
            window = slice(row, row + high - low)
            for h in range(2):
                value = scores[h, window, :]
                power = jnp.exp(value - jnp.max(value, axis=0, keepdims=True))
                share = 1.0 / jnp.sum(power, axis=0, keepdims=True)
                probs[2 * pair + h, window, :] = (power * share).astype(BF16)
        for b, (low, high, row) in enumerate(WINDOWS):
            window = slice(row, row + high - low)
            values = qkv[2 * PAIRS + pair, low:high, :]
            both = [tn(probs[2 * pair + h, window, :], values) for h in range(2)]
            mixed[b * QBLK : (b + 1) * QBLK, aligned(pair, TILE)] = jnp.where(
                halves[0], both[0], both[1]
            ).astype(BF16)

    loop(0, PAIRS, attend)

    def second_norm(i):
        block = aligned(i, ROWBLK)
        total = nn(mixed[block, :], wfull[:, 3 * WIDTH : 4 * WIDTH])
        total = tok[block, :].astype(F32) + total + vecs[4:5, :]
        middle[block, :] = total
        value, _ = normalize(total)
        routed[block, :] = (value * vecs[5:6, :] + vecs[6:7, :]).astype(BF16)

    loop(0, SLOTS // ROWBLK, second_norm)
    dispatch(routed, send_x, x_in, s_x, r_x)

    load_in.wait()
    load_out.wait()
    pack[...] = jnp.zeros_like(pack)

    def clear(t):
        ew[t] = jnp.zeros((FTILE, WIDTH), BF16)

    loop(0, ew.shape[0], clear)
    router = vecs[8 : 8 + experts, :].astype(BF16)
    f_tiles = w_in.shape[1] // FTILE
    bias_at = 8 + experts
    hot = jnp.where(lax.broadcasted_iota(jnp.int32, (1, experts), 1) == at.me, 1.0, 0.0)

    def give_back(buffer, into, send, recv, r):
        return remote(
            buffer.at[aligned(r, cap_rows), :],
            into.at[aligned(at.me, cap_rows), :],
            send.at[r],
            recv.at[r],
            at.fsdp_peer(r),
        )

    acc_o, acc_d = d_middle.at[0:chunk_rows, :], d_middle.at[chunk_rows : 2 * chunk_rows, :]

    def expert_chunk(step):
        pos = position(step, z_side)
        block = aligned(pos, chunk_rows)
        first = pos * sources

        def arrive(r):
            @pl.when(r > 0)
            def _():
                send_rows(send_g, g_in, s_g, r_g, n_f - r).wait_recv()
                send_rows(send_x, x_in, s_x, r_x, n_f - r).wait_recv()

        loop(first, first + sources, arrive)
        x_rows = x_in[block, :]
        logits = nt(x_rows, router)
        gates = jnp.exp(logits - jnp.max(logits, axis=-1, keepdims=True))
        gates = gates / jnp.sum(gates, axis=-1, keepdims=True)
        chosen = jnp.sum(gates * hot, axis=-1, keepdims=True)
        g_rows = (chosen * g_in[block, :].astype(F32)).astype(BF16)
        g_in[block, :] = g_rows
        pack[bias_at + 4 : bias_at + 5, :] += jnp.sum(g_rows.astype(F32), axis=0, keepdims=True)
        acc_o[...] = jnp.broadcast_to(b_out[...].astype(F32), acc_o.shape)
        acc_d[...] = jnp.zeros_like(acc_d)
        def tile(f):
            lanes = aligned(f, FTILE)
            pre = nn(x_in[block, :], w_in[:, lanes]) + b_in[:, lanes].astype(F32)
            d_act = nt(g_in[block, :], w_out[lanes, :])
            cdf = 0.5 + 0.5 * lax.erf(pre * 0.7071067811865476)
            act = (pre * cdf).astype(BF16)
            slope = cdf + pre * jnp.exp(-0.5 * pre * pre) * 0.3989422804014327
            d_row = (d_act * slope).astype(BF16)
            hidden[block, lanes] = act
            d_pre[block, lanes] = d_row
            pack[pl.ds(bias_at + f, 1), :] += jnp.sum(
                d_row.astype(F32), axis=0, keepdims=True
            )
            acc_o[...] += nn(act, w_out[lanes, :])
            acc_d[...] += nt(d_row, w_in[:, lanes])

        loop(0, f_tiles, tile)
        result = acc_o[...]
        weight = jnp.sum(g_in[block, :].astype(F32) * result, axis=-1, keepdims=True)
        d_logits = (weight * (hot - gates)).astype(BF16)
        pack[8:bias_at, :] += tn(d_logits, x_in[block, :])
        ret_d[block, :] = (acc_d[...] + nn(d_logits, router)).astype(BF16)
        ret_o[block, :] = (chosen * result).astype(BF16)

        def back(r):
            @pl.when(r > 0)
            def _():
                give_back(ret_d, table_d, s_d, r_d, r).start()

        loop(first, first + sources, back)

        @pl.when(step < CHUNKS - 1)
        def _():
            loop(0, f_tiles, lambda f: add_tiles(f, block))

    def add_tiles(f, block):
        lanes = aligned(f, FTILE)
        product = tn(x_in[block, :], d_pre[block, lanes])
        ew[2 * f] = (ew[2 * f].astype(F32) + product).astype(BF16)
        product = tn(hidden[block, lanes], g_in[block, :])
        ew[2 * f + 1] = (ew[2 * f + 1].astype(F32) + product).astype(BF16)

    loop(0, CHUNKS, expert_chunk)
    last = pl.ds(2 * chunk_rows, chunk_rows)
    mine = aligned(at.me, cap_rows)
    table_d[mine, :] = ret_d[0:cap_rows, :]

    part = FTILE // n_x
    per_core = f_tiles // 2

    def e_tile(core, j):
        return (core * per_core + j // 2) * 2 + j % 2

    def to_partner(j):
        return remote(ew.at[e_tile(other, j)], ew_core.at[j], s_ec.at[j], r_ec.at[j], at.partner())

    def to_x(i, j):
        src = ew.at[e_tile(at.core, j), aligned(at.x_index(i), part), :]
        return remote(src, ew_x.at[i - 1, j], s_ex.at[i - 1, j], r_ex.at[i - 1, j], at.x_peer(i))

    def e_part(core, j, x):
        return e_tile(core, j), aligned(x, part)

    def all_x(i, j):
        src = ew.at[e_tile(at.core, j), aligned(at.x, part), :]
        dst = ew_core.at[j, aligned(at.x, part), :]
        return remote(src, dst, s_ea.at[i - 1, j], r_ea.at[i - 1, j], at.x_peer(i))

    def from_x(i, j):
        dst = ew_core.at[j, aligned(x_back(i), part), :]
        return remote(dst, dst, s_ea.at[i - 1, j], r_ea.at[i - 1, j], at.x_peer(i))

    def e_result(i, j):
        piece = aligned(x_back(i), part)
        return ew.at[e_tile(at.core, j), piece, :] if i == 0 else ew_core.at[j, piece, :]

    def to_core(i, j, core):
        dst = o_expert.at[e_tile(core, j), aligned(x_back(i), part), :]
        return remote(e_result(i, j), dst, s_eb.at[i, j], r_eb.at[i, j], at.partner())

    def to_self(i, j):
        dst = o_expert.at[e_tile(at.core, j), aligned(x_back(i), part), :]
        return pltpu.make_async_copy(e_result(i, j), dst, s_self.at[i, j])

    n_mine = 2 * per_core

    def theirs(f):
        add_tiles(other * per_core + f, last)
        to_partner(2 * f).start()
        to_partner(2 * f + 1).start()

    def sum_cores(j):
        to_partner(j).wait_recv()
        tile = e_tile(at.core, j)
        ew[tile] = (ew[tile].astype(F32) + ew_core[j].astype(F32)).astype(BF16)
        for i in range(1, n_x):
            to_x(i, j).start()

    def tile_row(f):
        theirs(f)
        add_tiles(at.core * per_core + f, last)
        sum_cores(2 * f)
        sum_cores(2 * f + 1)

    loop(0, per_core, tile_row)

    table_o = send_x

    def left(k):
        send_rows(send_x, x_in, s_x, r_x, k).wait_send()

    loop(1, n_f, left)
    table_o[mine, :] = ret_o[0:cap_rows, :]

    def tell(k):
        pl.semaphore_signal(ready, inc=1, device_id=at.fsdp_peer(k), device_id_type=MESH)

    loop(1, n_f, tell)
    pl.semaphore_wait(ready, n_f - 1)

    def send_lot(lot):
        def one(step):
            r = 1 + lax.rem(1 + step, n_f - 1)
            give_back(ret_o, table_o, s_o, r_o, r).start()

        loop(lax.div((n_f - 1) * lot, LOTS), lax.div((n_f - 1) * (lot + 1), LOTS), one)

    loop(0, 3, send_lot)

    def returned(buffer, into, send, recv, r):
        home = at.ahead(n_f - r)
        return remote(
            buffer.at[aligned(r, cap_rows), :],
            into.at[aligned(home, cap_rows), :],
            send.at[r],
            recv.at[r],
            at.fsdp_peer(r),
        )

    def e_spread(j):
        for i in range(1, n_x):
            to_x(i, j).wait_recv()
        tile = e_tile(at.core, j)
        own = aligned(at.x, part)
        total = ew[tile, own, :].astype(F32)
        for i in range(1, n_x):
            total = total + ew_x[i - 1, j].astype(F32)
        ew[tile, own, :] = total.astype(BF16)
        for i in range(1, n_x):
            all_x(i, j).start()
        to_core(0, j, at.core).start()
        to_self(0, j).start()

    def e_forward(j):
        for i in range(1, n_x):
            from_x(i, j).wait_recv()
            to_core(i, j, at.core).start()
            to_self(i, j).start()

    loop(0, n_mine - 1, e_spread)
    loop(1, n_f, lambda r: returned(ret_d, table_d, s_d, r_d, r).wait_recv())

    loop(1, n_f, lambda k: send_rows(send_g, g_in, s_g, r_g, k).wait_send())
    d_mixed = send_g

    table_iota = lax.broadcasted_iota(jnp.int32, (ROWBLK, n_f * cap_rows), 1).astype(F32)

    def gather_rows(block):
        hit = (table_iota == place[block, 0:1]) | (table_iota == place[block, 1:2])
        return jnp.where(hit, 1.0, 0.0).astype(BF16)

    def norm_back(grad, value, inv_std, gain):
        scaled = grad * gain
        return inv_std * (
            scaled
            - jnp.mean(scaled, axis=-1, keepdims=True)
            - value * jnp.mean(scaled * value, axis=-1, keepdims=True)
        )

    def second_back(i):
        block = aligned(i, ROWBLK)
        grad = nn(gather_rows(block), table_d[...])
        value, inv_std = normalize(middle[block, :])
        pack[5:6, :] += jnp.sum(grad * value, axis=0, keepdims=True)
        pack[6:7, :] += jnp.sum(grad, axis=0, keepdims=True)
        total = cot[block, :].astype(F32) + norm_back(grad, value, inv_std, vecs[5:6, :])
        d_middle[block, :] = total
        low = total.astype(BF16)
        routed[block, :] = low
        pack[4:5, :] += jnp.sum(low.astype(F32), axis=0, keepdims=True)
        d_mixed[block, :] = nt(low, wfull[:, 3 * WIDTH : 4 * WIDTH]).astype(BF16)

    loop(0, SLOTS // ROWBLK, second_back)

    units = 16 // n_d
    pairs_in_unit = PAIRS // units

    y_rows = n_z * shard

    def dense(tile):
        return hidden.at[WIDTH * 2 : WIDTH * 3, aligned(tile, TILE)]

    def put_dense(tile, value):
        value = value.astype(BF16)
        for z in range(n_z):
            for y in range(n_y):
                low = (z * n_y + y) * shard
                row = WIDTH * 2 + (y * n_z + z) * shard
                hidden[row : row + shard, aligned(tile, TILE)] = value[low : low + shard, :]

    def y_block(tile, y):
        rows = pl.ds(pl.multiple_of(WIDTH * 2 + y * y_rows, shard), y_rows)
        return hidden.at[rows, aligned(tile, TILE)]

    def z_piece(tile, z):
        rows = pl.ds(pl.multiple_of(WIDTH * 2 + (my_y * n_z + z) * shard, shard), shard)
        return hidden.at[rows, aligned(tile, TILE)]

    def own_tile(u, x):
        return u * n_d + x * 2 + at.core

    def g_core(u, x):
        src = dense(u * n_d + x * 2 + other)
        return remote(src, dense_core.at[u, x], s_gc.at[u, x], r_gc.at[u, x], at.partner())

    def g_y(u, x, j):
        src = y_block(own_tile(u, x), lax.rem(my_y + j, n_y))
        sems = s_gy.at[u, x, j - 1], r_gy.at[u, x, j - 1]
        return remote(src, dense_y.at[u, x, j - 1], *sems, (at.d, member(0, j)))

    def g_z(u, x, i):
        src = z_piece(own_tile(u, x), lax.rem(my_z + i, n_z))
        sems = s_gz.at[u, x, i], r_gz.at[u, x, i]
        return remote(src, dense_z.at[u, x, i], *sems, (at.d, member(i, 0)))

    def g_x(u, i):
        sems = s_gx.at[u, i - 1], r_gx.at[u, i - 1]
        return remote(dense_s.at[u], dense_x.at[u, i - 1], *sems, at.x_peer(i))

    def g_d(u, core):
        src = final.at[u, core]
        return remote(src, src, s_gd.at[u], r_gd.at[u], at.partner())

    def first_hop(u):
        for x in range(n_x):
            g_core(u, x).start()

    def second_hop(u):
        for x in range(n_x):
            g_core(u, x).wait_recv()
            tile = dense(own_tile(u, x))
            tile[...] = (tile[...].astype(F32) + dense_core[u, x].astype(F32)).astype(BF16)
            for j in range(1, n_y):
                g_y(u, x, j).start()

    def third_hop(u):
        for x in range(n_x):
            mine = y_block(own_tile(u, x), my_y)
            total = mine[...].astype(F32)
            for j in range(1, n_y):
                g_y(u, x, j).wait_recv()
                total = total + dense_y[u, x, j - 1].astype(F32)
            mine[...] = total.astype(BF16)
            for i in range(1, n_z):
                g_z(u, x, i).start()

    def fourth_hop(u):
        for x in range(n_x):
            total = z_piece(own_tile(u, x), my_z)[...].astype(F32)
            for i in range(1, n_z):
                g_z(u, x, i).wait_recv()
                total = total + dense_z[u, x, i].astype(F32)
            dense_s[u, x] = total.astype(BF16)
        for i in range(1, n_x):
            g_x(u, i).start()

    def fifth_hop(u):
        total = dense_s[u].astype(F32)
        for i in range(1, n_x):
            g_x(u, i).wait_recv()
            total = total + dense_x[u, i - 1].astype(F32)
        final[u, at.core] = total.astype(BF16)
        g_d(u, at.core).start()

    hops = (first_hop, second_hop, third_hop, fourth_hop, fifth_hop)

    d_wo = tn(mixed[...], routed[...])
    for pair in range(PAIRS):
        put_dense(4 * pair + 3, d_wo[:, pair * TILE : (pair + 1) * TILE])

    def attend_back(pair):
        for b, (low, high, row) in enumerate(WINDOWS):
            window = slice(row, row + high - low)
            grad = d_mixed[b * QBLK : (b + 1) * QBLK, aligned(pair, TILE)]
            values = qkv[2 * PAIRS + pair, low:high, :]
            for h in range(2):
                one = jnp.where(halves[h], grad, jnp.zeros_like(grad))
                scores[h, window, :] = nt(values, one)
        for b, (low, high, row) in enumerate(WINDOWS):
            window = slice(row, row + high - low)
            for h in range(2):
                share = probs[2 * pair + h, window, :].astype(F32)
                moved = share * scores[h, window, :]
                moved = moved - share * jnp.sum(moved, axis=0, keepdims=True)
                d_pre[window, h * 256 : h * 256 + QBLK] = moved.astype(BF16)
        for array in (acc_k, acc_v):
            array[...] = jnp.zeros_like(array)
        for b, (low, high, row) in enumerate(WINDOWS):
            window = slice(row, row + high - low)
            block = slice(b * QBLK, (b + 1) * QBLK)
            keys = qkv[PAIRS + pair, low:high, :]
            query = qkv[pair, block, :]
            grad = d_mixed[block, aligned(pair, TILE)]
            both = [
                [
                    tn(d_pre[window, h * 256 : h * 256 + QBLK], keys),
                    nn(d_pre[window, h * 256 : h * 256 + QBLK], query),
                    nn(probs[2 * pair + h, window, :], grad),
                ]
                for h in range(2)
            ]
            d_q, d_k, d_v = [jnp.where(halves[0], one, two) for one, two in zip(*both)]
            hidden[block, pl.ds(pl.multiple_of(pair * 384, 128), 128)] = (d_q * 0.125).astype(BF16)
            acc_k[low:high, :] += d_k
            acc_v[low:high, :] += d_v
        hidden[0:SLOTS, pl.ds(pl.multiple_of(pair * 384 + 128, 128), 128)] = acc_k[...].astype(BF16)
        hidden[0:SLOTS, pl.ds(pl.multiple_of(pair * 384 + 256, 128), 128)] = acc_v[...].astype(BF16)
        d_qkv = hidden[0:SLOTS, pl.ds(pl.multiple_of(pair * 384, 128), 384)]
        sums = jnp.sum(d_qkv.astype(F32), axis=0, keepdims=True)
        pack[2:3, aligned(pair, TILE)] = sums[:, 0:128]
        pack[3:4, aligned(pair, TILE)] = sums[:, 256:384]
        d_w = tn(normed[...], d_qkv)
        for c in range(3):
            put_dense(4 * pair + c, d_w[:, c * TILE : (c + 1) * TILE])

        @pl.when(lax.rem(pair, pairs_in_unit) == pairs_in_unit - 1)
        def _():
            unit = lax.div(pair, pairs_in_unit)
            for age, hop in enumerate(hops):

                @pl.when(unit >= age)
                def _(age=age, hop=hop):
                    hop(unit - age)

        @pl.when(pair == 0)
        def _():
            loop(3, LOTS, send_lot)


    acc_k, acc_v = bias.at[0:SLOTS, 0:TILE], bias.at[0:SLOTS, TILE : 2 * TILE]
    loop(0, PAIRS, attend_back)

    def later(step):
        for age, hop in enumerate(hops):
            if 0 <= step - age < units:
                hop(step - age)


    def first_back(i):
        block = aligned(i, ROWBLK)
        grad = nt(hidden[block, 0 : 3 * WIDTH], wfull[:, 0 : 3 * WIDTH])
        value, inv_std = normalize(tok[block, :].astype(F32))
        pack[0:1, :] += jnp.sum(grad * value, axis=0, keepdims=True)
        pack[1:2, :] += jnp.sum(grad, axis=0, keepdims=True)
        d_middle[block, :] += norm_back(grad, value, inv_std, vecs[0:1, :])

    loop(0, SLOTS // ROWBLK, first_back)
    later(units)
    save_tokens = pltpu.make_async_copy(d_middle.at[0:SLOTS, :], o_tokens, s_own.at[2 + n_mine])
    save_tokens.start()

    def p_dp(i):
        return remote(pack, pack_dp.at[i], s_p.at[i], r_p.at[i], at.dp_peer(i))

    for i in range(1, n_d):
        p_dp(i).start()
    later(units + 1)
    e_spread(n_mine - 1)
    loop(0, n_mine - 1, e_forward)

    def vec_lane(owner):
        return aligned(lax.div(owner * shard, TILE), TILE)

    def qv_lane(owner):
        return aligned(lax.div(lax.rem(owner * 2 * shard, WIDTH), TILE), TILE)

    def p_vec(k):
        src = pack_dp.at[0, 0:bias_at, vec_lane(at.ahead(k))]
        return remote(src, vec_f.at[k], s_vf.at[k], r_vf.at[k], at.fsdp_peer(k))

    def p_qv(k):
        src = pack_dp.at[0, 0:8, qv_lane(at.ahead(k))]
        return remote(src, qv_f.at[k], s_qf.at[k], r_qf.at[k], at.fsdp_peer(k))

    pack_dp[0] = pack[...]
    for i in range(1, n_d):
        p_dp(i).wait_recv()
        pack_dp[0] += pack_dp[i]
    loop(1, n_f, lambda k: [p_vec(k).start(), p_qv(k).start()])
    save_bias = pltpu.make_async_copy(
        pack_dp.at[0, bias_at : bias_at + 8, :], o_bias, s_own.at[3 + n_mine]
    )
    save_bias.start()
    later(units + 2)
    e_forward(n_mine - 1)

    loop(1, n_f, lambda r: returned(ret_o, table_o, s_o, r_o, r).wait_recv())

    def combine(i):
        block = aligned(i, ROWBLK)
        total = middle[block, :] + nn(gather_rows(block), table_o[...])
        routed[block, :] = total.astype(BF16)

    loop(0, SLOTS // ROWBLK, combine)
    save_out = pltpu.make_async_copy(routed, o_out, s_own.at[4 + n_mine])
    save_out.start()
    later(units + 3)

    loop(1, n_f, lambda k: [p_vec(k).wait_recv(), p_qv(k).wait_recv()])
    vec_f[0] = pack_dp[0, 0:bias_at, vec_lane(at.me)]
    qv_f[0] = pack_dp[0, 0:8, qv_lane(at.me)]

    def add_lanes(k):
        vec_f[0] += vec_f[k]
        qv_f[0] += qv_f[k]

    loop(1, n_f, add_lanes)
    save_vec = pltpu.make_async_copy(vec_f.at[0], o_vec, s_own.at[5 + n_mine])
    save_qv = pltpu.make_async_copy(qv_f.at[0], o_qv, s_own.at[6 + n_mine])
    save_vec.start()
    save_qv.start()
    loop(0, units, lambda u: g_d(u, other).wait_recv())
    save_dense = pltpu.make_async_copy(final, o_dense, s_own.at[7 + n_mine])
    save_dense.start()

    def ended_f(k):
        send_v(k).wait_send()
        got_w(k).wait_send()
        for i in range(1, n_x):
            share_x(i, k).wait_send()
        for i in range(n_x):
            share_core(i, k).wait_send()
        give_back(ret_d, table_d, s_d, r_d, k).wait_send()
        give_back(ret_o, table_o, s_o, r_o, k).wait_send()
        p_vec(k).wait_send()
        p_qv(k).wait_send()

    loop(1, n_f, ended_f)

    def ended_e(j):
        to_partner(j).wait_send()
        for i in range(1, n_x):
            to_x(i, j).wait_send()
            all_x(i, j).wait_send()
        for i in range(n_x):
            to_core(i, j, at.core).wait_send()
            to_core(i, j, other).wait_recv()
            to_self(i, j).wait()

    loop(0, n_mine, ended_e)

    def ended_u(u):
        for x in range(n_x):
            g_core(u, x).wait_send()
            for j in range(1, n_y):
                g_y(u, x, j).wait_send()
            for i in range(1, n_z):
                g_z(u, x, i).wait_send()
        for i in range(1, n_x):
            g_x(u, i).wait_send()
        g_d(u, at.core).wait_send()

    loop(0, units, ended_u)
    for i in range(1, n_d):
        p_dp(i).wait_send()
    for copy in (save_tokens, save_bias, save_out, save_vec, save_qv, save_dense):
        copy.wait()


def block(n_f, n_d, experts, cap, cap_rows, small, w_in, w_out, b_in, b_out):
    vmem = pl.BlockSpec(memory_space=pltpu.VMEM)
    hbm = pl.BlockSpec(memory_space=pl.ANY)
    n_x = n_d // 2
    more_x = max(n_x - 1, 1)
    vec_rows = -(-(8 + experts) // 16) * 16
    shard = WIDTH // n_f
    table = n_f * cap_rows
    hid = w_in.shape[1]
    units = 16 // n_d
    n_mine = hid // FTILE
    n_y = y_members(n_f)
    more_y = max(n_y - 1, 1)
    pack_rows = 8 + experts + 8
    sds = jax.ShapeDtypeStruct
    vm = pltpu.VMEM
    dma = pltpu.SemaphoreType.DMA
    chunk_rows = table // CHUNKS
    pairs_of = lambda *shape: [dma(shape), dma(shape)]
    return pl.pallas_call(
        functools.partial(block_kernel, n_f, n_d, experts, cap, cap_rows),
        out_shape=(
            sds((SLOTS, WIDTH), BF16),
            sds((SLOTS, WIDTH), F32),
            sds((2 * n_mine, FTILE, WIDTH), BF16),
            sds((units, 2, n_x, shard, TILE), BF16),
            sds((8 + experts, TILE), F32),
            sds((8, TILE), F32),
            sds((8, WIDTH), F32),
        ),
        in_specs=[hbm] * 2 + [vmem] * (len(small) - 2) + [hbm] * 2 + [vmem] * 2,
        out_specs=[hbm] * 7,
        scratch_shapes=[
            vm((SLOTS, WIDTH), BF16),
            vm((SLOTS, WIDTH), BF16),
            vm((WIDTH, 4 * WIDTH), BF16),
            vm((vec_rows, WIDTH), BF16),
            vm((vec_rows, WIDTH), F32),
            vm((KEYS, 2 * TILE), F32),
            vm((2, KEYS, QBLK), F32),
            vm((2 * PAIRS, KEYS, QBLK), BF16),
            vm((3 * PAIRS, SLOTS, TILE), BF16),
            vm((SLOTS, WIDTH), BF16),
            vm((SLOTS, WIDTH), BF16),
            vm((SLOTS, WIDTH), F32),
            vm((SLOTS, WIDTH), BF16),
            vm((SLOTS, 8), F32),
        ]
        + [vm((table, WIDTH), BF16)] * 4
        + [
            vm((WIDTH, hid), BF16),
            vm((hid, WIDTH), BF16),
            vm((table, hid), BF16),
            vm((table, hid), BF16),
        ]
        + [vm((table, WIDTH), BF16)] * 3
        + [
            vm((2 * n_mine, FTILE, WIDTH), BF16),
            vm((n_mine, FTILE, WIDTH), BF16),
            vm((more_x, n_mine, FTILE // n_x, WIDTH), BF16),
            vm((units, n_x, WIDTH, TILE), BF16),
            vm((units, n_x, more_y, n_f // n_y * shard, TILE), BF16),
            vm((units, n_x, n_f // n_y, shard, TILE), BF16),
            vm((units, n_x, shard, TILE), BF16),
            vm((units, more_x, n_x, shard, TILE), BF16),
            vm((units, 2, n_x, shard, TILE), BF16),
            vm((pack_rows, WIDTH), F32),
            vm((n_d, pack_rows, WIDTH), F32),
            vm((n_f, 8 + experts, TILE), F32),
            vm((n_f, 8, TILE), F32),
            vm((max(2 * chunk_rows, SLOTS), WIDTH), F32),
        ]
        + pairs_of(n_f)
        + pairs_of(n_f)
        + pairs_of(more_x, n_f)
        + pairs_of(n_x, n_f)
        + pairs_of(n_f)
        + pairs_of(n_f)
        + pairs_of(n_f)
        + pairs_of(n_f)
        + pairs_of(n_mine)
        + pairs_of(more_x, n_mine)
        + pairs_of(more_x, n_mine)
        + pairs_of(n_x, n_mine)
        + pairs_of(units, n_x)
        + pairs_of(units, n_x, more_y)
        + pairs_of(units, n_x, n_f // n_y)
        + pairs_of(units, more_x)
        + pairs_of(units)
        + pairs_of(n_d)
        + pairs_of(n_f)
        + pairs_of(n_f)
        + [dma((8 + n_mine,)), dma((n_x, n_mine)), pltpu.SemaphoreType.REGULAR],
        compiler_params=pltpu.CompilerParams(
            collective_id=0, has_side_effects=True, vmem_limit_bytes=63 << 20
        ),
        name="block",
    )(*small, w_in, w_out, b_in, b_out)


def finish_kernel(
    n_f,
    experts,
    in_out,
    in_tokens,
    in_expert,
    dense,
    vec,
    qv,
    biases,
    o_out,
    o_tokens,
    o_g1,
    o_s1,
    o_qkv,
    o_bqv,
    o_wo,
    o_bo,
    o_g2,
    o_s2,
    o_router,
    o_w_in,
    o_b_in,
    o_w_out,
    o_b_out,
    low,
    wide,
    rows_low,
    rows_wide,
    s_load,
    s_save,
):
    me = lax.axis_index("fsdp")
    shard = WIDTH // n_f
    tiles = in_expert.shape[0]
    loads = [pltpu.make_async_copy(in_expert.at[t], low.at[t], s_load.at[t]) for t in range(tiles)]
    for load in loads:
        load.start()
    rows_in = [
        pltpu.make_async_copy(in_out, rows_low, s_load.at[tiles]),
        pltpu.make_async_copy(in_tokens, rows_wide, s_load.at[tiles + 1]),
    ]
    for load in rows_in:
        load.start()

    def my_lanes(value, size):
        place = lax.rem(me * size, TILE)
        total = jnp.zeros((value.shape[0], size), F32)
        for low_lane in range(0, TILE, size):
            total = total + jnp.where(place == low_lane, value[:, low_lane : low_lane + size], 0.0)
        return total

    own = my_lanes(vec[...], shard)
    for row, ref in ((0, o_g1), (1, o_s1), (4, o_bo), (5, o_g2), (6, o_s2)):
        ref[...] = own[row : row + 1, :]
    o_router[...] = own[8 : 8 + experts, :]
    lines = my_lanes(qv[...], 2 * shard)
    o_bqv[...] = jnp.where(me * 2 * shard < WIDTH, lines[2:3, :], lines[3:4, :])
    n_d = 2 * dense.shape[2]

    def tile(t):
        return dense[t // n_d, t % 2, t % n_d // 2].astype(F32)

    for pair in range(PAIRS):
        for c in range(3):
            at = c * WIDTH + pair * TILE
            o_qkv[:, at : at + TILE] = tile(4 * pair + c)
        o_wo[:, pair * TILE : (pair + 1) * TILE] = tile(4 * pair + 3)
    for f in range(tiles // 2):
        o_b_in[:, f * FTILE : (f + 1) * FTILE] = biases[f : f + 1, :]
    o_b_out[...] = biases[4:5, :]
    saves = []
    for t in range(tiles):
        loads[t].wait()
        wide[t] = low[t].astype(F32)
        piece = pl.ds(t // 2 * FTILE, FTILE)
        dst = o_w_out.at[0, piece, :] if t % 2 else o_w_in.at[0, :, piece]
        saves.append(pltpu.make_async_copy(wide.at[t], dst, s_save.at[t]))
        saves[-1].start()
    rows_out = [
        pltpu.make_async_copy(rows_low, o_out, s_save.at[tiles]),
        pltpu.make_async_copy(rows_wide, o_tokens, s_save.at[tiles + 1]),
    ]
    for load, save in zip(rows_in, rows_out):
        load.wait()
        save.start()
    for save in saves + rows_out:
        save.wait()


def finish(n_f, experts, hid, parts):
    vmem = pl.BlockSpec(memory_space=pltpu.VMEM)
    hbm = pl.BlockSpec(memory_space=pl.ANY)
    shard = WIDTH // n_f
    tiles = parts[2].shape[0]
    line = lambda *shape: jax.ShapeDtypeStruct(shape, F32)
    return pl.pallas_call(
        functools.partial(finish_kernel, n_f, experts),
        out_shape=(
            jax.ShapeDtypeStruct((SLOTS, WIDTH), BF16),
            line(SLOTS, WIDTH),
            line(1, shard),
            line(1, shard),
            line(shard, 3 * WIDTH),
            line(1, 2 * shard),
            line(shard, WIDTH),
            line(1, shard),
            line(1, shard),
            line(1, shard),
            line(experts, shard),
            line(1, WIDTH, hid),
            line(1, hid),
            line(1, hid, WIDTH),
            line(1, WIDTH),
        ),
        in_specs=[hbm] * 3 + [vmem] * 4,
        out_specs=[hbm] * 2 + [vmem] * 9 + [hbm, vmem, hbm, vmem],
        scratch_shapes=[
            pltpu.VMEM((tiles, FTILE, WIDTH), BF16),
            pltpu.VMEM((tiles, FTILE, WIDTH), F32),
            pltpu.VMEM((SLOTS, WIDTH), BF16),
            pltpu.VMEM((SLOTS, WIDTH), F32),
            pltpu.SemaphoreType.DMA((tiles + 2,)),
            pltpu.SemaphoreType.DMA((tiles + 2,)),
        ],
        compiler_params=pltpu.CompilerParams(vmem_limit_bytes=62 << 20),
        name="finish",
    )(*parts)


def shards(
    tokens,
    cotangent,
    segment_ids,
    pad_mask,
    expert_ids,
    priority,
    ln1_gain,
    ln1_shift,
    w_qkv,
    b_qv,
    w_o,
    b_o,
    ln2_gain,
    ln2_shift,
    w_router,
    w_in,
    b_in,
    w_out,
    b_out,
    n_f,
    n_d,
):
    experts = w_router.shape[1]
    cap = (21 * tokens.shape[0] + 10 * experts - 1) // (10 * experts)
    cap_rows = -(-cap // 16) * 16
    line = lambda vector: vector.reshape(1, -1)
    small = (
        tokens,
        cotangent,
        segment_ids,
        pad_mask,
        expert_ids.T,
        priority,
        w_qkv,
        w_o,
        line(ln1_gain),
        line(ln1_shift),
        line(b_qv),
        line(b_o),
        line(ln2_gain),
        line(ln2_shift),
        w_router.T,
    )
    parts = block(n_f, n_d, experts, cap, cap_rows, small, w_in[0], w_out[0], b_in, b_out)
    done = finish(n_f, experts, w_in.shape[2], parts)
    flat = (2, 3, 5, 7, 8, 9)
    done = [value.reshape(-1) if i in flat else value for i, value in enumerate(done)]
    done[10] = done[10].T
    return tuple(done)


def solution(mesh):
    both, one = P(("dp", "fsdp")), P("fsdp")
    n_f, n_d = mesh.shape["fsdp"], mesh.shape["dp"]
    return jax.shard_map(
        functools.partial(shards, n_f=n_f, n_d=n_d),
        mesh=mesh,
        in_specs=(both,) * 6 + (one,) * 13,
        out_specs=(both,) * 2 + (one,) * 13,
        check_vma=False,
    )
```

```python
import functools

import jax
import jax.numpy as jnp
from jax import lax
from jax.experimental import pallas as pl
from jax.experimental.pallas import tpu as pltpu
from jax.sharding import PartitionSpec as P

MESH = pl.DeviceIdType.MESH
BF16 = jnp.bfloat16
F32 = jnp.float32
SLOTS = 720
WIDTH = 512
PAIRS = 4
EPS = 1e-06
WINDOWS = ((0, 384, 0), (96, 624, 384), (336, 720, 912))
KEYS = 1296
QBLK = 240
ROWBLK = 240
TILE = 128
FTILE = 512
CHUNKS = 4
LOTS = 7


def nt(left, right):
    return lax.dot_general(left, right, (((1,), (1,)), ((), ())), preferred_element_type=F32)


def tn(left, right):
    return lax.dot_general(left, right, (((0,), (0,)), ((), ())), preferred_element_type=F32)


def nn(left, right):
    return jnp.dot(left, right, preferred_element_type=F32)


def normalize(value):
    centred = value - jnp.mean(value, axis=-1, keepdims=True)
    inv_std = lax.rsqrt(jnp.mean(centred * centred, axis=-1, keepdims=True) + EPS)
    return centred * inv_std, inv_std


def aligned(index, size):
    return pl.ds(pl.multiple_of(index * size, size), size)


class Place:
    def __init__(self, n_f, n_d):
        self.n_f, self.n_d, self.n_x = n_f, n_d, n_d // 2
        self.me = lax.axis_index("fsdp")
        self.d = lax.axis_index("dp")
        self.x = lax.div(self.d, 2)
        self.core = lax.rem(self.d, 2)

    def ahead(self, k):
        return lax.rem(self.me + k, self.n_f)

    def fsdp_peer(self, k):
        return (self.d, self.ahead(k))

    def x_index(self, i):
        return lax.rem(self.x + i, self.n_x)

    def x_peer(self, i):
        return (self.x_index(i) * 2 + self.core, self.me)

    def partner(self):
        return (self.x * 2 + 1 - self.core, self.me)

    def dp_peer(self, i):
        return (lax.rem(self.d + i, self.n_d), self.me)

    def enter(self):
        bar = pltpu.get_barrier_semaphore()

        def greet(k, _):
            pl.semaphore_signal(bar, inc=1, device_id=self.fsdp_peer(k), device_id_type=MESH)
            return 0

        lax.fori_loop(1, self.n_f, greet, 0)
        for i in range(1, self.n_d):
            pl.semaphore_signal(bar, inc=1, device_id=self.dp_peer(i), device_id_type=MESH)
        pl.semaphore_wait(bar, self.n_f - 1 + self.n_d - 1)


def remote(src, dst, send_sem, recv_sem, device):
    return pltpu.make_async_remote_copy(
        src_ref=src,
        dst_ref=dst,
        send_sem=send_sem,
        recv_sem=recv_sem,
        device_id=device,
        device_id_type=MESH,
    )


def loop(low, high, body):
    def step(k, carry):
        body(k)
        return carry

    lax.fori_loop(low, high, step, 0)


def y_members(n_f):
    return 1 << ((n_f.bit_length() - 1) // 2)


def block_kernel(
    n_f,
    n_d,
    experts,
    cap,
    cap_rows,
    tok_hbm,
    cot_hbm,
    segment,
    pad,
    chosen_ids,
    priority,
    w_qkv,
    w_o,
    gain_one,
    shift_one,
    b_qv,
    b_o,
    gain_two,
    shift_two,
    w_router,
    w_in_hbm,
    w_out_hbm,
    b_in,
    b_out,
    o_out,
    o_tokens,
    o_expert,
    o_dense,
    o_vec,
    o_qv,
    o_bias,
    tok,
    cot,
    wfull,
    vsh,
    vecs,
    bias,
    scores,
    probs,
    qkv,
    normed,
    mixed,
    middle,
    routed,
    place,
    send_x,
    send_g,
    x_in,
    g_in,
    w_in,
    w_out,
    hidden,
    d_pre,
    ret_d,
    ret_o,
    table_d,
    ew,
    ew_core,
    ew_x,
    dense_core,
    dense_y,
    dense_z,
    dense_s,
    dense_x,
    final,
    pack,
    pack_dp,
    vec_f,
    qv_f,
    d_middle,
    s_w,
    r_w,
    s_v,
    r_v,
    s_dx,
    r_dx,
    s_dc,
    r_dc,
    s_g,
    r_g,
    s_x,
    r_x,
    s_d,
    r_d,
    s_o,
    r_o,
    s_ec,
    r_ec,
    s_ex,
    r_ex,
    s_ea,
    r_ea,
    s_eb,
    r_eb,
    s_gc,
    r_gc,
    s_gy,
    r_gy,
    s_gz,
    r_gz,
    s_gx,
    r_gx,
    s_gd,
    r_gd,
    s_p,
    r_p,
    s_vf,
    r_vf,
    s_qf,
    r_qf,
    s_own,
    s_self,
    ready,
):
    at = Place(n_f, n_d)
    n_x = at.n_x
    shard = WIDTH // n_f
    colw = 4 * WIDTH // n_d
    other = 1 - at.core

    def cols_of(d):
        return aligned(d, colw)

    def w_piece(owner, d):
        return wfull.at[aligned(owner, shard), cols_of(d)]

    def x_back(i):
        return at.x_index(n_x - i)

    load_in = pltpu.make_async_copy(w_in_hbm, w_in, s_own.at[0])
    load_out = pltpu.make_async_copy(w_out_hbm, w_out, s_own.at[1])
    load_tok = pltpu.make_async_copy(tok_hbm, tok, s_own.at[2])
    load_cot = pltpu.make_async_copy(cot_hbm, cot, s_own.at[3])
    for load in (load_cot, load_tok, load_in, load_out):
        load.start()
    at.enter()

    n_y = y_members(n_f)
    n_z = n_f // n_y
    my_z, my_y = lax.div(at.me, n_y), lax.rem(at.me, n_y)

    def member(z, y):
        return lax.rem(my_z + z, n_z) * n_y + lax.rem(my_y + y, n_y)

    def owner(k):
        return member(n_z - lax.rem(k, n_z), n_y - lax.div(k, n_z))

    def along_z(k):
        piece = w_piece(at.me, at.d)
        return remote(piece, piece, s_w.at[k], r_w.at[k], (at.d, member(k, 0)))

    def along_y(j, i):
        piece, k = w_piece(member(n_z - i, 0), at.d), j * n_z + i
        return remote(piece, piece, s_w.at[k], r_w.at[k], (at.d, member(0, j)))

    def got_w(k):
        piece = w_piece(owner(k), at.d)
        return remote(piece, piece, s_w.at[k], r_w.at[k], (at.d, at.me))

    vec_rows = vsh.shape[0]

    def vec_piece(owner):
        return hidden.at[aligned(owner, vec_rows), 0:WIDTH]

    def send_v(k):
        return remote(vsh, vec_piece(at.me), s_v.at[k], r_v.at[k], at.fsdp_peer(k))

    def share_x(i, k):
        piece = w_piece(owner(k), at.d)
        return remote(piece, piece, s_dx.at[i - 1, k], r_dx.at[i - 1, k], at.x_peer(i))

    def share_core(i, k):
        piece = w_piece(owner(k), x_back(i) * 2 + at.core)
        return remote(piece, piece, s_dc.at[i, k], r_dc.at[i, k], at.partner())

    own = aligned(at.me, shard)
    for pair in range(PAIRS):
        for c in range(3):
            low = (3 * pair + c) * TILE
            src = c * WIDTH + pair * TILE
            wfull[own, low : low + TILE] = w_qkv[:, src : src + TILE]
    wfull[own, 3 * WIDTH : 4 * WIDTH] = w_o[...]
    loop(1, n_z, lambda k: along_z(k).start())
    loop(1, n_y, lambda j: along_y(j, 0).start())

    def placing(size, low):
        shape = (size, WIDTH)
        target = lax.broadcasted_iota(jnp.int32, shape, 1) + low
        source = lax.broadcasted_iota(jnp.int32, shape, 0) + at.me * size
        return jnp.where(target == source, 1.0, 0.0).astype(BF16)

    blank = jnp.zeros((1, shard), F32)
    stack = [
        blank if ref is None else ref[...].astype(F32)
        for ref in (gain_one, shift_one, None, None, b_o, gain_two, shift_two, None)
    ]
    spread = nn(jnp.concatenate(stack, axis=0).astype(BF16), placing(shard, 0))
    row_iota = lax.broadcasted_iota(jnp.int32, (8, WIDTH), 0)
    for r in range(2):
        line = nn(b_qv[...], placing(2 * shard, r * WIDTH))
        spread = spread + jnp.where(row_iota == 2 + r, line, 0.0)
    router_rows = nn(w_router[...], placing(shard, 0))
    rest = jnp.zeros((vec_rows - 8 - experts, WIDTH), F32)
    parts = [spread, router_rows] + ([rest] if vec_rows > 8 + experts else [])
    vsh[...] = jnp.concatenate(parts, axis=0).astype(BF16)
    vec_piece(at.me)[...] = vsh[...]
    loop(1, n_f, lambda k: send_v(k).start())

    seg_r, pad_r, pri_r = (
        ref[...].reshape(1, SLOTS).astype(F32) for ref in (segment, pad, priority)
    )
    lines = jnp.concatenate([seg_r, pad_r, pri_r, jnp.zeros((5, SLOTS), F32)], axis=0)
    columns = jnp.transpose(lines)
    seg_c, pad_c, pri_c = (columns[:, j : j + 1] for j in range(3))
    expert_iota = lax.broadcasted_iota(jnp.int32, (experts, SLOTS), 0)
    live = pad_r > 0
    before = jnp.where(pri_c < pri_r, 1.0, 0.0).astype(BF16)
    chose = [jnp.where((chosen_ids[k : k + 1, :] == expert_iota) & live, 1.0, 0.0) for k in range(2)]
    rank = [nn(one.astype(BF16), before) for one in chose]
    rank[1] = rank[1] + jnp.sum(chose[0], axis=1, keepdims=True)
    spot_r = []
    for k in range(2):
        slot = jnp.sum(chose[k] * rank[k], axis=0, keepdims=True)
        spot = chosen_ids[k : k + 1, :].astype(F32) * cap_rows + slot
        spot_r.append(jnp.where(live & (slot < cap), spot, -1.0))
    place[...] = jnp.transpose(jnp.concatenate(spot_r + [jnp.zeros((6, SLOTS), F32)], axis=0))
    slot_iota = lax.broadcasted_iota(jnp.int32, (cap_rows, SLOTS), 0)

    def pick(expert):
        mine = (slot_iota + expert * cap_rows).astype(F32)
        return jnp.where((mine == spot_r[0]) | (mine == spot_r[1]), 1.0, 0.0).astype(BF16)

    for b, (low, high, row) in enumerate(WINDOWS):
        queries = slice(b * QBLK, (b + 1) * QBLK)
        shape = (high - low, QBLK)
        same = seg_c[low:high, :] == seg_r[:, queries]
        itself = (lax.broadcasted_iota(jnp.int32, shape, 0) + low) == (
            lax.broadcasted_iota(jnp.int32, shape, 1) + b * QBLK
        )
        allowed = same & ((pad_c[low:high, :] > 0) | itself)
        bias[row : row + high - low, 0:QBLK] = jnp.where(allowed, 0.0, -1e30)

    chunk_rows = n_f * cap_rows // CHUNKS
    sources = n_f // CHUNKS

    def position(step, side):
        inner = lax.rem(lax.div(step + 1, 2), 2)
        near = 1 + 2 * lax.rem(step + 1 + side, 2)
        return inner * near + (1 - inner) * 2 * lax.div(step, 3)

    z_side = lax.rem(my_z, 2)

    def send_rows(buffer, into, send, recv, k):
        return remote(
            buffer.at[aligned(at.ahead(k), cap_rows), :],
            into.at[aligned(n_f - k, cap_rows), :],
            send.at[k],
            recv.at[n_f - k],
            at.fsdp_peer(k),
        )

    def dispatch(source, buffer, into, send, recv):
        into[0:cap_rows, :] = nn(pick(at.me), source[...]).astype(BF16)

        def stage(step):
            first = position(step, 1 - z_side) * sources

            def one(r):
                @pl.when(r > 0)
                def _():
                    k = n_f - r
                    expert = at.ahead(k)
                    rows = nn(pick(expert), source[...]).astype(BF16)
                    buffer[aligned(expert, cap_rows), :] = rows
                    send_rows(buffer, into, send, recv, k).start()

            loop(first, first + sources, one)

        loop(0, CHUNKS, stage)

    def pass_on(k):
        for i in range(1, n_x):
            share_x(i, k).start()
        share_core(0, k).start()

    def from_z(k):
        got_w(k).wait_recv()
        loop(1, n_y, lambda j: along_y(j, k).start())
        pass_on(k)

    def from_y(k):
        got_w(k).wait_recv()
        pass_on(k)

    loop(1, n_z, from_z)
    load_cot.wait()
    dispatch(cot, send_g, g_in, s_g, r_g)
    loop(n_z, n_f, from_y)

    loop(1, n_f, lambda k: send_v(k).wait_recv())
    vecs[...] = vec_piece(0)[...].astype(F32)

    def add_vectors(owner):
        vecs[...] += vec_piece(owner)[...].astype(F32)

    loop(1, n_f, add_vectors)

    load_tok.wait()

    def first_norm(i):
        block = aligned(i, ROWBLK)
        value, _ = normalize(tok[block, :].astype(F32))
        normed[block, :] = (value * vecs[0:1, :] + vecs[1:2, :]).astype(BF16)

    loop(0, SLOTS // ROWBLK, first_norm)

    for i in range(1, n_x):

        def cross(k, i=i):
            piece = w_piece(owner(k), x_back(i) * 2 + at.core)
            remote(piece, piece, s_dx.at[i - 1, k], r_dx.at[i - 1, k], at.x_peer(i)).wait_recv()
            share_core(i, k).start()

        loop(1, n_f, cross)
    for i in range(n_x):

        def arrive(k, i=i):
            piece = w_piece(owner(k), x_back(i) * 2 + other)
            remote(piece, piece, s_dc.at[i, k], r_dc.at[i, k], at.partner()).wait_recv()

        loop(1, n_f, arrive)

    def project(pair):
        out = nn(normed[...], wfull[:, pl.ds(pl.multiple_of(pair * 384, 128), 384)])
        lanes = aligned(pair, TILE)
        qkv[pair] = ((out[:, 0:128] + vecs[2:3, lanes]) * 0.125).astype(BF16)
        qkv[PAIRS + pair] = out[:, 128:256].astype(BF16)
        qkv[2 * PAIRS + pair] = (out[:, 256:384] + vecs[3:4, lanes]).astype(BF16)

    loop(0, PAIRS, project)

    lane = lax.broadcasted_iota(jnp.int32, (1, TILE), 1)
    halves = (lane < 64, lane >= 64)

    def attend(pair):
        for b, (low, high, row) in enumerate(WINDOWS):
            window = slice(row, row + high - low)
            query = qkv[pair, b * QBLK : (b + 1) * QBLK, :]
            keys = qkv[PAIRS + pair, low:high, :]
            for h in range(2):
                one = jnp.where(halves[h], query, jnp.zeros_like(query))
                scores[h, window, :] = nt(keys, one) + bias[window, 0:QBLK]
        for b, (low, high, row) in enumerate(WINDOWS):
            window = slice(row, row + high - low)
            for h in range(2):
                value = scores[h, window, :]
                power = jnp.exp(value - jnp.max(value, axis=0, keepdims=True))
                share = 1.0 / jnp.sum(power, axis=0, keepdims=True)
                probs[2 * pair + h, window, :] = (power * share).astype(BF16)
        for b, (low, high, row) in enumerate(WINDOWS):
            window = slice(row, row + high - low)
            values = qkv[2 * PAIRS + pair, low:high, :]
            both = [tn(probs[2 * pair + h, window, :], values) for h in range(2)]
            mixed[b * QBLK : (b + 1) * QBLK, aligned(pair, TILE)] = jnp.where(
                halves[0], both[0], both[1]
            ).astype(BF16)

    loop(0, PAIRS, attend)

    def second_norm(i):
        block = aligned(i, ROWBLK)
        total = nn(mixed[block, :], wfull[:, 3 * WIDTH : 4 * WIDTH])
        total = tok[block, :].astype(F32) + total + vecs[4:5, :]
        middle[block, :] = total
        value, _ = normalize(total)
        routed[block, :] = (value * vecs[5:6, :] + vecs[6:7, :]).astype(BF16)

    loop(0, SLOTS // ROWBLK, second_norm)
    dispatch(routed, send_x, x_in, s_x, r_x)

    load_in.wait()
    load_out.wait()
    pack[...] = jnp.zeros_like(pack)

    def clear(t):
        ew[t] = jnp.zeros((FTILE, WIDTH), BF16)

    loop(0, ew.shape[0], clear)
    router = vecs[8 : 8 + experts, :].astype(BF16)
    f_tiles = w_in.shape[1] // FTILE
    bias_at = 8 + experts
    hot = jnp.where(lax.broadcasted_iota(jnp.int32, (1, experts), 1) == at.me, 1.0, 0.0)

    def give_back(buffer, into, send, recv, r):
        return remote(
            buffer.at[aligned(r, cap_rows), :],
            into.at[aligned(at.me, cap_rows), :],
            send.at[r],
            recv.at[r],
            at.fsdp_peer(r),
        )

    acc_o, acc_d = d_middle.at[0:chunk_rows, :], d_middle.at[chunk_rows : 2 * chunk_rows, :]

    def expert_chunk(step):
        pos = position(step, z_side)
        block = aligned(pos, chunk_rows)
        first = pos * sources

        def arrive(r):
            @pl.when(r > 0)
            def _():
                send_rows(send_g, g_in, s_g, r_g, n_f - r).wait_recv()
                send_rows(send_x, x_in, s_x, r_x, n_f - r).wait_recv()

        loop(first, first + sources, arrive)
        x_rows = x_in[block, :]
        logits = nt(x_rows, router)
        gates = jnp.exp(logits - jnp.max(logits, axis=-1, keepdims=True))
        gates = gates / jnp.sum(gates, axis=-1, keepdims=True)
        chosen = jnp.sum(gates * hot, axis=-1, keepdims=True)
        g_rows = (chosen * g_in[block, :].astype(F32)).astype(BF16)
        g_in[block, :] = g_rows
        pack[bias_at + 4 : bias_at + 5, :] += jnp.sum(g_rows.astype(F32), axis=0, keepdims=True)
        acc_o[...] = jnp.broadcast_to(b_out[...].astype(F32), acc_o.shape)
        acc_d[...] = jnp.zeros_like(acc_d)
        def tile(f):
            lanes = aligned(f, FTILE)
            pre = nn(x_in[block, :], w_in[:, lanes]) + b_in[:, lanes].astype(F32)
            d_act = nt(g_in[block, :], w_out[lanes, :])
            cdf = 0.5 + 0.5 * lax.erf(pre * 0.7071067811865476)
            act = (pre * cdf).astype(BF16)
            slope = cdf + pre * jnp.exp(-0.5 * pre * pre) * 0.3989422804014327
            d_row = (d_act * slope).astype(BF16)
            hidden[block, lanes] = act
            d_pre[block, lanes] = d_row
            pack[pl.ds(bias_at + f, 1), :] += jnp.sum(
                d_row.astype(F32), axis=0, keepdims=True
            )
            acc_o[...] += nn(act, w_out[lanes, :])
            acc_d[...] += nt(d_row, w_in[:, lanes])

        loop(0, f_tiles, tile)
        result = acc_o[...]
        weight = jnp.sum(g_in[block, :].astype(F32) * result, axis=-1, keepdims=True)
        d_logits = (weight * (hot - gates)).astype(BF16)
        pack[8:bias_at, :] += tn(d_logits, x_in[block, :])
        ret_d[block, :] = (acc_d[...] + nn(d_logits, router)).astype(BF16)
        ret_o[block, :] = (chosen * result).astype(BF16)

        def back(r):
            @pl.when(r > 0)
            def _():
                give_back(ret_d, table_d, s_d, r_d, r).start()

        loop(first, first + sources, back)

        @pl.when(step < CHUNKS - 1)
        def _():
            loop(0, f_tiles, lambda f: add_tiles(f, block))

    def add_tiles(f, block):
        lanes = aligned(f, FTILE)
        product = tn(x_in[block, :], d_pre[block, lanes])
        ew[2 * f] = (ew[2 * f].astype(F32) + product).astype(BF16)
        product = tn(hidden[block, lanes], g_in[block, :])
        ew[2 * f + 1] = (ew[2 * f + 1].astype(F32) + product).astype(BF16)

    loop(0, CHUNKS, expert_chunk)
    last = pl.ds(2 * chunk_rows, chunk_rows)
    mine = aligned(at.me, cap_rows)
    table_d[mine, :] = ret_d[0:cap_rows, :]

    part = FTILE // n_x
    per_core = f_tiles // 2

    def e_tile(core, j):
        return (core * per_core + j // 2) * 2 + j % 2

    def to_partner(j):
        return remote(ew.at[e_tile(other, j)], ew_core.at[j], s_ec.at[j], r_ec.at[j], at.partner())

    def to_x(i, j):
        src = ew.at[e_tile(at.core, j), aligned(at.x_index(i), part), :]
        return remote(src, ew_x.at[i - 1, j], s_ex.at[i - 1, j], r_ex.at[i - 1, j], at.x_peer(i))

    def e_part(core, j, x):
        return e_tile(core, j), aligned(x, part)

    def all_x(i, j):
        src = ew.at[e_tile(at.core, j), aligned(at.x, part), :]
        dst = ew_core.at[j, aligned(at.x, part), :]
        return remote(src, dst, s_ea.at[i - 1, j], r_ea.at[i - 1, j], at.x_peer(i))

    def from_x(i, j):
        dst = ew_core.at[j, aligned(x_back(i), part), :]
        return remote(dst, dst, s_ea.at[i - 1, j], r_ea.at[i - 1, j], at.x_peer(i))

    def e_result(i, j):
        piece = aligned(x_back(i), part)
        return ew.at[e_tile(at.core, j), piece, :] if i == 0 else ew_core.at[j, piece, :]

    def to_core(i, j, core):
        dst = o_expert.at[e_tile(core, j), aligned(x_back(i), part), :]
        return remote(e_result(i, j), dst, s_eb.at[i, j], r_eb.at[i, j], at.partner())

    def to_self(i, j):
        dst = o_expert.at[e_tile(at.core, j), aligned(x_back(i), part), :]
        return pltpu.make_async_copy(e_result(i, j), dst, s_self.at[i, j])

    n_mine = 2 * per_core

    def theirs(f):
        add_tiles(other * per_core + f, last)
        to_partner(2 * f).start()
        to_partner(2 * f + 1).start()

    def sum_cores(j):
        to_partner(j).wait_recv()
        tile = e_tile(at.core, j)
        ew[tile] = (ew[tile].astype(F32) + ew_core[j].astype(F32)).astype(BF16)
        for i in range(1, n_x):
            to_x(i, j).start()

    def tile_row(f):
        theirs(f)
        add_tiles(at.core * per_core + f, last)
        sum_cores(2 * f)
        sum_cores(2 * f + 1)

    loop(0, per_core, tile_row)

    table_o = send_x

    def left(k):
        send_rows(send_x, x_in, s_x, r_x, k).wait_send()

    loop(1, n_f, left)
    table_o[mine, :] = ret_o[0:cap_rows, :]

    def tell(k):
        pl.semaphore_signal(ready, inc=1, device_id=at.fsdp_peer(k), device_id_type=MESH)

    loop(1, n_f, tell)
    pl.semaphore_wait(ready, n_f - 1)

    def send_lot(lot):
        def one(step):
            r = 1 + lax.rem(1 + step, n_f - 1)
            give_back(ret_o, table_o, s_o, r_o, r).start()

        loop(lax.div((n_f - 1) * lot, LOTS), lax.div((n_f - 1) * (lot + 1), LOTS), one)

    loop(0, 3, send_lot)

    def returned(buffer, into, send, recv, r):
        home = at.ahead(n_f - r)
        return remote(
            buffer.at[aligned(r, cap_rows), :],
            into.at[aligned(home, cap_rows), :],
            send.at[r],
            recv.at[r],
            at.fsdp_peer(r),
        )

    def e_spread(j):
        for i in range(1, n_x):
            to_x(i, j).wait_recv()
        tile = e_tile(at.core, j)
        own = aligned(at.x, part)
        total = ew[tile, own, :].astype(F32)
        for i in range(1, n_x):
            total = total + ew_x[i - 1, j].astype(F32)
        ew[tile, own, :] = total.astype(BF16)
        for i in range(1, n_x):
            all_x(i, j).start()
        to_core(0, j, at.core).start()
        to_self(0, j).start()

    def e_forward(j):
        for i in range(1, n_x):
            from_x(i, j).wait_recv()
            to_core(i, j, at.core).start()
            to_self(i, j).start()

    loop(0, n_mine - 1, e_spread)
    loop(1, n_f, lambda r: returned(ret_d, table_d, s_d, r_d, r).wait_recv())

    loop(1, n_f, lambda k: send_rows(send_g, g_in, s_g, r_g, k).wait_send())
    d_mixed = send_g

    table_iota = lax.broadcasted_iota(jnp.int32, (ROWBLK, n_f * cap_rows), 1).astype(F32)

    def gather_rows(block):
        hit = (table_iota == place[block, 0:1]) | (table_iota == place[block, 1:2])
        return jnp.where(hit, 1.0, 0.0).astype(BF16)

    def norm_back(grad, value, inv_std, gain):
        scaled = grad * gain
        return inv_std * (
            scaled
            - jnp.mean(scaled, axis=-1, keepdims=True)
            - value * jnp.mean(scaled * value, axis=-1, keepdims=True)
        )

    def second_back(i):
        block = aligned(i, ROWBLK)
        grad = nn(gather_rows(block), table_d[...])
        value, inv_std = normalize(middle[block, :])
        pack[5:6, :] += jnp.sum(grad * value, axis=0, keepdims=True)
        pack[6:7, :] += jnp.sum(grad, axis=0, keepdims=True)
        total = cot[block, :].astype(F32) + norm_back(grad, value, inv_std, vecs[5:6, :])
        d_middle[block, :] = total
        low = total.astype(BF16)
        routed[block, :] = low
        pack[4:5, :] += jnp.sum(low.astype(F32), axis=0, keepdims=True)
        d_mixed[block, :] = nt(low, wfull[:, 3 * WIDTH : 4 * WIDTH]).astype(BF16)

    loop(0, SLOTS // ROWBLK, second_back)

    units = 16 // n_d
    pairs_in_unit = PAIRS // units

    y_rows = n_z * shard

    def dense(tile):
        return hidden.at[WIDTH * 2 : WIDTH * 3, aligned(tile, TILE)]

    def put_dense(tile, value):
        value = value.astype(BF16)
        for z in range(n_z):
            for y in range(n_y):
                low = (z * n_y + y) * shard
                row = WIDTH * 2 + (y * n_z + z) * shard
                hidden[row : row + shard, aligned(tile, TILE)] = value[low : low + shard, :]

    def y_block(tile, y):
        rows = pl.ds(pl.multiple_of(WIDTH * 2 + y * y_rows, shard), y_rows)
        return hidden.at[rows, aligned(tile, TILE)]

    def z_piece(tile, z):
        rows = pl.ds(pl.multiple_of(WIDTH * 2 + (my_y * n_z + z) * shard, shard), shard)
        return hidden.at[rows, aligned(tile, TILE)]

    def own_tile(u, x):
        return u * n_d + x * 2 + at.core

    def g_core(u, x):
        src = dense(u * n_d + x * 2 + other)
        return remote(src, dense_core.at[u, x], s_gc.at[u, x], r_gc.at[u, x], at.partner())

    def g_y(u, x, j):
        src = y_block(own_tile(u, x), lax.rem(my_y + j, n_y))
        sems = s_gy.at[u, x, j - 1], r_gy.at[u, x, j - 1]
        return remote(src, dense_y.at[u, x, j - 1], *sems, (at.d, member(0, j)))

    def g_z(u, x, i):
        src = z_piece(own_tile(u, x), lax.rem(my_z + i, n_z))
        sems = s_gz.at[u, x, i], r_gz.at[u, x, i]
        return remote(src, dense_z.at[u, x, i], *sems, (at.d, member(i, 0)))

    def g_x(u, i):
        sems = s_gx.at[u, i - 1], r_gx.at[u, i - 1]
        return remote(dense_s.at[u], dense_x.at[u, i - 1], *sems, at.x_peer(i))

    def g_d(u, core):
        src = final.at[u, core]
        return remote(src, src, s_gd.at[u], r_gd.at[u], at.partner())

    def first_hop(u):
        for x in range(n_x):
            g_core(u, x).start()

    def second_hop(u):
        for x in range(n_x):
            g_core(u, x).wait_recv()
            tile = dense(own_tile(u, x))
            tile[...] = (tile[...].astype(F32) + dense_core[u, x].astype(F32)).astype(BF16)
            for j in range(1, n_y):
                g_y(u, x, j).start()

    def third_hop(u):
        for x in range(n_x):
            mine = y_block(own_tile(u, x), my_y)
            total = mine[...].astype(F32)
            for j in range(1, n_y):
                g_y(u, x, j).wait_recv()
                total = total + dense_y[u, x, j - 1].astype(F32)
            mine[...] = total.astype(BF16)
            for i in range(1, n_z):
                g_z(u, x, i).start()

    def fourth_hop(u):
        for x in range(n_x):
            total = z_piece(own_tile(u, x), my_z)[...].astype(F32)
            for i in range(1, n_z):
                g_z(u, x, i).wait_recv()
                total = total + dense_z[u, x, i].astype(F32)
            dense_s[u, x] = total.astype(BF16)
        for i in range(1, n_x):
            g_x(u, i).start()

    def fifth_hop(u):
        total = dense_s[u].astype(F32)
        for i in range(1, n_x):
            g_x(u, i).wait_recv()
            total = total + dense_x[u, i - 1].astype(F32)
        final[u, at.core] = total.astype(BF16)
        g_d(u, at.core).start()

    hops = (first_hop, second_hop, third_hop, fourth_hop, fifth_hop)

    d_wo = tn(mixed[...], routed[...])
    for pair in range(PAIRS):
        put_dense(4 * pair + 3, d_wo[:, pair * TILE : (pair + 1) * TILE])

    def attend_back(pair):
        for b, (low, high, row) in enumerate(WINDOWS):
            window = slice(row, row + high - low)
            grad = d_mixed[b * QBLK : (b + 1) * QBLK, aligned(pair, TILE)]
            values = qkv[2 * PAIRS + pair, low:high, :]
            for h in range(2):
                one = jnp.where(halves[h], grad, jnp.zeros_like(grad))
                scores[h, window, :] = nt(values, one)
        for b, (low, high, row) in enumerate(WINDOWS):
            window = slice(row, row + high - low)
            for h in range(2):
                share = probs[2 * pair + h, window, :].astype(F32)
                moved = share * scores[h, window, :]
                moved = moved - share * jnp.sum(moved, axis=0, keepdims=True)
                d_pre[window, h * 256 : h * 256 + QBLK] = moved.astype(BF16)
        for array in (acc_k, acc_v):
            array[...] = jnp.zeros_like(array)
        for b, (low, high, row) in enumerate(WINDOWS):
            window = slice(row, row + high - low)
            block = slice(b * QBLK, (b + 1) * QBLK)
            keys = qkv[PAIRS + pair, low:high, :]
            query = qkv[pair, block, :]
            grad = d_mixed[block, aligned(pair, TILE)]
            both = [
                [
                    tn(d_pre[window, h * 256 : h * 256 + QBLK], keys),
                    nn(d_pre[window, h * 256 : h * 256 + QBLK], query),
                    nn(probs[2 * pair + h, window, :], grad),
                ]
                for h in range(2)
            ]
            d_q, d_k, d_v = [jnp.where(halves[0], one, two) for one, two in zip(*both)]
            hidden[block, pl.ds(pl.multiple_of(pair * 384, 128), 128)] = (d_q * 0.125).astype(BF16)
            acc_k[low:high, :] += d_k
            acc_v[low:high, :] += d_v
        hidden[0:SLOTS, pl.ds(pl.multiple_of(pair * 384 + 128, 128), 128)] = acc_k[...].astype(BF16)
        hidden[0:SLOTS, pl.ds(pl.multiple_of(pair * 384 + 256, 128), 128)] = acc_v[...].astype(BF16)
        d_qkv = hidden[0:SLOTS, pl.ds(pl.multiple_of(pair * 384, 128), 384)]
        sums = jnp.sum(d_qkv.astype(F32), axis=0, keepdims=True)
        pack[2:3, aligned(pair, TILE)] = sums[:, 0:128]
        pack[3:4, aligned(pair, TILE)] = sums[:, 256:384]
        d_w = tn(normed[...], d_qkv)
        for c in range(3):
            put_dense(4 * pair + c, d_w[:, c * TILE : (c + 1) * TILE])

        @pl.when(lax.rem(pair, pairs_in_unit) == pairs_in_unit - 1)
        def _():
            unit = lax.div(pair, pairs_in_unit)
            for age, hop in enumerate(hops):

                @pl.when(unit >= age)
                def _(age=age, hop=hop):
                    hop(unit - age)

        @pl.when(pair == 0)
        def _():
            loop(3, LOTS, send_lot)


    acc_k, acc_v = bias.at[0:SLOTS, 0:TILE], bias.at[0:SLOTS, TILE : 2 * TILE]
    loop(0, PAIRS, attend_back)

    def later(step):
        for age, hop in enumerate(hops):
            if 0 <= step - age < units:
                hop(step - age)


    def first_back(i):
        block = aligned(i, ROWBLK)
        grad = nt(hidden[block, 0 : 3 * WIDTH], wfull[:, 0 : 3 * WIDTH])
        value, inv_std = normalize(tok[block, :].astype(F32))
        pack[0:1, :] += jnp.sum(grad * value, axis=0, keepdims=True)
        pack[1:2, :] += jnp.sum(grad, axis=0, keepdims=True)
        d_middle[block, :] += norm_back(grad, value, inv_std, vecs[0:1, :])

    loop(0, SLOTS // ROWBLK, first_back)
    save_tokens = pltpu.make_async_copy(d_middle.at[0:SLOTS, :], o_tokens, s_own.at[2 + n_mine])
    save_tokens.start()

    def p_dp(i):
        return remote(pack, pack_dp.at[i], s_p.at[i], r_p.at[i], at.dp_peer(i))

    for i in range(1, n_d):
        p_dp(i).start()
    later(units)
    later(units + 1)
    e_spread(n_mine - 1)
    loop(0, n_mine - 1, e_forward)

    def vec_lane(owner):
        return aligned(lax.div(owner * shard, TILE), TILE)

    def qv_lane(owner):
        return aligned(lax.div(lax.rem(owner * 2 * shard, WIDTH), TILE), TILE)

    def p_vec(k):
        src = pack_dp.at[0, 0:bias_at, vec_lane(at.ahead(k))]
        return remote(src, vec_f.at[k], s_vf.at[k], r_vf.at[k], at.fsdp_peer(k))

    def p_qv(k):
        src = pack_dp.at[0, 0:8, qv_lane(at.ahead(k))]
        return remote(src, qv_f.at[k], s_qf.at[k], r_qf.at[k], at.fsdp_peer(k))

    pack_dp[0] = pack[...]
    for i in range(1, n_d):
        p_dp(i).wait_recv()
        pack_dp[0] += pack_dp[i]
    loop(1, n_f, lambda k: [p_vec(k).start(), p_qv(k).start()])
    save_bias = pltpu.make_async_copy(
        pack_dp.at[0, bias_at : bias_at + 8, :], o_bias, s_own.at[3 + n_mine]
    )
    save_bias.start()
    later(units + 2)
    e_forward(n_mine - 1)

    loop(1, n_f, lambda r: returned(ret_o, table_o, s_o, r_o, r).wait_recv())

    def combine(i):
        block = aligned(i, ROWBLK)
        total = middle[block, :] + nn(gather_rows(block), table_o[...])
        routed[block, :] = total.astype(BF16)

    loop(0, SLOTS // ROWBLK, combine)
    save_out = pltpu.make_async_copy(routed, o_out, s_own.at[4 + n_mine])
    save_out.start()
    later(units + 3)

    loop(1, n_f, lambda k: [p_vec(k).wait_recv(), p_qv(k).wait_recv()])
    vec_f[0] = pack_dp[0, 0:bias_at, vec_lane(at.me)]
    qv_f[0] = pack_dp[0, 0:8, qv_lane(at.me)]

    def add_lanes(k):
        vec_f[0] += vec_f[k]
        qv_f[0] += qv_f[k]

    loop(1, n_f, add_lanes)
    save_vec = pltpu.make_async_copy(vec_f.at[0], o_vec, s_own.at[5 + n_mine])
    save_qv = pltpu.make_async_copy(qv_f.at[0], o_qv, s_own.at[6 + n_mine])
    save_vec.start()
    save_qv.start()
    loop(0, units, lambda u: g_d(u, other).wait_recv())
    save_dense = pltpu.make_async_copy(final, o_dense, s_own.at[7 + n_mine])
    save_dense.start()

    def ended_f(k):
        send_v(k).wait_send()
        got_w(k).wait_send()
        for i in range(1, n_x):
            share_x(i, k).wait_send()
        for i in range(n_x):
            share_core(i, k).wait_send()
        give_back(ret_d, table_d, s_d, r_d, k).wait_send()
        give_back(ret_o, table_o, s_o, r_o, k).wait_send()
        p_vec(k).wait_send()
        p_qv(k).wait_send()

    loop(1, n_f, ended_f)

    def ended_e(j):
        to_partner(j).wait_send()
        for i in range(1, n_x):
            to_x(i, j).wait_send()
            all_x(i, j).wait_send()
        for i in range(n_x):
            to_core(i, j, at.core).wait_send()
            to_core(i, j, other).wait_recv()
            to_self(i, j).wait()

    loop(0, n_mine, ended_e)

    def ended_u(u):
        for x in range(n_x):
            g_core(u, x).wait_send()
            for j in range(1, n_y):
                g_y(u, x, j).wait_send()
            for i in range(1, n_z):
                g_z(u, x, i).wait_send()
        for i in range(1, n_x):
            g_x(u, i).wait_send()
        g_d(u, at.core).wait_send()

    loop(0, units, ended_u)
    for i in range(1, n_d):
        p_dp(i).wait_send()
    for copy in (save_tokens, save_bias, save_out, save_vec, save_qv, save_dense):
        copy.wait()


def block(n_f, n_d, experts, cap, cap_rows, small, w_in, w_out, b_in, b_out):
    vmem = pl.BlockSpec(memory_space=pltpu.VMEM)
    hbm = pl.BlockSpec(memory_space=pl.ANY)
    n_x = n_d // 2
    more_x = max(n_x - 1, 1)
    vec_rows = -(-(8 + experts) // 16) * 16
    shard = WIDTH // n_f
    table = n_f * cap_rows
    hid = w_in.shape[1]
    units = 16 // n_d
    n_mine = hid // FTILE
    n_y = y_members(n_f)
    more_y = max(n_y - 1, 1)
    pack_rows = 8 + experts + 8
    sds = jax.ShapeDtypeStruct
    vm = pltpu.VMEM
    dma = pltpu.SemaphoreType.DMA
    chunk_rows = table // CHUNKS
    pairs_of = lambda *shape: [dma(shape), dma(shape)]
    return pl.pallas_call(
        functools.partial(block_kernel, n_f, n_d, experts, cap, cap_rows),
        out_shape=(
            sds((SLOTS, WIDTH), BF16),
            sds((SLOTS, WIDTH), F32),
            sds((2 * n_mine, FTILE, WIDTH), BF16),
            sds((units, 2, n_x, shard, TILE), BF16),
            sds((8 + experts, TILE), F32),
            sds((8, TILE), F32),
            sds((8, WIDTH), F32),
        ),
        in_specs=[hbm] * 2 + [vmem] * (len(small) - 2) + [hbm] * 2 + [vmem] * 2,
        out_specs=[hbm] * 7,
        scratch_shapes=[
            vm((SLOTS, WIDTH), BF16),
            vm((SLOTS, WIDTH), BF16),
            vm((WIDTH, 4 * WIDTH), BF16),
            vm((vec_rows, WIDTH), BF16),
            vm((vec_rows, WIDTH), F32),
            vm((KEYS, 2 * TILE), F32),
            vm((2, KEYS, QBLK), F32),
            vm((2 * PAIRS, KEYS, QBLK), BF16),
            vm((3 * PAIRS, SLOTS, TILE), BF16),
            vm((SLOTS, WIDTH), BF16),
            vm((SLOTS, WIDTH), BF16),
            vm((SLOTS, WIDTH), F32),
            vm((SLOTS, WIDTH), BF16),
            vm((SLOTS, 8), F32),
        ]
        + [vm((table, WIDTH), BF16)] * 4
        + [
            vm((WIDTH, hid), BF16),
            vm((hid, WIDTH), BF16),
            vm((table, hid), BF16),
            vm((table, hid), BF16),
        ]
        + [vm((table, WIDTH), BF16)] * 3
        + [
            vm((2 * n_mine, FTILE, WIDTH), BF16),
            vm((n_mine, FTILE, WIDTH), BF16),
            vm((more_x, n_mine, FTILE // n_x, WIDTH), BF16),
            vm((units, n_x, WIDTH, TILE), BF16),
            vm((units, n_x, more_y, n_f // n_y * shard, TILE), BF16),
            vm((units, n_x, n_f // n_y, shard, TILE), BF16),
            vm((units, n_x, shard, TILE), BF16),
            vm((units, more_x, n_x, shard, TILE), BF16),
            vm((units, 2, n_x, shard, TILE), BF16),
            vm((pack_rows, WIDTH), F32),
            vm((n_d, pack_rows, WIDTH), F32),
            vm((n_f, 8 + experts, TILE), F32),
            vm((n_f, 8, TILE), F32),
            vm((max(2 * chunk_rows, SLOTS), WIDTH), F32),
        ]
        + pairs_of(n_f)
        + pairs_of(n_f)
        + pairs_of(more_x, n_f)
        + pairs_of(n_x, n_f)
        + pairs_of(n_f)
        + pairs_of(n_f)
        + pairs_of(n_f)
        + pairs_of(n_f)
        + pairs_of(n_mine)
        + pairs_of(more_x, n_mine)
        + pairs_of(more_x, n_mine)
        + pairs_of(n_x, n_mine)
        + pairs_of(units, n_x)
        + pairs_of(units, n_x, more_y)
        + pairs_of(units, n_x, n_f // n_y)
        + pairs_of(units, more_x)
        + pairs_of(units)
        + pairs_of(n_d)
        + pairs_of(n_f)
        + pairs_of(n_f)
        + [dma((8 + n_mine,)), dma((n_x, n_mine)), pltpu.SemaphoreType.REGULAR],
        compiler_params=pltpu.CompilerParams(
            collective_id=0, has_side_effects=True, vmem_limit_bytes=63 << 20
        ),
        name="block",
    )(*small, w_in, w_out, b_in, b_out)


def finish_kernel(
    n_f,
    experts,
    in_out,
    in_tokens,
    in_expert,
    dense,
    vec,
    qv,
    biases,
    o_out,
    o_tokens,
    o_g1,
    o_s1,
    o_qkv,
    o_bqv,
    o_wo,
    o_bo,
    o_g2,
    o_s2,
    o_router,
    o_w_in,
    o_b_in,
    o_w_out,
    o_b_out,
    low,
    wide,
    rows_low,
    rows_wide,
    s_load,
    s_save,
):
    me = lax.axis_index("fsdp")
    shard = WIDTH // n_f
    tiles = in_expert.shape[0]
    loads = [pltpu.make_async_copy(in_expert.at[t], low.at[t], s_load.at[t]) for t in range(tiles)]
    for load in loads:
        load.start()
    rows_in = [
        pltpu.make_async_copy(in_out, rows_low, s_load.at[tiles]),
        pltpu.make_async_copy(in_tokens, rows_wide, s_load.at[tiles + 1]),
    ]
    for load in rows_in:
        load.start()

    def my_lanes(value, size):
        place = lax.rem(me * size, TILE)
        total = jnp.zeros((value.shape[0], size), F32)
        for low_lane in range(0, TILE, size):
            total = total + jnp.where(place == low_lane, value[:, low_lane : low_lane + size], 0.0)
        return total

    own = my_lanes(vec[...], shard)
    for row, ref in ((0, o_g1), (1, o_s1), (4, o_bo), (5, o_g2), (6, o_s2)):
        ref[...] = own[row : row + 1, :]
    o_router[...] = own[8 : 8 + experts, :]
    lines = my_lanes(qv[...], 2 * shard)
    o_bqv[...] = jnp.where(me * 2 * shard < WIDTH, lines[2:3, :], lines[3:4, :])
    n_d = 2 * dense.shape[2]

    def tile(t):
        return dense[t // n_d, t % 2, t % n_d // 2].astype(F32)

    for pair in range(PAIRS):
        for c in range(3):
            at = c * WIDTH + pair * TILE
            o_qkv[:, at : at + TILE] = tile(4 * pair + c)
        o_wo[:, pair * TILE : (pair + 1) * TILE] = tile(4 * pair + 3)
    for f in range(tiles // 2):
        o_b_in[:, f * FTILE : (f + 1) * FTILE] = biases[f : f + 1, :]
    o_b_out[...] = biases[4:5, :]
    saves = []
    for t in range(tiles):
        loads[t].wait()
        wide[t] = low[t].astype(F32)
        piece = pl.ds(t // 2 * FTILE, FTILE)
        dst = o_w_out.at[0, piece, :] if t % 2 else o_w_in.at[0, :, piece]
        saves.append(pltpu.make_async_copy(wide.at[t], dst, s_save.at[t]))
        saves[-1].start()
    rows_out = [
        pltpu.make_async_copy(rows_low, o_out, s_save.at[tiles]),
        pltpu.make_async_copy(rows_wide, o_tokens, s_save.at[tiles + 1]),
    ]
    for load, save in zip(rows_in, rows_out):
        load.wait()
        save.start()
    for save in saves + rows_out:
        save.wait()


def finish(n_f, experts, hid, parts):
    vmem = pl.BlockSpec(memory_space=pltpu.VMEM)
    hbm = pl.BlockSpec(memory_space=pl.ANY)
    shard = WIDTH // n_f
    tiles = parts[2].shape[0]
    line = lambda *shape: jax.ShapeDtypeStruct(shape, F32)
    return pl.pallas_call(
        functools.partial(finish_kernel, n_f, experts),
        out_shape=(
            jax.ShapeDtypeStruct((SLOTS, WIDTH), BF16),
            line(SLOTS, WIDTH),
            line(1, shard),
            line(1, shard),
            line(shard, 3 * WIDTH),
            line(1, 2 * shard),
            line(shard, WIDTH),
            line(1, shard),
            line(1, shard),
            line(1, shard),
            line(experts, shard),
            line(1, WIDTH, hid),
            line(1, hid),
            line(1, hid, WIDTH),
            line(1, WIDTH),
        ),
        in_specs=[hbm] * 3 + [vmem] * 4,
        out_specs=[hbm] * 2 + [vmem] * 9 + [hbm, vmem, hbm, vmem],
        scratch_shapes=[
            pltpu.VMEM((tiles, FTILE, WIDTH), BF16),
            pltpu.VMEM((tiles, FTILE, WIDTH), F32),
            pltpu.VMEM((SLOTS, WIDTH), BF16),
            pltpu.VMEM((SLOTS, WIDTH), F32),
            pltpu.SemaphoreType.DMA((tiles + 2,)),
            pltpu.SemaphoreType.DMA((tiles + 2,)),
        ],
        compiler_params=pltpu.CompilerParams(vmem_limit_bytes=62 << 20),
        name="finish",
    )(*parts)


def shards(
    tokens,
    cotangent,
    segment_ids,
    pad_mask,
    expert_ids,
    priority,
    ln1_gain,
    ln1_shift,
    w_qkv,
    b_qv,
    w_o,
    b_o,
    ln2_gain,
    ln2_shift,
    w_router,
    w_in,
    b_in,
    w_out,
    b_out,
    n_f,
    n_d,
):
    experts = w_router.shape[1]
    cap = (21 * tokens.shape[0] + 10 * experts - 1) // (10 * experts)
    cap_rows = -(-cap // 16) * 16
    line = lambda vector: vector.reshape(1, -1)
    small = (
        tokens,
        cotangent,
        segment_ids,
        pad_mask,
        expert_ids.T,
        priority,
        w_qkv,
        w_o,
        line(ln1_gain),
        line(ln1_shift),
        line(b_qv),
        line(b_o),
        line(ln2_gain),
        line(ln2_shift),
        w_router.T,
    )
    parts = block(n_f, n_d, experts, cap, cap_rows, small, w_in[0], w_out[0], b_in, b_out)
    done = finish(n_f, experts, w_in.shape[2], parts)
    flat = (2, 3, 5, 7, 8, 9)
    done = [value.reshape(-1) if i in flat else value for i, value in enumerate(done)]
    done[10] = done[10].T
    return tuple(done)


def solution(mesh):
    both, one = P(("dp", "fsdp")), P("fsdp")
    n_f, n_d = mesh.shape["fsdp"], mesh.shape["dp"]
    return jax.shard_map(
        functools.partial(shards, n_f=n_f, n_d=n_d),
        mesh=mesh,
        in_specs=(both,) * 6 + (one,) * 13,
        out_specs=(both,) * 2 + (one,) * 13,
        check_vma=False,
    )
```
